32 devices in a mesh: seq: 2 (over y), ctx: 4 (over x, core), wt: 4 (over z).
Axes of the slice: x: 2, y: 2, z: 4, core: 2. Of those that a mesh axis runs over, the one named last changes fastest.
Arguments:
- tokens: bfloat16 [16, 1024, 768], P(('seq', 'wt'), 'ctx'), may hold values from -6 to 6
- cotangent: bfloat16 [16, 1024, 768], P(('seq', 'wt'), 'ctx'), may hold values from -6 to 6
- segment_ids: int32 [16, 1024], P(('seq', 'wt'), 'ctx'), may hold values from 0 to 4, as said below
- lengths: int32 [16, 4], P(('seq', 'wt')), may hold values from 32 to 928, as said below
- w_query: bfloat16 [768, 768], P('wt'), may hold values from -0.21875 to 0.21875
- b_query: bfloat16 [768], P('wt'), may hold values from -3 to 3
- w_key: bfloat16 [768, 768], P('wt'), may hold values from -0.21875 to 0.21875
- w_value: bfloat16 [768, 768], P('wt'), may hold values from -0.21875 to 0.21875
- b_value: bfloat16 [768], P('wt'), may hold values from -3 to 3
- w_attn: bfloat16 [768, 768], P('wt'), may hold values from -1.75 to 1.75
- b_attn: bfloat16 [768], P('wt'), may hold values from -2 to 2
- ln1_gain: bfloat16 [768], P('wt'), may hold values from 0.5 to 1.5
- ln1_shift: bfloat16 [768], P('wt'), may hold values from -2 to 2
- w_inner: bfloat16 [768, 3072], P('wt'), may hold values from -0.21875 to 0.21875
- b_inner: bfloat16 [3072], P('wt'), may hold values from -3 to 3
- w_outer: bfloat16 [3072, 768], P('wt'), may hold values from -0.109375 to 0.109375
- b_outer: bfloat16 [768], P('wt'), may hold values from -2 to 2
- ln2_gain: bfloat16 [768], P('wt'), may hold values from 0.5 to 1.5
- ln2_shift: bfloat16 [768], P('wt'), may hold values from -2 to 2
Outputs:
- layer_out: bfloat16 [16, 1024, 768], P(('seq', 'wt'), 'ctx')
- grad_input: bfloat16 [16, 1024, 768], P(('seq', 'wt'), 'ctx')
- grad_w_query: float32 [768, 768], P('wt')
- grad_b_query: float32 [768], P('wt')
- grad_w_key: float32 [768, 768], P('wt')
- grad_w_value: float32 [768, 768], P('wt')
- grad_b_value: float32 [768], P('wt')
- grad_w_attn: float32 [768, 768], P('wt')
- grad_b_attn: float32 [768], P('wt')
- grad_ln1_gain: float32 [768], P('wt')
- grad_ln1_shift: float32 [768], P('wt')
- grad_w_inner: float32 [768, 3072], P('wt')
- grad_b_inner: float32 [3072], P('wt')
- grad_w_outer: float32 [3072, 768], P('wt')
- grad_b_outer: float32 [768], P('wt')
- grad_ln2_gain: float32 [768], P('wt')
- grad_ln2_shift: float32 [768], P('wt')
The draws below stay inside these ranges and needn't reach their ends.
Inputs may be any that keep to these rules, and one draw needn't show every extreme that they name: `lengths`: the 4 documents of a sequence lie end to end from its first position, and the positions after them are padding; among the 2 sequences that one device holds, one has a single document of 1024 - 3 * max(1, 32) positions, at a place among its documents that varies, and its other documents have max(1, 32) positions each; every other sequence has documents of 64 to 256 positions. `segment_ids`: position t holds d + 1 where it lies in the sequence's document d (counted from 0 in the order of lengths), and 0 in the padding.
All inputs are finite; a program needn't handle non-finite values.
Results may differ from the reference program's by a relative error of at most 0.02.
Values may be sent and summed in bfloat16 or wider, within the bound.
No kernel may reach another device: no remote copies, remote signals or barrier semaphores. Data moves between devices by JAX's collectives and lax.ppermute only.
A program may use at most 320 MiB of HBM per device.

```python
import math
import jax
import jax.numpy as jnp
from jax import lax

D = 768
H = 12
HD = 64
FF = 3072
TOK_SHARD = 256
SEQ_DEV = 2
NDOC = 4
LEN = 1024
SEQS = 16


def doc_lengths(key):
    drawn = jax.random.randint(jax.random.fold_in(key, 11), (SEQS, NDOC), LEN // 16, LEN // 4 + 1)
    group_count = SEQS // SEQ_DEV
    picked = jax.random.randint(jax.random.fold_in(key, 12), (group_count,), 0, SEQ_DEV)
    places_long = jax.random.randint(jax.random.fold_in(key, 13), (SEQS,), 0, NDOC)
    seq_index = jnp.arange(SEQS, dtype=jnp.int32)
    is_long = seq_index % SEQ_DEV == picked[seq_index // SEQ_DEV]
    short_len = max(1, TOK_SHARD // 8)
    doc_index = jnp.arange(NDOC, dtype=jnp.int32)
    long_rows = jnp.where(doc_index[None, :] == places_long[:, None], LEN - (NDOC - 1) * short_len, short_len)
    drawn = jnp.where(is_long[:, None], long_rows, drawn)
    return drawn.astype(jnp.int32)


def draw_lengths(key, part):
    return doc_lengths(key)


def draw_segment_ids(key, part):
    drawn = doc_lengths(key)
    doc_ends = jnp.cumsum(drawn, axis=-1)
    places = jnp.arange(LEN, dtype=jnp.int32)
    passed = jnp.sum((places[None, :, None] >= doc_ends[:, None, :]).astype(jnp.int32), axis=-1)
    return jnp.where(places[None, :] < doc_ends[:, -1:], passed + 1, 0).astype(jnp.int32)


def steps_of(own_key, dims, cuts, least, largest):
    loudness, own = 1.0, jax.random.fold_in(own_key, 6)
    for dim, shards_of in cuts:
        steps = jnp.exp(jax.random.uniform(jax.random.fold_in(own, dim), (shards_of,), jnp.float32, least / len(cuts), largest / len(cuts)))
        loudness = loudness * jnp.repeat(steps, dims[dim] // shards_of).reshape([-1 if axis == dim else 1 for axis in range(len(dims))])
    return loudness


def centred(own_key, shape, deviation, reach, split=(), kind=jnp.bfloat16):
    values = jax.random.normal(own_key, shape, jnp.float32) * deviation
    if len(split) > 0:
        values = steps_of(own_key, shape, split, -0.22, 0.18) * values
    return jnp.clip(values, min=-reach, max=reach).astype(kind)


def setup_inputs(seed: int = 0) -> dict:
    splits = jax.random.split(jax.random.key(seed), 20)
    tokens = centred(splits[0], (SEQS, LEN, D), 1.0, 6.0, ((0, 8), (1, 4)))
    cotangent = centred(splits[1], (SEQS, LEN, D), 1.0, 6.0, ((0, 8), (1, 4)))
    segment_ids = draw_segment_ids(jax.random.fold_in(splits[19], 71), 0)
    lengths = draw_lengths(jax.random.fold_in(splits[19], 71), 0)
    w_query = centred(splits[4], (D, D), D ** -0.5, 0.21875, ((0, 4),))
    b_query = centred(splits[5], (D,), 0.5, 3.0, ((0, 4),))
    w_key = centred(splits[6], (D, D), D ** -0.5, 0.21875, ((0, 4),))
    w_value = centred(splits[7], (D, D), D ** -0.5, 0.21875, ((0, 4),))
    b_value = centred(splits[8], (D,), 0.5, 3.0, ((0, 4),))
    w_attn = centred(splits[9], (D, D), (D * 16 // LEN) ** -0.5, 1.75, ((0, 4),))
    b_attn = centred(splits[10], (D,), 0.3, 2.0, ((0, 4),))
    ln1_gain = jnp.clip(1.0 + 0.1 * jax.random.normal(splits[11], (D,), jnp.float32), 0.5, 1.5).astype(jnp.bfloat16)
    ln1_shift = centred(splits[12], (D,), 0.3, 2.0, ((0, 4),))
    w_inner = centred(splits[13], (D, FF), D ** -0.5, 0.21875, ((0, 4),))
    b_inner = centred(splits[14], (FF,), 0.5, 3.0, ((0, 4),))
    w_outer = centred(splits[15], (FF, D), FF ** -0.5, 0.109375, ((0, 4),))
    b_outer = centred(splits[16], (D,), 0.3, 2.0, ((0, 4),))
    ln2_gain = jnp.clip(1.0 + 0.1 * jax.random.normal(splits[17], (D,), jnp.float32), 0.5, 1.5).astype(jnp.bfloat16)
    ln2_shift = centred(splits[18], (D,), 0.3, 2.0, ((0, 4),))
    return dict(tokens=tokens, cotangent=cotangent, segment_ids=segment_ids, lengths=lengths, w_query=w_query, b_query=b_query, w_key=w_key, w_value=w_value, b_value=b_value, w_attn=w_attn, b_attn=b_attn, ln1_gain=ln1_gain, ln1_shift=ln1_shift, w_inner=w_inner, b_inner=b_inner, w_outer=w_outer, b_outer=b_outer, ln2_gain=ln2_gain, ln2_shift=ln2_shift)


NEG = -1000000000.0
EPS = 1e-05
HIGH = lax.Precision.HIGHEST

@jax.custom_vjp
def low(v):
    return lax.optimization_barrier(v.astype(jnp.bfloat16)).astype(jnp.float32)

@jax.custom_vjp
def low_back(v):
    return v

def low_keep(v):
    return (low(v), None)

def low_pass(kept, grad):
    return (grad,)

def back_keep(v):
    return (v, None)

def back_low(kept, grad):
    return (low(grad),)
low.defvjp(low_keep, low_pass)
low_back.defvjp(back_keep, back_low)

def product(former, latter):
    return jnp.dot(former, latter, precision=HIGH, preferred_element_type=jnp.float32)

def norm_rows(values, gain, shift):
    center = lax.optimization_barrier(jnp.mean(values, axis=-1, keepdims=True))
    offset = values - center
    spread = lax.optimization_barrier(jnp.mean(offset * offset, axis=-1, keepdims=True))
    return offset * lax.rsqrt(spread + EPS) * gain + shift

def key_segments(doc_lens, length):
    doc_ends = jnp.cumsum(doc_lens)
    places = jnp.arange(length, dtype=jnp.int32)
    passed = lax.optimization_barrier(jnp.sum((places[:, None] >= doc_ends[None, :]).astype(jnp.int32), axis=-1))
    return jnp.where(places < doc_ends[-1], passed + 1, 0).astype(jnp.int32)

def block_layer(rows, params, query_seg, key_seg):
    w_query, b_query, w_key, w_value, b_value, w_attn, b_attn, ln1_gain, ln1_shift, w_inner, b_inner, w_outer, b_outer, ln2_gain, ln2_shift = params
    length = rows.shape[0]
    factor = 1.0 / math.sqrt(HD)
    query = low(low_back(product(rows, w_query) + b_query))
    keys = low(low_back(product(rows, w_key)))
    values = low(low_back(product(rows, w_value) + b_value))
    matching = query_seg[:, None] == key_seg[None, :]

    def per_head(pieces):
        head_q, head_k, head_v = pieces
        scores = low_back(jnp.where(matching, product(head_q, head_k.T) * factor, NEG))
        probs = low(jax.nn.softmax(scores, axis=-1))
        return product(probs, head_v)

    def by_heads(matrix):
        return matrix.reshape(length, H, HD).transpose(1, 0, 2)
    heads = lax.map(jax.checkpoint(per_head), (by_heads(query), by_heads(keys), by_heads(values)))
    attn = low(low_back(heads.transpose(1, 0, 2).reshape(length, D)))
    first_sum = rows + low_back(product(attn, w_attn) + b_attn)
    hidden = norm_rows(first_sum, ln1_gain, ln1_shift)
    inner = low_back(product(low(hidden), w_inner) + b_inner)
    active = low(jax.nn.gelu(inner, approximate=False))
    second_sum = hidden + low_back(product(active, w_outer) + b_outer)
    return norm_rows(second_sum, ln2_gain, ln2_shift)

def reference(tokens, cotangent, segment_ids, lengths, w_query, b_query, w_key, w_value, b_value, w_attn, b_attn, ln1_gain, ln1_shift, w_inner, b_inner, w_outer, b_outer, ln2_gain, ln2_shift):
    params = tuple((piece.astype(jnp.float32) for piece in (w_query, b_query, w_key, w_value, b_value, w_attn, b_attn, ln1_gain, ln1_shift, w_inner, b_inner, w_outer, b_outer, ln2_gain, ln2_shift)))

    def one_sequence(totals, item):
        rows, grad_rows, query_seg, doc_lens = item
        key_seg = key_segments(doc_lens, rows.shape[0])
        live = (query_seg != 0).astype(jnp.float32)[:, None]

        def forward(inputs, weights):
            return block_layer(inputs, weights, query_seg, key_seg)
        result, pull = jax.vjp(forward, rows.astype(jnp.float32), params)
        d_rows, d_params = pull(grad_rows.astype(jnp.float32) * live)
        totals = jax.tree.map(jnp.add, totals, d_params)
        return (totals, (result.astype(jnp.bfloat16), d_rows.astype(jnp.bfloat16)))
    zeros = jax.tree.map(jnp.zeros_like, params)
    totals, outputs = lax.scan(one_sequence, zeros, (tokens, cotangent, segment_ids, lengths))
    return (outputs[0], outputs[1], totals[0], totals[1], totals[2], totals[3], totals[4], totals[5], totals[6], totals[7], totals[8], totals[9], totals[10], totals[11], totals[12], totals[13], totals[14])
```

```python
import functools
import math

import jax
import jax.numpy as jnp
from jax import lax
from jax.experimental import pallas as pl
from jax.experimental.pallas import tpu as pltpu
from jax.sharding import Mesh
from jax.sharding import PartitionSpec as P

H = 12
HD = 64
NEG = -1000000000.0
EPS = 1e-05
BF = jnp.bfloat16
F32 = jnp.float32
AX = ("seq", "pg", "x", "core", "wt")
VM = pl.BlockSpec(memory_space=pltpu.VMEM)
SM = pl.BlockSpec(memory_space=pltpu.SMEM)
ANY = pl.BlockSpec(memory_space=pl.ANY)
OFFS = (0, 2, 1, 3)
VMEM_LIMIT = 62 * 2**20


def mm(a, b):
    return jnp.dot(a, b, preferred_element_type=F32)


def mm_nt(a, b):
    return lax.dot_general(a, b, (((1,), (1,)), ((), ())), preferred_element_type=F32)


def mm_tn(a, b):
    return lax.dot_general(a, b, (((0,), (0,)), ((), ())), preferred_element_type=F32)


def span(bounds, s, first, last):
    low = jnp.int32(0)
    high = bounds[s, 5]
    for d in range(1, 5):
        low = jnp.where(bounds[s, d] <= first, bounds[s, d], low)
        e = 5 - d
        high = jnp.where(bounds[s, e] > last, bounds[s, e], high)
    return low, high


def attn_fwd_kernel(pg, bounds, idx, qa, qb, o_ref, q_out, k_out, v_out, m_s, acc_s):
    c, mine = idx[0], idx[1]
    T = qa.shape[3]
    lane = lax.broadcasted_iota(jnp.int32, (T, 128), 1)
    row = lax.broadcasted_iota(jnp.int32, (T, 128), 0)
    lower = lane < 64

    def per_seq(s, _):
        for g in range(pg):
            for n, off in enumerate(OFFS):
                src = qa if n < 2 else qb
                tile = g * 4 + (c ^ off)
                place = pl.multiple_of(tile * T, T)
                pos = row + place
                seg = jnp.zeros((T, 128), jnp.int32)
                for d in range(1, 5):
                    seg = seg + (pos >= bounds[s, d]).astype(jnp.int32)
                rel = lane & 63
                hot = rel == seg
                q_aug = jnp.where(hot, 1.0, 0.0)
                k_aug = jnp.where(rel < 5, jnp.where(hot, 0.0, NEG), jnp.where(rel < 11, 1.0, 0.0))

                def part(i):
                    return src[g, n % 2, s, :, i * 128 : (i + 1) * 128].astype(F32)

                q01, k01, v01, v2q2, k2 = (part(i) for i in range(5))
                keep = (lower, ~lower, ~lower)
                for h, (q, k) in enumerate(((q01, k01), (q01, k01), (v2q2, k2))):
                    k_out[s, h, pl.ds(place, T)] = jnp.where(keep[h], k, k_aug).astype(BF)
                    v = v01 if h < 2 else v2q2
                    kv = lower if h != 1 else ~lower
                    v_out[s, h, pl.ds(place, T)] = jnp.where(kv, v, 1.0).astype(BF)

                @pl.when(mine == g)
                def _():
                    own = pl.multiple_of((c ^ off) * T, T)
                    for h, q in enumerate((q01, q01, v2q2)):
                        q_out[s, h, pl.ds(own, T)] = jnp.where(keep[h], q * 0.125, q_aug).astype(BF)

        def per_tile(i, _):
            here = pl.multiple_of(i * T, T)
            first = (mine * 4 + i) * T
            low, high = span(bounds, s, first, first + T - 1)
            for h in range(3):
                m_s[h] = jnp.full((T, 128), -jnp.inf, F32)
                acc_s[h] = jnp.zeros((T, 128), F32)

            def step(kt, _):
                at = pl.multiple_of(kt * T, T)
                for h in range(3):
                    sc = mm_nt(q_out[s, h, pl.ds(here, T)], k_out[s, h, pl.ds(at, T)])
                    old = m_s[h]
                    new = jnp.maximum(old, jnp.max(sc, axis=1, keepdims=True))
                    p = jnp.exp(sc - new[:, :1])
                    acc_s[h] = acc_s[h] * jnp.exp(old - new) + mm(
                        p.astype(BF), v_out[s, h, pl.ds(at, T)]
                    )
                    m_s[h] = new
                return 0

            lax.fori_loop(low // T, (high + T - 1) // T, step, 0)
            outs = []
            for h in range(3):
                acc = acc_s[h]
                other = pltpu.roll(acc, 64, 1)
                data = lower if h != 1 else ~lower
                total = jnp.where(data, other, acc)
                outs.append(acc / total)
                lse = m_s[h] + jnp.log(total)
                l1 = lse.astype(BF).astype(F32)
                l2 = (lse - l1).astype(BF).astype(F32)
                l3 = lse - l1 - l2
                rel = lane if h > 0 else lane - 64
                q = q_out[s, h, pl.ds(here, T)].astype(F32)
                q = jnp.where(rel == 8, -l1, jnp.where(rel == 9, -l2, jnp.where(rel == 10, -l3, q)))
                q_out[s, h, pl.ds(here, T)] = q.astype(BF)
            o_ref[i, s, :, 0:128] = jnp.where(lower, outs[0], outs[1]).astype(BF)
            o_ref[i, s, :, 128:192] = outs[2][:, 0:64].astype(BF)
            return 0

        lax.fori_loop(0, 4, per_tile, 0)
        return 0

    lax.fori_loop(0, 2, per_seq, 0)


def attn_bwd_kernel(pg, bounds, idx, q_ref, k_ref, v_ref, o_ref, do_ref, d_ref, dq_s, dk_s, dv_s, do_s):
    c, mine = idx[0], idx[1]
    T = o_ref.shape[2]
    lane = lax.broadcasted_iota(jnp.int32, (T, 128), 1)
    lower = lane < 64

    def per_seq(s, _):
        dk_s[...] = jnp.zeros_like(dk_s)
        dv_s[...] = jnp.zeros_like(dv_s)
        dq_s[...] = jnp.zeros_like(dq_s)
        live = bounds[s, 4]

        def per_tile(i, _):
            here = pl.multiple_of(i * T, T)
            first = (mine * 4 + i) * T
            low, high = span(bounds, s, first, first + T - 1)
            high = jnp.minimum(high, live)
            pair = do_ref[i, s, :, 0:128].astype(F32)
            last = do_ref[i, s, :, 128:192].astype(F32)
            last = jnp.concatenate([last, jnp.zeros_like(last)], axis=1)
            o_last = o_ref[i, s, :, 128:192].astype(F32)
            o_last = jnp.concatenate([o_last, jnp.zeros_like(o_last)], axis=1)
            prod = pair * o_ref[i, s, :, 0:128].astype(F32)
            zero = jnp.zeros_like(prod)
            for h in range(3):
                data = lower if h != 1 else ~lower
                full = prod if h < 2 else last * o_last
                delta = jnp.sum(jnp.where(data, full, zero), axis=1, keepdims=True)
                d1 = delta.astype(BF).astype(F32)
                d2 = (delta - d1).astype(BF).astype(F32)
                d3 = delta - d1 - d2
                rel = lane if h == 1 else lane - 64
                aug = jnp.where(rel == 8, -d1, jnp.where(rel == 9, -d2, jnp.where(rel == 10, -d3, zero)))
                do_s[h] = jnp.where(data, pair if h < 2 else last, aug).astype(BF)

            def step(kt, _):
                at = pl.multiple_of(kt * T, T)
                for h in range(3):
                    q = q_ref[s, h, pl.ds(here, T)]
                    k = k_ref[s, h, pl.ds(at, T)]
                    d = do_s[h]
                    pt = jnp.exp(mm_nt(k, q))
                    ds = (pt * mm_nt(v_ref[s, h, pl.ds(at, T)], d)).astype(BF)
                    dv_s[h, pl.ds(at, T)] += mm(pt.astype(BF), d)
                    dk_s[h, pl.ds(at, T)] += mm(ds, q)
                    dq_s[h, pl.ds(here, T)] += mm_tn(ds, k)
                return 0

            lax.fori_loop(low // T, (high + T - 1) // T, step, 0)
            return 0

        lax.fori_loop(0, 4, per_tile, 0)
        for g in range(pg):
            for n, off in enumerate(OFFS):
                at = pl.multiple_of((g * 4 + (c ^ off)) * T, T)
                own = pl.multiple_of((c ^ off) * T, T)
                keep = jnp.where(mine == g, 0.125, 0.0)
                dq = [dq_s[h, pl.ds(own, T)] * keep for h in range(3)]
                dk = [dk_s[h, pl.ds(at, T)] for h in range(3)]
                dv = [dv_s[h, pl.ds(at, T)] for h in range(3)]
                d_ref[g, n, s, :, 0:128] = jnp.where(lower, dq[0], dq[1]).astype(BF)
                d_ref[g, n, s, :, 128:256] = jnp.where(lower, dk[0], dk[1]).astype(BF)
                d_ref[g, n, s, :, 256:384] = jnp.where(lower, dv[0], dv[1]).astype(BF)
                d_ref[g, n, s, :, 384:512] = jnp.where(lower, dv[2], dq[2]).astype(BF)
                d_ref[g, n, s, :, 512:640] = jnp.where(lower, 0.0, dk[2]).astype(BF)
        return 0

    lax.fori_loop(0, 2, per_seq, 0)


def gelu_parts(u):
    t = 1.0 / (1.0 + (0.3275911 * 0.7071067811865476) * jnp.abs(u))
    e = jnp.exp(-0.5 * u * u)
    poly = t * (
        0.127414796
        + t * (-0.142248368 + t * (0.7107068705 + t * (-0.7265760135 + t * 0.5307027145)))
    )
    tail = poly * e
    cdf = jnp.where(u >= 0, 1.0 - tail, tail)
    return u * cdf, cdf + u * e * 0.3989422804014327


def fold8(v):
    return jnp.sum(v.reshape(v.shape[0] // 8, 8, v.shape[1]), axis=0)


def ffn_kernel(
    idx, attn, tok, cot, live, vec, b1,
    s1a, r2a, c1a, c2a, s1b, r2b, c1b, c2b,
    out, dfirst, dattn, g1o, g1x, g2o, g2x, small, gb1,
    w1, w2, wa, hid, hlow, xhat, rstd, acc, act, gp, din, dlow, sums, g2s, sem,
):
    c = idx[0]
    R, D = tok.shape
    FB = b1.shape[2]
    TR = 128
    copies = []
    for n, ref in enumerate((s1a, r2a, c1a, c2a)):
        for k in range(2):
            p = idx[2 + 2 * n + k]
            copies.append((ref.at[k, :, 0:192], w1.at[:, :, pl.ds(pl.multiple_of(p * FB, 128), FB)]))
            q, half = p // 2, p % 2
            copies.append((
                ref.at[k, :, 192:240],
                wa.at[:, pl.ds(pl.multiple_of(q * 48, 16), 48), pl.ds(pl.multiple_of(half * FB, 128), FB)],
            ))
    for n, ref in enumerate((s1b, r2b, c1b, c2b)):
        for k in range(2):
            p = idx[2 + 2 * n + k]
            copies.append((ref.at[k], w2.at[:, pl.ds(pl.multiple_of(p * 96, 16), 96)]))
    copies = [pltpu.make_async_copy(a, b, sem.at[i]) for i, (a, b) in enumerate(copies)]
    for cp in copies:
        cp.start()
    for cp in copies:
        cp.wait()

    b_attn, g1v, s1v, b_out, g2v, s2v = (vec[i : i + 1, :] for i in range(6))
    sums[...] = jnp.zeros_like(sums)

    def first(r, _):
        rows = pl.ds(pl.multiple_of(r * TR, TR), TR)
        v = tok[rows, :].astype(F32) + b_attn
        for g in range(4):
            v = v + mm(attn[g, rows, :], wa[g])
        mean = jnp.mean(v, axis=-1, keepdims=True)
        v = v - mean
        rs = lax.rsqrt(jnp.mean(v * v, axis=-1, keepdims=True) + EPS)
        xh = v * rs
        xhat[rows, :] = xh
        rstd[rows, :] = jnp.broadcast_to(rs, (TR, 128))
        h = xh * g1v + s1v
        hid[rows, :] = h
        hlow[rows, :] = h.astype(BF)
        acc[rows, :] = h + b_out
        return 0

    lax.fori_loop(0, R // TR, first, 0)

    def block(z, half):
        return w2[z, half * FB : (half + 1) * FB, :]

    def forward(z, _):
        for half in range(2):
            j = z * 2 + half
            cols = pl.ds(pl.multiple_of(j * FB, 128), FB)
            w = w1[:, :, cols].reshape(D, FB)
            for r in range(R // TR):
                rows = slice(r * TR, (r + 1) * TR)
                u = mm(hlow[rows, :], w) + b1[j]
                a, d = gelu_parts(u)
                a = a.astype(BF)
                act[j, rows, :] = a
                gp[j, rows, :] = d.astype(BF)
                acc[rows, :] += mm(a, block(z, half))
        return 0

    lax.fori_loop(0, 4, forward, 0)

    def second(r, _):
        rows = pl.ds(pl.multiple_of(r * TR, TR), TR)
        v = acc[rows, :]
        mean = jnp.mean(v, axis=-1, keepdims=True)
        v = v - mean
        rs = lax.rsqrt(jnp.mean(v * v, axis=-1, keepdims=True) + EPS)
        xh = v * rs
        out[rows, :] = (xh * g2v + s2v).astype(BF)
        dy = cot[rows, :].astype(F32) * live[rows, :]
        sums[4] += fold8(dy * xh)
        sums[5] += fold8(dy)
        dx = dy * g2v
        m1 = jnp.mean(dx, axis=-1, keepdims=True)
        m2 = jnp.mean(dx * xh, axis=-1, keepdims=True)
        ds = rs * (dx - m1 - xh * m2)
        low = ds.astype(BF)
        dlow[rows, :] = low
        sums[3] += fold8(low.astype(F32))
        acc[rows, :] = ds
        return 0

    lax.fori_loop(0, R // TR, second, 0)

    def backward(yx, _):
        for o in range(2):
            half = c if o == 0 else 1 - c
            j = yx * 2 + half
            cols = pl.ds(pl.multiple_of(j * FB, 128), FB)
            w2j = w2[yx, pl.ds(pl.multiple_of(half * FB, 128), FB), :]
            w1j = w1[:, :, cols].reshape(D, FB)
            g2s[...] = mm_tn(act[j], dlow[...]).astype(BF)
            for xx in range(2):
                for o2, ref in ((0, g2o), (1, g2x)):
                    cc = c if o2 == 0 else 1 - c
                    at = pl.multiple_of((xx * 2 + cc) * 96, 16)
                    ref[half * 2 + xx, yx] = g2s[pl.ds(at, 96), :]
            gsum = jnp.zeros((8, FB), F32)
            for r in range(R // TR):
                rows = slice(r * TR, (r + 1) * TR)
                di = (mm_nt(dlow[rows, :], w2j) * gp[j, rows, :].astype(F32)).astype(BF)
                din[rows, :] = di
                gsum = gsum + fold8(di.astype(F32))
                acc[rows, :] += mm_nt(di, w1j)
            gb1[j] = gsum
            g1 = mm_tn(hlow[...], din[...]).astype(BF)
            ref = g1o if o == 0 else g1x
            for z in range(4):
                ref[yx, z, 0:192, :] = g1[z * 192 : (z + 1) * 192, :]
        return 0

    lax.fori_loop(0, 4, backward, 0)

    def last(r, _):
        rows = pl.ds(pl.multiple_of(r * TR, TR), TR)
        dy = acc[rows, :]
        xh = xhat[rows, :]
        sums[1] += fold8(dy * xh)
        sums[2] += fold8(dy)
        dx = dy * g1v
        m1 = jnp.mean(dx, axis=-1, keepdims=True)
        m2 = jnp.mean(dx * xh, axis=-1, keepdims=True)
        df = rstd[rows, :1] * (dx - m1 - xh * m2)
        dfirst[rows, :] = df
        low = df.astype(BF)
        dlow[rows, :] = low
        sums[0] += fold8(low.astype(F32))
        for g in range(4):
            dattn[g, rows, :] = mm_nt(low, wa[g]).astype(BF)
        return 0

    lax.fori_loop(0, R // TR, last, 0)
    for g in range(4):
        ga = mm_tn(attn[g], dlow[...]).astype(BF)
        for q in range(4):
            for o, ref in ((0, g1o), (1, g1x)):
                cc = c if o == 0 else 1 - c
                left, right = ga[q * 48 : (q + 1) * 48, :FB], ga[q * 48 : (q + 1) * 48, FB:]
                ref[q, g, 192:240, :] = jnp.where(cc == 0, left.astype(F32), right.astype(F32)).astype(BF)
    for i in range(6):
        small[i : i + 1, :] = jnp.sum(sums[i], axis=0, keepdims=True)


def bcast_a2a(a, axes, n):
    return lax.all_to_all(jnp.broadcast_to(a[None], (n,) + a.shape), axes, 0, 0, tiled=True)


def make_body(sizes):
    pg = sizes["pg"]
    order = [sizes[a] for a in AX]

    def send(a, fn):
        pairs = []
        for flat in range(math.prod(order)):
            at, rest = [], flat
            for n in reversed(order):
                at.append(rest % n)
                rest //= n
            to = fn(*reversed(at))
            dest = 0
            for n, v in zip(order, to):
                dest = dest * n + v
            pairs.append((flat, dest))
        return lax.ppermute(a, AX, pairs)

    to_x = functools.partial(send, fn=lambda s, g, x, c, z: (s, g, 1 - x, c, z))
    to_core = functools.partial(send, fn=lambda s, g, x, c, z: (s, g, x, 1 - c, z))
    mix_a = functools.partial(send, fn=lambda s, g, x, c, z: (s, g, 1 - x, c, z) if c == 0 else (1 - s, g, x, c, z))
    mix_b = functools.partial(send, fn=lambda s, g, x, c, z: (1 - s, g, x, c, z) if c == 0 else (s, g, 1 - x, c, z))

    def spread(own):
        s1 = jnp.stack([own, mix_a(own)])
        r2 = mix_b(s1)
        return s1, r2, to_core(s1), to_core(r2)

    def body(
        tokens, cotangent, segment_ids, lengths, w_query, b_query, w_key, w_value, b_value, w_attn, b_attn,
        ln1_gain, ln1_shift, w_inner, b_inner, w_outer, b_outer, ln2_gain, ln2_shift,
    ):
        S, T, D = tokens.shape
        R = S * T
        y, x, c = (lax.axis_index(a) for a in ("seq", "x", "core"))
        mine, z = lax.axis_index("pg"), lax.axis_index("wt")
        h = x * 2 + c
        p = y * 4 + h
        L = 4 * pg * T
        FB = w_inner.shape[1] // 8

        tok_a = jnp.stack([tokens, to_x(tokens)])
        tok_b = to_core(tok_a)

        def cols(w):
            return lax.dynamic_slice_in_dim(w, h * 192, 192, 1)

        wq, wk, wv = cols(w_query), cols(w_key), cols(w_value)
        pack = jnp.concatenate([wq[:, :128], wk[:, :128], wv[:, :128], wv[:, 128:], wq[:, 128:], wk[:, 128:]], axis=1)
        smalls = jnp.concatenate([b_query, b_value, b_attn, ln1_gain, ln1_shift, b_outer, ln2_gain, ln2_shift, b_inner])
        pack = jnp.concatenate([pack, smalls.reshape(4, 576), jnp.zeros((12, 576), BF)], axis=0)
        got = bcast_a2a(pack, "wt", 4)
        w_qkv = got[:, :192].reshape(D, 576)
        w_qkv = jnp.concatenate([w_qkv[:, :512], jnp.zeros((D, 64), BF), w_qkv[:, 512:]], axis=1)
        small_in = got[:, 192:196].reshape(4, 2304).astype(F32)
        vec = small_in[:, 384:1536].reshape(4, 6, 192).transpose(1, 0, 2).reshape(6, D)
        vec = jnp.concatenate([vec, jnp.zeros((2, D), F32)], axis=0)
        b1 = small_in[:, 1536:].reshape(8, 1, FB)
        mine_small = lax.dynamic_slice_in_dim(small_in, h, 1, 0)[0]
        bq, bv = mine_small[:192], mine_small[192:384]
        zero = jnp.zeros((128,), F32)
        b_qkv = jnp.concatenate([bq[:128], zero, bv[:128], bv[128:], bq[128:], zero])

        own1 = lax.dynamic_slice_in_dim(w_inner, p * FB, FB, 1)
        own_a = lax.dynamic_slice(w_attn, ((p // 2) * 48, c * FB), (48, FB))
        own2 = lax.dynamic_slice_in_dim(w_outer, p * 96, 96, 0)
        piece1 = bcast_a2a(jnp.concatenate([own1, own_a], axis=0), "wt", 4)
        piece2 = bcast_a2a(own2, "wt", 4)
        one = spread(piece1)
        two = spread(piece2)

        def project(t):
            v = jnp.dot(t.reshape(-1, D), w_qkv, preferred_element_type=F32) + b_qkv
            return v.astype(BF).reshape(1, 2, S, T, 640)

        qkv_a, qkv_b = project(tok_a), project(tok_b)
        if pg > 1:
            qkv_a = lax.all_gather(qkv_a, "pg", axis=0, tiled=True)
            qkv_b = lax.all_gather(qkv_b, "pg", axis=0, tiled=True)
        ends = [lengths[:, :1]]
        for d in range(1, 4):
            ends.append(ends[-1] + lengths[:, d : d + 1])
        bounds = jnp.concatenate(
            [jnp.zeros_like(ends[0])] + ends + [jnp.full_like(ends[0], L), jnp.zeros((S, 2), jnp.int32)], axis=1
        ).astype(jnp.int32)
        a_of = jnp.where(c == 0, 2, 4)
        mates = [p, p ^ a_of, p ^ (6 - a_of), p ^ 6]
        other = p ^ 1
        mates += [other, other ^ (6 - a_of), other ^ a_of, other ^ 6]
        idx = jnp.stack([h, mine] + mates).astype(jnp.int32)
        idx_f = jnp.stack([c, mine] + mates).astype(jnp.int32)
        head = (S, 3, L, 128)
        own_head = (S, 3, 4 * T, 128)
        params = pltpu.CompilerParams(vmem_limit_bytes=VMEM_LIMIT)
        o, q_aug, k_aug, v_aug = pl.pallas_call(
            functools.partial(attn_fwd_kernel, pg),
            out_shape=(
                jax.ShapeDtypeStruct((4, S, T, 192), BF),
                jax.ShapeDtypeStruct(own_head, BF),
                jax.ShapeDtypeStruct(head, BF),
                jax.ShapeDtypeStruct(head, BF),
            ),
            in_specs=[SM, SM, VM, VM],
            out_specs=(VM,) * 4,
            scratch_shapes=[pltpu.VMEM((3, T, 128), F32), pltpu.VMEM((3, T, 128), F32)],
            compiler_params=params,
            cost_estimate=pl.CostEstimate(flops=30 * 10**9, bytes_accessed=10 * 2**20, transcendentals=0),
            name="attn_fwd",
        )(bounds, idx, qkv_a, qkv_b)
        attn = lax.all_to_all(o, ("x", "core"), 0, 0, tiled=True)

        live = (segment_ids != 0).astype(F32).reshape(R, 1)
        res = pl.pallas_call(
            ffn_kernel,
            out_shape=(
                jax.ShapeDtypeStruct((R, D), BF),
                jax.ShapeDtypeStruct((R, D), F32),
                jax.ShapeDtypeStruct((4, R, 192), BF),
                jax.ShapeDtypeStruct((4, 4, 240, FB), BF),
                jax.ShapeDtypeStruct((4, 4, 240, FB), BF),
                jax.ShapeDtypeStruct((4, 4, 96, D), BF),
                jax.ShapeDtypeStruct((4, 4, 96, D), BF),
                jax.ShapeDtypeStruct((8, D), F32),
                jax.ShapeDtypeStruct((8, 8, FB), F32),
            ),
            in_specs=[SM] + [VM] * 6 + [ANY] * 8,
            out_specs=(VM,) * 9,
            scratch_shapes=[
                pltpu.VMEM((4, 192, 8 * FB), BF),
                pltpu.VMEM((4, 8 * FB // 4, D), BF),
                pltpu.VMEM((4, 192, D), BF),
                pltpu.VMEM((R, D), F32),
                pltpu.VMEM((R, D), BF),
                pltpu.VMEM((R, D), F32),
                pltpu.VMEM((R, 128), F32),
                pltpu.VMEM((R, D), F32),
                pltpu.VMEM((8, R, FB), BF),
                pltpu.VMEM((8, R, FB), BF),
                pltpu.VMEM((R, FB), BF),
                pltpu.VMEM((R, D), BF),
                pltpu.VMEM((8, 8, D), F32),
                pltpu.VMEM((FB, D), BF),
                pltpu.SemaphoreType.DMA((24,)),
            ],
            compiler_params=params,
            cost_estimate=pl.CostEstimate(flops=40 * 10**9, bytes_accessed=20 * 2**20, transcendentals=0),
            name="ffn",
        )(
            idx_f, attn.reshape(4, R, 192), tokens.reshape(R, D), cotangent.reshape(R, D), live, vec, b1,
            *one, *two,
        )
        layer_out, d_first, d_attn, g1o, g1x, g2o, g2x, small, gb1 = res

        def reduce(own, other):
            v = (own.astype(F32) + to_core(other).astype(F32)).astype(BF)
            v = lax.all_to_all(v, ("seq", "x"), 0, 0, tiled=True)
            v = jnp.sum(v.astype(F32), axis=0).astype(BF)
            v = lax.all_to_all(v, "wt", 0, 0, tiled=True)
            v = jnp.sum(v.astype(F32), axis=0)
            if pg > 1:
                v = lax.psum(v, "pg")
            return bcast_a2a(v.astype(BF), ("seq", "x", "core"), 8)

        g2 = reduce(g2o, g2x)
        g1 = reduce(g1o, g1x)
        small_sum = jnp.concatenate([small[:6].reshape(-1), jnp.sum(gb1, axis=1).reshape(-1)]).reshape(10, D)
        small_sum = lax.psum(small_sum, AX)

        d_o = lax.all_to_all(d_attn.reshape(4, S, T, 192), ("x", "core"), 0, 0, tiled=True)
        d = pl.pallas_call(
            functools.partial(attn_bwd_kernel, pg),
            out_shape=jax.ShapeDtypeStruct((pg, 4, S, T, 640), BF),
            in_specs=[SM, SM] + [VM] * 5,
            out_specs=VM,
            scratch_shapes=[
                pltpu.VMEM((3, 4 * T, 128), F32),
                pltpu.VMEM((3, L, 128), F32),
                pltpu.VMEM((3, L, 128), F32),
                pltpu.VMEM((3, T, 128), BF),
            ],
            compiler_params=params,
            cost_estimate=pl.CostEstimate(flops=40 * 10**9, bytes_accessed=10 * 2**20, transcendentals=0),
            name="attn_bwd",
        )(bounds, idx, q_aug, k_aug, v_aug, o, d_o)
        if pg > 1:
            d = lax.psum_scatter(d, "pg", scatter_dimension=0, tiled=True)
        d = d.reshape(4, R, 640)
        d_a, d_b = d[:2].reshape(2 * R, 640), d[2:].reshape(2 * R, 640)

        def back(v):
            return lax.dot_general(v, w_qkv, (((1,), (1,)), ((), ())), preferred_element_type=F32)

        def over_rows(a, b):
            return lax.dot_general(a, b, (((0,), (0,)), ((), ())), preferred_element_type=F32)

        gi_b = to_core(back(d_b).astype(BF))
        gi_a = back(d_a) + gi_b.astype(F32)
        gi_x = to_x(gi_a[R:].astype(BF))
        grad_input = (gi_a[:R] + gi_x.astype(F32) + d_first).astype(BF).reshape(tokens.shape)

        gq = over_rows(tok_a.reshape(2 * R, D), d_a) + over_rows(tok_b.reshape(2 * R, D), d_b)
        col = jnp.sum(d.astype(F32), axis=(0, 1))
        gq = jnp.concatenate([gq[:, :512], gq[:, 576:]], axis=1).astype(BF)
        if pg > 1:
            gq = lax.psum(gq, "pg")
        gq = lax.all_to_all(gq.reshape(8, 96, 576), ("wt", "seq"), 0, 0, tiled=True)
        gq = jnp.sum(gq.astype(F32), axis=0).astype(BF)
        gq = bcast_a2a(gq, ("seq", "x", "core"), 8).astype(F32).reshape(2, 4, 96, 576)

        def rows_of(*parts):
            return jnp.concatenate(parts, axis=-1).transpose(0, 2, 1, 3).reshape(192, D)

        g_wq = rows_of(gq[..., 0:128], gq[..., 448:512])
        g_wk = rows_of(gq[..., 128:256], gq[..., 512:576])
        g_wv = rows_of(gq[..., 256:384], gq[..., 384:448])
        bias = jnp.stack([jnp.concatenate([col[0:128], col[448:512]]), jnp.concatenate([col[256:384], col[384:448]])])
        wide = jnp.where((jnp.arange(4) == h)[None, :, None], bias[:, None, :], 0.0).reshape(2, D)
        bias_sum = lax.psum(wide, AX)

        def shard(v):
            n = v.shape[0] // 4
            return lax.dynamic_slice_in_dim(v, z * n, n, 0)

        g1 = g1.astype(F32)
        g_wi = g1[:, :192].transpose(1, 0, 2).reshape(192, 8 * FB)
        g_wa = g1[:, 192:].reshape(4, 2, 48, FB).transpose(0, 2, 1, 3).reshape(192, D)
        g_wo = g2.astype(F32).reshape(768, D)
        return (
            layer_out.reshape(tokens.shape), grad_input,
            g_wq, shard(bias_sum[0]), g_wk, g_wv, shard(bias_sum[1]),
            g_wa, shard(small_sum[0]), shard(small_sum[1]), shard(small_sum[2]),
            g_wi, shard(small_sum[6:].reshape(-1)), g_wo, shard(small_sum[3]),
            shard(small_sum[4]), shard(small_sum[5]),
        )

    return body


def solution(mesh):
    sizes = dict(mesh.shape)
    pg = sizes["ctx"] // 4
    fine = dict(zip(AX, (sizes["seq"], pg, 2, 2, sizes["wt"])))
    split = Mesh(mesh.devices.reshape(tuple(fine.values())), AX)
    rows = P(("seq", "wt"), ("pg", "x", "core"), None)
    mat, vec = P("wt", None), P("wt")
    in_specs = (
        rows, rows, P(("seq", "wt"), ("pg", "x", "core")), P(("seq", "wt"), None),
        mat, vec, mat, mat, vec, mat, vec, vec, vec, mat, vec, mat, vec, vec, vec,
    )
    out_specs = (rows, rows, mat, vec, mat, mat, vec, mat, vec, vec, vec, mat, vec, mat, vec, vec, vec)
    return jax.shard_map(make_body(fine), mesh=split, in_specs=in_specs, out_specs=out_specs, check_vma=False)
```

```python
import functools
import math

import jax
import jax.numpy as jnp
from jax import lax
from jax.experimental import pallas as pl
from jax.experimental.pallas import tpu as pltpu
from jax.sharding import Mesh
from jax.sharding import PartitionSpec as P

NEG = -1000000000.0
EPS = 1e-05
BF = jnp.bfloat16
F32 = jnp.float32
AX = ("seq", "pg", "x", "core", "wt")
VM = pl.BlockSpec(memory_space=pltpu.VMEM)
SM = pl.BlockSpec(memory_space=pltpu.SMEM)
ANY = pl.BlockSpec(memory_space=pl.ANY)
OFFS = (0, 2, 1, 3)
VMEM_LIMIT = 60 * 2**20


def mm(a, b):
    return jnp.dot(a, b, preferred_element_type=F32)


def mm_nt(a, b):
    return lax.dot_general(a, b, (((1,), (1,)), ((), ())), preferred_element_type=F32)


def mm_tn(a, b):
    return lax.dot_general(a, b, (((0,), (0,)), ((), ())), preferred_element_type=F32)


def span(bounds, s, first, last):
    low = jnp.int32(0)
    high = bounds[s, 5]
    for d in range(1, 5):
        low = jnp.where(bounds[s, d] <= first, bounds[s, d], low)
        e = 5 - d
        high = jnp.where(bounds[s, e] > last, bounds[s, e], high)
    return low, high


def attn_fwd_kernel(pg, KC, bounds, idx, t0, t1, t2, t3, bias, w_own, w_z1, w_z2, w_z3, w_y,
                    o_ref, q_out, k_out, v_out, w, m_s, acc_s, sem):
    c, mine, y, z = (idx[i] for i in range(4))
    T = t0.shape[2]
    D = t0.shape[3]
    copies = [(w_own, w.at[z])]
    for k, ref in enumerate((w_z1, w_z2, w_z3)):
        copies.append((ref.at[0:96], w.at[z ^ (k + 1), pl.ds(pl.multiple_of(y * 96, 16), 96)]))
        copies.append((w_y.at[k, 0:96], w.at[z ^ (k + 1), pl.ds(pl.multiple_of((1 - y) * 96, 16), 96)]))
    copies = [pltpu.make_async_copy(a, b, sem.at[i]) for i, (a, b) in enumerate(copies)]
    for cp in copies:
        cp.start()
    for cp in copies:
        cp.wait()
    lane = lax.broadcasted_iota(jnp.int32, (T, 128), 1)
    row = lax.broadcasted_iota(jnp.int32, (T, 128), 0)
    lower = lane < 64
    rel = lane & 63
    zero64 = jnp.zeros((T, 64), F32)

    for g in range(pg):
        for n, src in enumerate((t0, t1, t2, t3)):
            off = OFFS[n]
            place = pl.multiple_of((g * 4 + (c ^ off)) * T, T)
            own = pl.multiple_of((c ^ off) * T, T)
            pos = row + place
            for s in range(2):
                qkv = mm(src[g, s], w[...].reshape(D, 576)) + bias[...]
                qkv = qkv.astype(BF).astype(F32)
                seg = jnp.zeros((T, 128), jnp.int32)
                for d in range(1, 5):
                    seg = seg + (pos >= bounds[s, d]).astype(jnp.int32)
                hot = rel == seg
                q_aug = jnp.where(hot, 1.0, 0.0)
                k_aug = jnp.where(rel < 5, jnp.where(hot, 0.0, NEG), jnp.where(rel < 11, 1.0, 0.0))
                q01, k01, v01, q2v2 = (qkv[:, j * 128 : (j + 1) * 128] for j in range(4))
                k2 = jnp.concatenate([qkv[:, 512:576], zero64], axis=1)
                for h, (k, v) in enumerate(((k01, v01), (k01, v01), (k2, q2v2))):
                    half = ~lower if h == 1 else lower
                    k_out[s, h, pl.ds(place, T)] = jnp.where(half, k, k_aug).astype(BF)
                    half = lower if h == 0 else ~lower
                    v_out[s, h, pl.ds(place, T)] = jnp.where(half, v, 1.0).astype(BF)

                def store_q():
                    for h, q in enumerate((q01, q01, q2v2)):
                        half = ~lower if h == 1 else lower
                        q_out[s, h, pl.ds(own, T)] = jnp.where(half, q * 0.125, q_aug).astype(BF)

                if pg == 1:
                    store_q()
                else:
                    pl.when(mine == g)(store_q)

    def per_tile(si, _):
        s, i = si // 4, si % 4
        here = pl.multiple_of(i * T, T)
        first = (mine * 4 + i) * T
        low, high = span(bounds, s, first, first + T - 1)
        for h in range(3):
            m_s[h] = jnp.full((T, 128), -jnp.inf, F32)
            acc_s[h] = jnp.zeros((T, 128), F32)

        def step(kt, _):
            at = pl.multiple_of(kt * KC, KC)
            for h in range(3):
                sc = mm_nt(q_out[s, h, pl.ds(here, T)], k_out[s, h, pl.ds(at, KC)])
                old = m_s[h]
                parts = [sc[:, j * 128 : (j + 1) * 128] for j in range(KC // 128)]
                top = functools.reduce(jnp.maximum, parts)
                new = jnp.maximum(old, jnp.broadcast_to(jnp.max(top, axis=1, keepdims=True), (T, 128)))
                p = jnp.concatenate([jnp.exp(v - new).astype(BF) for v in parts], axis=1)
                acc_s[h] = acc_s[h] * jnp.exp(old - new) + mm(p, v_out[s, h, pl.ds(at, KC)])
                m_s[h] = new
            return 0

        lax.fori_loop(low // KC, (high + KC - 1) // KC, step, 0)
        outs = []
        for h in range(3):
            acc = acc_s[h]
            turned = pltpu.roll(acc, 64, 1)
            data = lower if h == 0 else ~lower
            total = jnp.where(data, turned, acc)
            outs.append(acc / total)
            lse = m_s[h] + jnp.log(total)
            l1 = lse.astype(BF).astype(F32)
            l2 = (lse - l1).astype(BF).astype(F32)
            l3 = lse - l1 - l2
            at = lane if h == 1 else lane - 64
            q = q_out[s, h, pl.ds(here, T)].astype(F32)
            q = jnp.where(at == 8, -l1, jnp.where(at == 9, -l2, jnp.where(at == 10, -l3, q)))
            q_out[s, h, pl.ds(here, T)] = q.astype(BF)
        o_ref[i, :, pl.ds(pl.multiple_of(s * 128, 128), 128)] = jnp.where(lower, outs[0], outs[1]).astype(BF)

        @pl.when(s == 0)
        def _():
            o_ref[i, :, 256:384] = pltpu.roll(outs[2], 64, 1).astype(BF)

        @pl.when(s == 1)
        def _():
            o_ref[i, :, 256:384] = jnp.where(lower, o_ref[i, :, 256:384].astype(F32), outs[2]).astype(BF)

        return 0

    lax.fori_loop(0, 8, per_tile, 0)


def attn_bwd_kernel(pg, KC, bounds, idx, q_ref, k_ref, v_ref, o_ref, do_ref, d_ref, dq_s, dk_s, dv_s, do_s):
    c, mine = idx[0], idx[1]
    T = o_ref.shape[1]
    lane = lax.broadcasted_iota(jnp.int32, (T, 128), 1)
    lower = lane < 64
    zero = jnp.zeros((T, 128), F32)

    def per_seq(s, _):
        dk_s[...] = jnp.zeros_like(dk_s)
        dv_s[...] = jnp.zeros_like(dv_s)
        live = bounds[s, 4]
        cols = pl.ds(pl.multiple_of(s * 128, 128), 128)

        def per_tile(i, _):
            here = pl.multiple_of(i * T, T)
            first = (mine * 4 + i) * T
            low, high = span(bounds, s, first, first + T - 1)
            high = jnp.minimum(high, live)
            pair = do_ref[i, :, cols].astype(F32)
            third = do_ref[i, :, 256:384].astype(F32)
            third = jnp.where(s == 0, pltpu.roll(third, 64, 1), third)
            o_third = o_ref[i, :, 256:384].astype(F32)
            o_third = jnp.where(s == 0, pltpu.roll(o_third, 64, 1), o_third)
            prod = pair * o_ref[i, :, cols].astype(F32)
            for h in range(3):
                data = lower if h == 0 else ~lower
                full = prod if h < 2 else third * o_third
                delta = jnp.sum(jnp.where(data, full, zero), axis=1, keepdims=True)
                d1 = delta.astype(BF).astype(F32)
                d2 = (delta - d1).astype(BF).astype(F32)
                d3 = delta - d1 - d2
                at = lane - 64 if h == 0 else lane
                aug = jnp.where(at == 8, -d1, jnp.where(at == 9, -d2, jnp.where(at == 10, -d3, zero)))
                do_s[h] = jnp.where(data, pair if h < 2 else third, aug).astype(BF)
                dq_s[h, pl.ds(here, T)] = zero

            def step(kt, _):
                at = pl.multiple_of(kt * KC, KC)
                for h in range(3):
                    q = q_ref[s, h, pl.ds(here, T)]
                    k = k_ref[s, h, pl.ds(at, KC)]
                    d = do_s[h]
                    pt = jnp.exp(mm_nt(k, q))
                    ds = (pt * mm_nt(v_ref[s, h, pl.ds(at, KC)], d)).astype(BF)
                    dv_s[h, pl.ds(at, KC)] += mm(pt.astype(BF), d)
                    dk_s[h, pl.ds(at, KC)] += mm(ds, q)
                    dq_s[h, pl.ds(here, T)] += mm_tn(ds, k)
                return 0

            lax.fori_loop(low // KC, (high + KC - 1) // KC, step, 0)
            return 0

        lax.fori_loop(0, 4, per_tile, 0)
        for g in range(pg):
            for n, off in enumerate(OFFS):
                at = pl.multiple_of((g * 4 + (c ^ off)) * T, T)
                own = pl.multiple_of((c ^ off) * T, T)
                keep = 0.125 if pg == 1 else jnp.where(mine == g, 0.125, 0.0)
                dq = [dq_s[h, pl.ds(own, T)] * keep for h in range(3)]
                dk = [dk_s[h, pl.ds(at, T)] for h in range(3)]
                dv = [dv_s[h, pl.ds(at, T)] for h in range(3)]
                d_ref[g, n, s, :, 0:128] = jnp.where(lower, dq[0], dq[1]).astype(BF)
                d_ref[g, n, s, :, 128:256] = jnp.where(lower, dk[0], dk[1]).astype(BF)
                d_ref[g, n, s, :, 256:384] = jnp.where(lower, dv[0], dv[1]).astype(BF)
                d_ref[g, n, s, :, 384:512] = jnp.where(lower, dq[2], dv[2]).astype(BF)
                d_ref[g, n, s, :, 512:576] = dk[2][:, 0:64].astype(BF)
        return 0

    lax.fori_loop(0, 2, per_seq, 0)


def gelu_parts(u):
    t = 1.0 / (1.0 + (0.3275911 * 0.7071067811865476) * jnp.abs(u))
    e = jnp.exp(-0.5 * u * u)
    poly = t * (
        0.127414796
        + t * (-0.142248368 + t * (0.7107068705 + t * (-0.7265760135 + t * 0.5307027145)))
    )
    tail = poly * e
    cdf = jnp.where(u >= 0, 1.0 - tail, tail)
    return u * cdf, cdf + u * e * 0.3989422804014327


def fold8(v):
    return jnp.sum(v.reshape(v.shape[0] // 8, 8, v.shape[1]), axis=0)


def gather_heads(tiles):
    (pair0, third0), (pair1, third1) = tiles
    lower = lax.broadcasted_iota(jnp.int32, pair0.shape, 1) < 64
    turned = pltpu.roll(pair1, 64, 1)
    return pair0, jnp.where(lower, third0, turned), jnp.where(lower, turned, pltpu.roll(third1, 64, 1))


def ffn_kernel(
    idx, bounds, attn, tok, cot, vec, b1, w_in, w_at, w_out,
    s1a, r2a, c1a, c2a, s1b, r2b, c1b, c2b,
    out, dfirst, dattn, g1o, g1x, g2o, g2x, small, gb1,
    w1, w2, wa, att, hlow, xhat, rstd, acc, act, gp, din, dlow, sums, g1s, g2s, gas, sem, gsem,
):
    c, z, h, y, x, mine = (idx[i] for i in range(6))
    R, D = tok.shape
    T = attn.shape[1]
    FB = b1.shape[2]
    TR = 128
    first_copies = [(w_at, wa.at[z])]
    copies = [(w_in, w1.at[z]), (w_out, w2.at[z])]
    for n, (ra, rb) in enumerate(((s1a, s1b), (r2a, r2b), (c1a, c1b), (c2a, c2b))):
        for k in range(2):
            p = idx[6 + 2 * n + k]
            q, half = p // 2, p % 2
            for kz in range(3):
                zz = z ^ (kz + 1)
                at = pl.ds(pl.multiple_of(half * FB, 128), FB)
                first_copies.append((ra.at[k, kz, 192:240], wa.at[zz, pl.ds(pl.multiple_of(q * 48, 16), 48), at]))
                copies.append((ra.at[k, kz, 0:192], w1.at[zz, :, pl.ds(pl.multiple_of(p * FB, 128), FB)]))
                copies.append((rb.at[k, kz], w2.at[zz, pl.ds(pl.multiple_of(p * 96, 16), 96)]))
    many = len(first_copies)
    first_copies = [pltpu.make_async_copy(a, b, sem.at[i]) for i, (a, b) in enumerate(first_copies)]
    copies = [pltpu.make_async_copy(a, b, sem.at[many + i]) for i, (a, b) in enumerate(copies)]
    for cp in first_copies + copies:
        cp.start()

    b_attn, g1v, s1v, b_out, g2v, s2v = (vec[i : i + 1, :] for i in range(6))
    sums[...] = jnp.zeros_like(sums)

    lower = lax.broadcasted_iota(jnp.int32, (T, 128), 1) < 64
    for s in range(2):
        for g in range(0, 4, 2):
            tiles = []
            for n in (g, g + 1):
                third = attn[n, :, 256:384].astype(F32)
                tiles.append((
                    attn[n, :, s * 128 : (s + 1) * 128].astype(F32),
                    third if s == 0 else pltpu.roll(third, 64, 1),
                ))
            for j, tile in enumerate(gather_heads(tiles)):
                at = g * 192 + j * 128
                att[s * T : (s + 1) * T, at : at + 128] = tile.astype(BF)

    for cp in first_copies:
        cp.wait()

    acc[...] = mm(att[...], wa[...].reshape(D, D))

    def first(r, _):
        rows = pl.ds(pl.multiple_of(r * TR, TR), TR)
        v = acc[rows, :] + tok[rows, :].astype(F32) + b_attn
        mean = jnp.mean(v, axis=-1, keepdims=True)
        v = v - mean
        rs = lax.rsqrt(jnp.mean(v * v, axis=-1, keepdims=True) + EPS)
        xh = v * rs
        xhat[rows, :] = xh
        rstd[rows, :] = jnp.broadcast_to(rs, (TR, 128))
        hid = xh * g1v + s1v
        hlow[rows, :] = hid.astype(BF)
        acc[rows, :] = hid + b_out
        return 0

    lax.fori_loop(0, R // TR, first, 0)
    for cp in copies:
        cp.wait()

    def forward(zz, _):
        for half in range(2):
            j = zz * 2 + half
            w = w1[:, :, pl.ds(pl.multiple_of(j * FB, 128), FB)].reshape(D, FB)
            u = mm(hlow[...], w) + b1[j]
            for r in range(R // TR):
                rows = slice(r * TR, (r + 1) * TR)
                a, d = gelu_parts(u[rows])
                act[j, rows, :] = a.astype(BF)
                gp[j, rows, :] = d.astype(BF)
            acc[...] += mm(act[j], w2[zz, half * FB : (half + 1) * FB, :])
        return 0

    lax.fori_loop(0, 4, forward, 0)

    def second(r, _):
        rows = pl.ds(pl.multiple_of(r * TR, TR), TR)
        s = r // (T // TR)
        v = acc[rows, :]
        mean = jnp.mean(v, axis=-1, keepdims=True)
        v = v - mean
        rs = lax.rsqrt(jnp.mean(v * v, axis=-1, keepdims=True) + EPS)
        xh = v * rs
        out[rows, :] = (xh * g2v + s2v).astype(BF)
        place = (mine * 4 + h) * T + r * TR - s * T
        pos = lax.broadcasted_iota(jnp.int32, (TR, D), 0) + place
        dy = jnp.where(pos < bounds[s, 4], cot[rows, :].astype(F32), 0.0)
        sums[4] += fold8(dy * xh)
        sums[5] += fold8(dy)
        dx = dy * g2v
        m1 = jnp.mean(dx, axis=-1, keepdims=True)
        m2 = jnp.mean(dx * xh, axis=-1, keepdims=True)
        ds = rs * (dx - m1 - xh * m2)
        low = ds.astype(BF)
        dlow[rows, :] = low
        sums[3] += fold8(low.astype(F32))
        acc[rows, :] = ds
        return 0

    lax.fori_loop(0, R // TR, second, 0)

    def place_of(yy, xx, cc):
        dy, dx = yy ^ y, xx ^ x
        return jnp.where(cc == 0, dy, dx), jnp.where(cc == 0, dx, dy)

    def emit(src, own, other, cc, s):
        @pl.when(cc == c)
        def _():
            pltpu.make_async_copy(src, own, s).start()

        @pl.when(cc != c)
        def _():
            pltpu.make_async_copy(src, other, s).start()

    def wait_block(slot):
        pltpu.make_async_copy(g1s.at[slot], g1o.at[0, 0, :, 0:192], gsem.at[slot]).wait()
        for i in range(4):
            pltpu.make_async_copy(g2s.at[slot, i], g2o.at[0, 0, 0], gsem.at[2 + slot * 4 + i]).wait()

    def backward(zz, _):
        for half in range(2):
            j = zz * 2 + half

            @pl.when(zz > 0)
            def _():
                wait_block(half)

            w2j = w2[zz, half * FB : (half + 1) * FB, :]
            w1j = w1[:, :, pl.ds(pl.multiple_of(j * FB, 128), FB)].reshape(D, FB)
            g2s[half] = mm_tn(act[j], dlow[...]).astype(BF).reshape(4, 96, D)
            for i in range(4):
                u, v = place_of(half, i // 2, i % 2)
                emit(g2s.at[half, i], g2o.at[u, v, zz], g2x.at[u, v, zz], i % 2, gsem.at[2 + half * 4 + i])
            da = mm_nt(dlow[...], w2j)
            gsum = jnp.zeros((8, FB), F32)
            for r in range(R // TR):
                rows = slice(r * TR, (r + 1) * TR)
                di = (da[rows] * gp[j, rows, :].astype(F32)).astype(BF)
                din[rows, :] = di
                gsum = gsum + fold8(di.astype(F32))
            gb1[j] = gsum
            acc[...] += mm_nt(din[...], w1j)
            g1s[half] = mm_tn(hlow[...], din[...]).astype(BF).reshape(4, 192, FB)
            u, v = place_of(zz // 2, zz % 2, half)
            emit(g1s.at[half], g1o.at[u, v, :, 0:192], g1x.at[u, v, :, 0:192], half, gsem.at[half])
        return 0

    lax.fori_loop(0, 4, backward, 0)

    def last(r, _):
        rows = pl.ds(pl.multiple_of(r * TR, TR), TR)
        dy = acc[rows, :]
        xh = xhat[rows, :]
        sums[1] += fold8(dy * xh)
        sums[2] += fold8(dy)
        dx = dy * g1v
        m1 = jnp.mean(dx, axis=-1, keepdims=True)
        m2 = jnp.mean(dx * xh, axis=-1, keepdims=True)
        df = rstd[rows, :1] * (dx - m1 - xh * m2)
        dfirst[rows, :] = df
        low = df.astype(BF)
        dlow[rows, :] = low
        sums[0] += fold8(low.astype(F32))
        return 0

    lax.fori_loop(0, R // TR, last, 0)
    acc[...] = mm_nt(dlow[...], wa[...].reshape(D, D))
    for g in range(0, 4, 2):
        thirds = []
        for s in range(2):
            t0, t1, t2 = (acc[s * T : (s + 1) * T, g * 192 + j * 128 : g * 192 + (j + 1) * 128] for j in range(3))
            t1r, t2r = pltpu.roll(t1, 64, 1), pltpu.roll(t2, 64, 1)
            dattn[g, :, s * 128 : (s + 1) * 128] = t0.astype(BF)
            dattn[g + 1, :, s * 128 : (s + 1) * 128] = jnp.where(lower, t1r, t2r).astype(BF)
            thirds.append((t1, t1r, t2, t2r))
        (a1, _, _, a2r), (_, b1r, b2, _) = thirds
        dattn[g, :, 256:384] = jnp.where(lower, a1, b1r).astype(BF)
        dattn[g + 1, :, 256:384] = jnp.where(lower, a2r, b2).astype(BF)
    gas[...] = mm_tn(att[...], dlow[...]).astype(BF).reshape(4, 192, D)
    for p in range(8):
        q, cc = p // 2, p % 2
        u, v = place_of(q // 2, q % 2, cc)
        src = gas.at[:, q * 48 : (q + 1) * 48, cc * FB : (cc + 1) * FB]
        emit(src, g1o.at[u, v, :, 192:240], g1x.at[u, v, :, 192:240], cc, gsem.at[10 + p])
    for i in range(6):
        small[i : i + 1, :] = jnp.sum(sums[i], axis=0, keepdims=True)
    small[6:8, :] = jnp.zeros((2, D), F32)
    for half in range(2):
        wait_block(half)
    for p in range(8):
        cc = p % 2
        src = gas.at[:, (p // 2) * 48 : (p // 2 + 1) * 48, cc * FB : (cc + 1) * FB]
        pltpu.make_async_copy(src, g1o.at[0, 0, :, 192:240], gsem.at[10 + p]).wait()


def grad_qkv_kernel(idx, d, t0, t1, t2, t3, extra, gq, acc):
    h = idx[2]
    R = t0.shape[0]
    for n, t in enumerate((t0, t1, t2, t3)):
        part = mm_tn(t[...], d[n])
        if n == 0:
            acc[...] = part
        else:
            acc[...] += part
    col = jnp.zeros((8, 576), F32)
    for n in range(4):
        col = col + fold8(d[n].astype(F32))
    col = jnp.sum(col, axis=0, keepdims=True)
    top = lax.broadcasted_iota(jnp.int32, (8, 576), 0) == 0
    for z in range(4):
        tail = jnp.where(top & (h == z), col, extra[z])
        for yy in range(2):
            gq[z * 2 + yy, 0:96, :] = acc[z * 192 + yy * 96 : z * 192 + (yy + 1) * 96, :].astype(BF)
            gq[z * 2 + yy, 96:104, :] = tail.astype(BF)


def grad_in_kernel(d, w, dfirst, gi_own, gi_x, gi_b):
    gi_b[0] = mm_nt(d[2], w[...]).astype(BF)
    gi_b[1] = mm_nt(d[3], w[...]).astype(BF)
    gi_x[...] = mm_nt(d[1], w[...])
    gi_own[...] = mm_nt(d[0], w[...]) + dfirst[...]


def out_ffn_kernel(idx, s1a, r2a, c1a, c2a, s1b, r2b, c1b, c2b, g_wi, g_wa, g_wo):
    FB = s1a.shape[2]
    for n, (ra, rb) in enumerate(((s1a, s1b), (r2a, r2b), (c1a, c1b), (c2a, c2b))):
        for k in range(2):
            p = idx[6 + 2 * n + k]
            g_wi[:, pl.ds(pl.multiple_of(p * FB, 128), FB)] = ra[k, 0:192, :].astype(F32)
            rows = pl.ds(pl.multiple_of((p // 2) * 48, 16), 48)
            g_wa[rows, pl.ds(pl.multiple_of((p % 2) * FB, 128), FB)] = ra[k, 192:240, :].astype(F32)
            g_wo[pl.ds(pl.multiple_of(p * 96, 16), 96), :] = rb[k].astype(F32)


def out_qkv_kernel(idx, g, g_wq, g_wk, g_wv, tail):
    z = idx[1]
    lower = lax.broadcasted_iota(jnp.int32, (96, 128), 1) < 64
    for yy in range(2):
        rows = slice(yy * 96, (yy + 1) * 96)
        for h in range(0, 4, 2):
            a, b = g[yy * 4 + h], g[yy * 4 + h + 1]

            def tile(m, i):
                return m[0:96, i * 128 : (i + 1) * 128].astype(F32)

            k2 = [jnp.concatenate([m[0:96, 512:576], jnp.zeros((96, 64), BF)], axis=1).astype(F32) for m in (a, b)]
            q2v2 = [tile(a, 3), tile(b, 3)]
            thirds = (q2v2, k2, [pltpu.roll(v, 64, 1) for v in q2v2])
            for ref, i, (ta, tb) in zip((g_wq, g_wk, g_wv), range(3), thirds):
                turned = pltpu.roll(tile(b, i), 64, 1)
                at = h * 192
                ref[rows, at : at + 128] = tile(a, i)
                ref[rows, at + 128 : at + 256] = jnp.where(lower, ta, turned)
                ref[rows, at + 256 : at + 384] = jnp.where(lower, turned, pltpu.roll(tb, 64, 1))
    total = jnp.zeros((8, 576), F32)
    for h in range(4):
        total = total + g[h, 96:104, :].astype(F32)
    top = lax.broadcasted_iota(jnp.int32, (8, 576), 0) == 0
    tail[...] = jnp.where(top, g[z, 96:104, :].astype(F32), total)


def call(kernel, outs, in_specs, out_specs, scratch=(), flops=0, size=0, name=None):
    return pl.pallas_call(
        kernel,
        out_shape=outs,
        in_specs=in_specs,
        out_specs=out_specs,
        scratch_shapes=list(scratch),
        compiler_params=pltpu.CompilerParams(vmem_limit_bytes=VMEM_LIMIT),
        cost_estimate=pl.CostEstimate(flops=flops, bytes_accessed=size, transcendentals=0),
        name=name,
    )


def make_body(sizes):
    pg = sizes["pg"]
    order = [sizes[a] for a in AX]

    def send(fn, a):
        pairs = []
        for flat in range(math.prod(order)):
            at, rest = [], flat
            for n in reversed(order):
                at.append(rest % n)
                rest //= n
            dest = 0
            for n, v in zip(order, fn(*reversed(at))):
                dest = dest * n + v
            pairs.append((flat, dest))
        return lax.ppermute(a, AX, pairs)

    to_x = functools.partial(send, lambda s, g, x, c, z: (s, g, 1 - x, c, z))
    to_y = functools.partial(send, lambda s, g, x, c, z: (1 - s, g, x, c, z))
    to_core = functools.partial(send, lambda s, g, x, c, z: (s, g, x, 1 - c, z))
    to_z = [functools.partial(send, lambda s, g, x, c, z, k=k: (s, g, x, c, z ^ k)) for k in (1, 2, 3)]
    mix_a = functools.partial(send, lambda s, g, x, c, z: (s, g, 1 - x, c, z) if c == 0 else (1 - s, g, x, c, z))
    mix_b = functools.partial(send, lambda s, g, x, c, z: (1 - s, g, x, c, z) if c == 0 else (s, g, 1 - x, c, z))

    def spread(own):
        s1 = jnp.stack([own, mix_a(own)])
        r2 = mix_b(s1)
        return s1, r2, to_core(s1), to_core(r2)

    def body(
        tokens, cotangent, segment_ids, lengths, w_query, b_query, w_key, w_value, b_value, w_attn, b_attn,
        ln1_gain, ln1_shift, w_inner, b_inner, w_outer, b_outer, ln2_gain, ln2_shift,
    ):
        S, T, D = tokens.shape
        R = S * T
        y, x, c = (lax.axis_index(a) for a in ("seq", "x", "core"))
        mine, z = lax.axis_index("pg"), lax.axis_index("wt")
        h = x * 2 + c
        p = y * 4 + h
        L = 4 * pg * T
        FB = w_inner.shape[1] // 8

        ends = [lengths[:, :1]]
        for d in range(1, 4):
            ends.append(ends[-1] + lengths[:, d : d + 1])
        bounds = jnp.concatenate(
            [jnp.zeros_like(ends[0])] + ends + [jnp.full_like(ends[0], L), jnp.zeros((S, 2), jnp.int32)], axis=1
        ).astype(jnp.int32)
        a_of = jnp.where(c == 0, 2, 4)
        other = p ^ 1
        mates = [p, p ^ a_of, p ^ (6 - a_of), p ^ 6, other, other ^ (6 - a_of), other ^ a_of, other ^ 6]
        idx_a = jnp.stack([h, mine, y, z]).astype(jnp.int32)
        idx = jnp.stack([c, z, h, y, x, mine] + mates).astype(jnp.int32)

        def cols(w):
            return lax.dynamic_slice_in_dim(w, h * 192, 192, 1)

        wq, wk, wv = cols(w_query), cols(w_key), cols(w_value)
        w_own = jnp.concatenate([wq[:, :128], wk[:, :128], wv[:, :128], wq[:, 128:], wv[:, 128:], wk[:, 128:]], axis=1)
        none = jnp.zeros((128,), BF)
        rest = [b_attn, ln1_gain, ln1_shift, b_outer, ln2_gain, ln2_shift, b_inner, jnp.zeros((384 + 3 * 576,), BF)]
        smalls = jnp.concatenate(
            [b_query[:128], none, b_value[:128], b_query[128:], b_value[128:], none[:64]] + rest
        ).reshape(8, 576)
        pack = jnp.concatenate([lax.dynamic_slice_in_dim(w_own, y * 96, 96, 0), smalls], axis=0)
        w_z = [f(pack) for f in to_z]
        tok_x = to_x(tokens)
        tok_c = to_core(tokens)
        w_y = to_y(jnp.stack(w_z))
        tok_xc = to_core(tok_x)

        piece1 = jnp.concatenate(
            [lax.dynamic_slice_in_dim(w_inner, p * FB, FB, 1), lax.dynamic_slice(w_attn, ((p // 2) * 48, c * FB), (48, FB))],
            axis=0,
        )
        piece2 = lax.dynamic_slice_in_dim(w_outer, p * 96, 96, 0)
        one = spread(jnp.stack([f(piece1) for f in to_z]))
        two = spread(jnp.stack([f(piece2) for f in to_z]))

        sm = jnp.stack([smalls] + [v[96:] for v in w_z]).astype(F32).reshape(4, 8 * 576)
        sm = jnp.where((z & 1) == 0, sm, sm[jnp.array([1, 0, 3, 2])])
        sm = jnp.where((z & 2) == 0, sm, sm[jnp.array([2, 3, 0, 1])])
        bias = lax.dynamic_slice_in_dim(sm, h, 1, 0)[:, :576]
        vec = sm[:, 576:1728].reshape(4, 6, 192).transpose(1, 0, 2).reshape(6, D)
        vec = jnp.concatenate([vec, jnp.zeros((2, D), F32)], axis=0)
        b1 = sm[:, 1728:2496].reshape(8, 1, FB)

        toks = [tokens[None], tok_x[None], tok_c[None], tok_xc[None]]
        if pg > 1:
            toks = [lax.all_gather(t, "pg", axis=0, tiled=True) for t in toks]
        head = jax.ShapeDtypeStruct((S, 3, L, 128), BF)
        o, q_aug, k_aug, v_aug, w_qkv = call(
            functools.partial(attn_fwd_kernel, pg, 1024),
            (
                jax.ShapeDtypeStruct((4, T, 384), BF), jax.ShapeDtypeStruct((S, 3, 4 * T, 128), BF), head, head,
                jax.ShapeDtypeStruct((4, 192, 576), BF),
            ),
            [SM, SM] + [VM] * 5 + [ANY] * 5,
            (VM,) * 5,
            [pltpu.VMEM((3, T, 128), F32), pltpu.VMEM((3, T, 128), F32), pltpu.SemaphoreType.DMA((7,))],
            flops=20 * 10**9, size=10 * 2**20, name="attn_fwd",
        )(bounds, idx_a, *toks, bias, w_own, *w_z, w_y)
        w_qkv = w_qkv.reshape(D, 576)
        attn = lax.all_to_all(o, ("x", "core"), 0, 0, tiled=True)

        g1s = jax.ShapeDtypeStruct((2, 2, 4, 240, FB), BF)
        g2s = jax.ShapeDtypeStruct((2, 2, 4, 96, D), BF)
        layer_out, d_first, d_attn, g1o, g1x, g2o, g2x, small, gb1 = call(
            ffn_kernel,
            (
                jax.ShapeDtypeStruct((R, D), BF), jax.ShapeDtypeStruct((R, D), F32), jax.ShapeDtypeStruct((4, T, 384), BF),
                g1s, g1s, g2s, g2s, jax.ShapeDtypeStruct((8, D), F32), jax.ShapeDtypeStruct((8, 8, FB), F32),
            ),
            [SM, SM] + [VM] * 5 + [ANY] * 11,
            (VM, VM, VM, ANY, ANY, ANY, ANY, VM, VM),
            [
                pltpu.VMEM((4, 192, 8 * FB), BF),
                pltpu.VMEM((4, 2 * FB, D), BF),
                pltpu.VMEM((4, 192, D), BF),
                pltpu.VMEM((R, D), BF),
                pltpu.VMEM((R, D), BF),
                pltpu.VMEM((R, D), F32),
                pltpu.VMEM((R, 128), F32),
                pltpu.VMEM((R, D), F32),
                pltpu.VMEM((8, R, FB), BF),
                pltpu.VMEM((8, R, FB), BF),
                pltpu.VMEM((R, FB), BF),
                pltpu.VMEM((R, D), BF),
                pltpu.VMEM((8, 8, D), F32),
                pltpu.VMEM((2, 4, 192, FB), BF),
                pltpu.VMEM((2, 4, 96, D), BF),
                pltpu.VMEM((4, 192, D), BF),
                pltpu.SemaphoreType.DMA((75,)),
                pltpu.SemaphoreType.DMA((18,)),
            ],
            flops=30 * 10**9, size=20 * 2**20, name="ffn",
        )(
            idx, bounds, attn, tokens.reshape(R, D), cotangent.reshape(R, D), vec, b1, w_inner, w_attn, w_outer, *one, *two
        )

        d_o = lax.all_to_all(d_attn, ("x", "core"), 0, 0, tiled=True)

        def add(*parts):
            return sum(v.astype(F32) for v in parts)

        def reduce(own, other):
            got = to_core(other)
            first = mix_b(add(own[1], got[1]).astype(BF))
            second = mix_a(add(own[0, 1], got[0, 1], first[1]).astype(BF))

            def chunk(k):
                return add(*(lax.dynamic_index_in_dim(v, z ^ k, 0, False) for v in (own[0, 0], got[0, 0], first[0], second)))

            sent = [f(chunk(k + 1).astype(BF)) for k, f in enumerate(to_z)]
            v = add(chunk(0), *sent)
            if pg > 1:
                v = lax.psum(v, "pg")
            return spread(v.astype(BF))

        g2 = reduce(g2o, g2x)
        g1 = reduce(g1o, g1x)
        g_wi, g_wa, g_wo = call(
            out_ffn_kernel,
            (jax.ShapeDtypeStruct((192, 8 * FB), F32), jax.ShapeDtypeStruct((192, D), F32), jax.ShapeDtypeStruct((D, D), F32)),
            [SM] + [VM] * 8, (VM,) * 3, size=8 * 2**20, name="out_ffn",
        )(idx, *g1, *g2)

        d = call(
            functools.partial(attn_bwd_kernel, pg, 512),
            jax.ShapeDtypeStruct((pg, 4, S, T, 576), BF),
            [SM, SM] + [VM] * 5,
            VM,
            [pltpu.VMEM((3, 4 * T, 128), F32), pltpu.VMEM((3, L, 128), F32), pltpu.VMEM((3, L, 128), F32), pltpu.VMEM((3, T, 128), BF)],
            flops=25 * 10**9, size=10 * 2**20, name="attn_bwd",
        )(bounds, idx_a, q_aug, k_aug, v_aug, o, d_o)
        if pg > 1:
            d = lax.psum_scatter(d, "pg", scatter_dimension=0, tiled=True)
        d = d.reshape(4, R, 576)

        extra = jnp.concatenate(
            [
                small[:6].reshape(6, 4, 192).transpose(1, 0, 2).reshape(4, 6 * 192),
                jnp.sum(gb1, axis=1).reshape(4, 2 * FB),
                jnp.zeros((4, 384 + 3 * 576), F32),
            ],
            axis=1,
        ).reshape(4, 7, 576)
        extra = jnp.concatenate([jnp.zeros((4, 1, 576), F32), extra], axis=1)
        gq = call(
            grad_qkv_kernel, jax.ShapeDtypeStruct((8, 104, 576), BF), [SM] + [VM] * 6, VM,
            [pltpu.VMEM((D, 576), F32)], flops=2 * 10**9, size=6 * 2**20, name="grad_qkv",
        )(idx, d, *(t.reshape(R, D) for t in (tokens, tok_x, tok_c, tok_xc)), extra)
        gi_own, gi_x, gi_b = call(
            grad_in_kernel,
            (jax.ShapeDtypeStruct((R, D), F32), jax.ShapeDtypeStruct((R, D), F32), jax.ShapeDtypeStruct((2, R, D), BF)),
            [VM] * 3, (VM,) * 3, flops=2 * 10**9, size=10 * 2**20, name="grad_in",
        )(d, w_qkv, d_first)
        if pg > 1:
            gq = lax.psum(gq, "pg")
        gq = lax.all_to_all(gq, ("wt", "seq"), 0, 0, tiled=True)
        gi_b = to_core(gi_b)
        gi_x = to_x(add(gi_x, gi_b[1]).astype(BF))
        grad_input = add(gi_own, gi_b[0], gi_x).astype(BF).reshape(tokens.shape)
        gq = jnp.sum(gq.astype(F32), axis=0).astype(BF)
        gq = lax.all_to_all(jnp.broadcast_to(gq[None], (8, 104, 576)), ("seq", "x", "core"), 0, 0, tiled=True)
        mat = jax.ShapeDtypeStruct((192, D), F32)
        g_wq, g_wk, g_wv, tail = call(
            out_qkv_kernel, (mat, mat, mat, jax.ShapeDtypeStruct((8, 576), F32)), [SM, VM], (VM,) * 4,
            size=3 * 2**20, name="out_qkv",
        )(idx, gq)
        g_bq = jnp.concatenate([tail[0, 0:128], tail[0, 384:448]])
        g_bv = jnp.concatenate([tail[0, 256:384], tail[0, 448:512]])
        t = tail[1:].reshape(-1)
        six = [t[i * 192 : (i + 1) * 192] for i in range(6)]
        return (
            layer_out.reshape(tokens.shape), grad_input,
            g_wq, g_bq, g_wk, g_wv, g_bv, g_wa, six[0], six[1], six[2], g_wi, t[1152 : 1152 + 2 * FB], g_wo, six[3],
            six[4], six[5],
        )

    return body


def solution(mesh):
    sizes = dict(mesh.shape)
    pg = sizes["ctx"] // 4
    fine = dict(zip(AX, (sizes["seq"], pg, 2, 2, sizes["wt"])))
    split = Mesh(mesh.devices.reshape(tuple(fine.values())), AX)
    rows = P(("seq", "wt"), ("pg", "x", "core"), None)
    mat, vec = P("wt", None), P("wt")
    in_specs = (
        rows, rows, P(("seq", "wt"), ("pg", "x", "core")), P(("seq", "wt"), None),
        mat, vec, mat, mat, vec, mat, vec, vec, vec, mat, vec, mat, vec, vec, vec,
    )
    out_specs = (rows, rows, mat, vec, mat, mat, vec, mat, vec, vec, vec, mat, vec, mat, vec, vec, vec)
    return jax.shard_map(make_body(fine), mesh=split, in_specs=in_specs, out_specs=out_specs, check_vma=False)
```

```python
import functools
import math

import jax
import jax.numpy as jnp
from jax import lax
from jax.experimental import pallas as pl
from jax.experimental.pallas import tpu as pltpu
from jax.sharding import Mesh
from jax.sharding import PartitionSpec as P

NEG = -1000000000.0
EPS = 1e-05
BF = jnp.bfloat16
F32 = jnp.float32
AX = ("seq", "pg", "x", "core", "wt")
VM = pl.BlockSpec(memory_space=pltpu.VMEM)
SM = pl.BlockSpec(memory_space=pltpu.SMEM)
ANY = pl.BlockSpec(memory_space=pl.ANY)
OFFS = (0, 2, 1, 3)
VMEM_LIMIT = 60 * 2**20


def mm(a, b):
    return jnp.dot(a, b, preferred_element_type=F32)


def mm_nt(a, b):
    return lax.dot_general(a, b, (((1,), (1,)), ((), ())), preferred_element_type=F32)


def mm_tn(a, b):
    return lax.dot_general(a, b, (((0,), (0,)), ((), ())), preferred_element_type=F32)


def fold8(v):
    return jnp.sum(v.reshape(v.shape[0] // 8, 8, v.shape[1]), axis=0)


def limits(lengths, s, length):
    out = [jnp.int32(0)]
    for d in range(4):
        out.append(out[-1] + lengths[s, d])
    return out + [jnp.int32(length)]


def span(bounds, first, last):
    low, high = bounds[0], bounds[5]
    for d in range(1, 5):
        low = jnp.where(bounds[d] <= first, bounds[d], low)
        high = jnp.where(bounds[5 - d] > last, bounds[5 - d], high)
    return low, high


def prep_kernel(idx, wq, wk, wv, w_at, w_in, w_out, *rest):
    vecs, (w_own, pack, piece1, piece2) = rest[:9], rest[9:]
    c, h, y = idx[0], idx[2], idx[3]
    p = y * 4 + h
    FB = piece1.shape[1]
    for head in range(4):

        @pl.when(h == head)
        def _():
            a = head * 192
            for i, w in enumerate((wq, wk, wv)):
                w_own[0:192, i * 128 : (i + 1) * 128] = w[:, a : a + 128]
            w_own[0:192, 384:448] = wq[:, a + 128 : a + 192]
            w_own[0:192, 448:512] = wv[:, a + 128 : a + 192]
            w_own[0:192, 512:576] = wk[:, a + 128 : a + 192]

    bq, bv = (v[...].reshape(1, 192) for v in vecs[:2])
    w_own[192:200, :] = jnp.zeros((8, 576), BF)
    w_own[192:193, 0:128] = bq[:, 0:128]
    w_own[192:193, 256:384] = bv[:, 0:128]
    w_own[192:193, 384:448] = bq[:, 128:192]
    w_own[192:193, 448:512] = bv[:, 128:192]
    pack[0:96, :] = w_own[pl.ds(pl.multiple_of(y * 96, 16), 96), :]
    pack[96:104, :] = w_own[192:200, :]
    piece1[0:192, :] = w_in[:, pl.ds(pl.multiple_of(p * FB, 128), FB)]
    piece1[192:240, :] = w_at[pl.ds(pl.multiple_of((p // 2) * 48, 16), 48), pl.ds(pl.multiple_of(c * FB, 128), FB)]
    piece1[240:256, :] = jnp.zeros((16, FB), BF)
    for i, v in enumerate(vecs[:8]):
        piece1[240 + i : 241 + i, 0:192] = v[...].reshape(1, 192)
    for i in range(4):
        piece1[248 + i : 249 + i, 0:192] = vecs[8][i * 192 : (i + 1) * 192].reshape(1, 192)
    piece2[...] = w_out[pl.ds(pl.multiple_of(c * FB + (p // 2) * 96, 16), 96), :]


def qkv_kernel(pg, lengths, idx, *refs):
    toks, (w_own, w_z1, w_z2, w_z3, w_y, q_out, k_out, v_out, w, bs, sem) = refs[:4], refs[4:]
    z, c, y, mine = idx[1], idx[2], idx[3], idx[5]
    T, D = toks[0].shape[2:]
    copies = [(w_own.at[0:192], w.at[z]), (w_own.at[192:200], bs.at[0])]
    for k, ref in enumerate((w_z1, w_z2, w_z3)):
        copies.append((ref.at[0:96], w.at[z ^ (k + 1), pl.ds(pl.multiple_of(y * 96, 16), 96)]))
        copies.append((ref.at[96:104], bs.at[k + 1]))
        copies.append((w_y.at[k, 0:96], w.at[z ^ (k + 1), pl.ds(pl.multiple_of((1 - y) * 96, 16), 96)]))
    copies = [pltpu.make_async_copy(a, b, sem.at[i]) for i, (a, b) in enumerate(copies)]
    for cp in copies:
        cp.start()
    for cp in copies:
        cp.wait()
    lane = lax.broadcasted_iota(jnp.int32, (T, 128), 1)
    row = lax.broadcasted_iota(jnp.int32, (T, 128), 0)
    lower = lane < 64
    rel = lane & 63
    zero64 = jnp.zeros((T, 64), F32)

    bias = bs[c ^ z, 0:1, :].astype(F32)
    for g in range(pg):
        for n, off in enumerate(OFFS):
            place = pl.multiple_of((g * 4 + (c ^ off)) * T, T)
            own = pl.multiple_of((c ^ off) * T, T)
            pos = row + place
            for s in range(2):
                qkv = mm(toks[n][g, s], w[...].reshape(D, 576)) + bias
                qkv = qkv.astype(BF).astype(F32)
                seg = jnp.zeros((T, 128), jnp.int32)
                for start in limits(lengths, s, 0)[1:5]:
                    seg = seg + (pos >= start).astype(jnp.int32)
                hot = rel == seg
                q_aug = jnp.where(hot, 1.0, 0.0)
                k_aug = jnp.where(rel < 5, jnp.where(hot, 0.0, NEG), jnp.where(rel < 11, 1.0, 0.0))
                q01, k01, v01, q2v2 = (qkv[:, j * 128 : (j + 1) * 128] for j in range(4))
                k2 = jnp.concatenate([qkv[:, 512:576], zero64], axis=1)
                for h, (k, v) in enumerate(((k01, v01), (k01, v01), (k2, q2v2))):
                    half = ~lower if h == 1 else lower
                    k_out[s, h, pl.ds(place, T)] = jnp.where(half, k, k_aug).astype(BF)
                    half = lower if h == 0 else ~lower
                    v_out[s, h, pl.ds(place, T)] = jnp.where(half, v, 1.0).astype(BF)

                def store_q():
                    for h, q in enumerate((q01, q01, q2v2)):
                        half = ~lower if h == 1 else lower
                        q_out[s, h, pl.ds(own, T)] = jnp.where(half, q * 0.125, q_aug).astype(BF)

                if pg == 1:
                    store_q()
                else:
                    pl.when(mine == g)(store_q)


def attn_fwd_kernel(KC, lengths, idx, q_ref, k_ref, v_ref, o_ref, q_out, m_s, acc_s):
    mine = idx[5]
    T, L = o_ref.shape[1], k_ref.shape[2]
    lane = lax.broadcasted_iota(jnp.int32, (T, 128), 1)
    lower = lane < 64

    def per_tile(si, _):
        s, i = si // 4, si % 4
        here = pl.multiple_of(i * T, T)
        first = (mine * 4 + i) * T
        low, high = span(limits(lengths, s, L), first, first + T - 1)
        for h in range(3):
            m_s[h] = jnp.full((T, 128), -jnp.inf, F32)
            acc_s[h] = jnp.zeros((T, 128), F32)

        def step(kt, _):
            at = pl.multiple_of(kt * KC, KC)
            for h in range(3):
                sc = mm_nt(q_ref[s, h, pl.ds(here, T)], k_ref[s, h, pl.ds(at, KC)])
                old = m_s[h]
                parts = [sc[:, j * 128 : (j + 1) * 128] for j in range(KC // 128)]
                top = functools.reduce(jnp.maximum, parts)
                new = jnp.maximum(old, jnp.broadcast_to(jnp.max(top, axis=1, keepdims=True), (T, 128)))
                p = jnp.concatenate([jnp.exp(v - new).astype(BF) for v in parts], axis=1)
                acc_s[h] = acc_s[h] * jnp.exp(old - new) + mm(p, v_ref[s, h, pl.ds(at, KC)])
                m_s[h] = new
            return 0

        lax.fori_loop(low // KC, (high + KC - 1) // KC, step, 0)
        outs = []
        for h in range(3):
            acc = acc_s[h]
            turned = pltpu.roll(acc, 64, 1)
            data = lower if h == 0 else ~lower
            total = jnp.where(data, turned, acc)
            outs.append(acc / total)
            lse = m_s[h] + jnp.log(total)
            l1 = lse.astype(BF).astype(F32)
            l2 = (lse - l1).astype(BF).astype(F32)
            l3 = lse - l1 - l2
            at = lane if h == 1 else lane - 64
            q = q_ref[s, h, pl.ds(here, T)].astype(F32)
            q = jnp.where(at == 8, -l1, jnp.where(at == 9, -l2, jnp.where(at == 10, -l3, q)))
            q_out[s, h, pl.ds(here, T)] = q.astype(BF)
        o_ref[i, :, pl.ds(pl.multiple_of(s * 128, 128), 128)] = jnp.where(lower, outs[0], outs[1]).astype(BF)

        @pl.when(s == 0)
        def _():
            o_ref[i, :, 256:384] = pltpu.roll(outs[2], 64, 1).astype(BF)

        @pl.when(s == 1)
        def _():
            o_ref[i, :, 256:384] = jnp.where(lower, o_ref[i, :, 256:384].astype(F32), outs[2]).astype(BF)

        return 0

    lax.fori_loop(0, 8, per_tile, 0)


def attn_bwd_kernel(pg, KC, s, lengths, idx, q_ref, k_ref, v_ref, o_ref, do_ref, *rest):
    *rest, dq_s, dk_s, dv_s, do_s, d_ref, gq_s = rest
    if s == 1:
        rest = (*rest, gq_s)
    if pg > 1:
        d_ref = rest[0]
    c, mine = idx[2], idx[5]
    T, L = o_ref.shape[1], k_ref.shape[2]
    bounds = limits(lengths, s, L)
    lane = lax.broadcasted_iota(jnp.int32, (T, 128), 1)
    lower = lane < 64
    zero = jnp.zeros((T, 128), F32)

    dk_s[...] = jnp.zeros_like(dk_s)
    dv_s[...] = jnp.zeros_like(dv_s)
    live = bounds[4]
    cols = slice(s * 128, (s + 1) * 128)

    def per_tile(i, _):
        here = pl.multiple_of(i * T, T)
        first = (mine * 4 + i) * T
        low, high = span(bounds, first, first + T - 1)
        high = jnp.minimum(high, live)
        pair = do_ref[i, :, cols].astype(F32)
        third = do_ref[i, :, 256:384].astype(F32)
        if s == 0:
            third = pltpu.roll(third, 64, 1)
        o_third = o_ref[i, :, 256:384].astype(F32)
        if s == 0:
            o_third = pltpu.roll(o_third, 64, 1)
        prod = pair * o_ref[i, :, cols].astype(F32)
        for h in range(3):
            data = lower if h == 0 else ~lower
            full = prod if h < 2 else third * o_third
            delta = jnp.sum(jnp.where(data, full, zero), axis=1, keepdims=True)
            d1 = delta.astype(BF).astype(F32)
            d2 = (delta - d1).astype(BF).astype(F32)
            d3 = delta - d1 - d2
            at = lane - 64 if h == 0 else lane
            aug = jnp.where(at == 8, -d1, jnp.where(at == 9, -d2, jnp.where(at == 10, -d3, zero)))
            do_s[h] = jnp.where(data, pair if h < 2 else third, aug).astype(BF)
            dq_s[h, pl.ds(here, T)] = zero

        def step(kt, _):
            at = pl.multiple_of(kt * KC, KC)
            for h in range(3):
                q = q_ref[0, h, pl.ds(here, T)]
                k = k_ref[0, h, pl.ds(at, KC)]
                d = do_s[h]
                pt = jnp.exp(mm_nt(k, q))
                ds = (pt * mm_nt(v_ref[0, h, pl.ds(at, KC)], d)).astype(BF)
                dv_s[h, pl.ds(at, KC)] += mm(pt.astype(BF), d)
                dk_s[h, pl.ds(at, KC)] += mm(ds, q)
                dq_s[h, pl.ds(here, T)] += mm_tn(ds, k)
            return 0

        lax.fori_loop(low // KC, (high + KC - 1) // KC, step, 0)
        return 0

    lax.fori_loop(0, 4, per_tile, 0)
    for g in range(pg):
        for n, off in enumerate(OFFS):
            at = pl.multiple_of((g * 4 + (c ^ off)) * T, T)
            own = pl.multiple_of((c ^ off) * T, T)
            keep = 0.125 if pg == 1 else jnp.where(mine == g, 0.125, 0.0)
            dq = [dq_s[h, pl.ds(own, T)] * keep for h in range(3)]
            dk = [dk_s[h, pl.ds(at, T)] for h in range(3)]
            dv = [dv_s[h, pl.ds(at, T)] for h in range(3)]
            d_ref[g, n, :, 0:128] = jnp.where(lower, dq[0], dq[1]).astype(BF)
            d_ref[g, n, :, 128:256] = jnp.where(lower, dk[0], dk[1]).astype(BF)
            d_ref[g, n, :, 256:384] = jnp.where(lower, dv[0], dv[1]).astype(BF)
            d_ref[g, n, :, 384:512] = jnp.where(lower, dq[2], dv[2]).astype(BF)
            d_ref[g, n, :, 512:576] = dk[2][:, 0:64].astype(BF)
    if pg == 1:
        products(s, idx, d_ref, *rest)


def products(s, idx, d, w, dfirst, t0, t1, t2, t3, *rest):
    if s == 0:
        gq, gi_own, gi_x, gi_b = rest
    else:
        prev, extra, gq_own, gq_other, gi_own, gi_x, gi_b, gq = rest
    zw, h, y = idx[1], idx[2], idx[3]
    D = w.shape[0]
    for n in range(2):
        gi_b[n] = mm_nt(d[0, n + 2], w[...]).astype(BF)
    gi_x[...] = mm_nt(d[0, 1], w[...])
    gi_own[...] = mm_nt(d[0, 0], w[...]) + dfirst[...]
    toks = (t0, t1, t2, t3)
    acc = sum(mm_tn(t[0], d[0, n]) for n, t in enumerate(toks))
    col = sum(fold8(d[0, n].astype(F32)) for n in range(4))
    if s == 0:
        gq[0:D, :] = acc
        gq[D : D + 8, :] = col
        return
    gq[0:D, :] = acc + prev[0:D, :]
    col = jnp.sum(col + prev[D : D + 8, :], axis=0, keepdims=True)
    top = lax.broadcasted_iota(jnp.int32, (8, 576), 0) == 0
    for k in range(4):
        z = zw ^ k
        tail = jnp.where(top & (h == z), col, extra[z]).astype(BF)
        for ref, yy in ((gq_own, y), (gq_other, 1 - y)):
            ref[k, 0:96, :] = gq[pl.ds(pl.multiple_of(z * 192 + yy * 96, 8), 96), :].astype(BF)
            ref[k, 96:104, :] = tail


def gelu_parts(u):
    t = 1.0 / (1.0 + (0.3275911 * 0.7071067811865476) * jnp.abs(u))
    e = jnp.exp(-0.5 * u * u)
    poly = t * (
        0.127414796
        + t * (-0.142248368 + t * (0.7107068705 + t * (-0.7265760135 + t * 0.5307027145)))
    )
    tail = poly * e
    cdf = jnp.where(u >= 0, 1.0 - tail, tail)
    return u * cdf, cdf + u * e * 0.3989422804014327


def gather_heads(tiles):
    (pair0, third0), (pair1, third1) = tiles
    lower = lax.broadcasted_iota(jnp.int32, pair0.shape, 1) < 64
    turned = pltpu.roll(pair1, 64, 1)
    return pair0, jnp.where(lower, third0, turned), jnp.where(lower, turned, pltpu.roll(third1, 64, 1))


def ffn_kernel(
    idx, lengths, attn, tok, cot, sm_own, w_in, w_at, w_out,
    s1a, r2a, c1a, c2a, s1b, r2b, c1b, c2b,
    out, dfirst, dattn, sent, kept, extra,
    w1, w2, wa, sm, b1, att, hlow, xhat, rstd, acc, act, gp, dlow, sums, sem, osem,
):
    c, z, h, y, x, mine = (idx[i] for i in range(6))
    R, D = tok.shape
    T = attn.shape[1]
    FB = w_in.shape[1] // 8
    TR = 128
    first_copies = [(w_at, wa.at[z]), (sm_own.at[240:256], sm.at[0])]
    first_copies += [(s1a.at[0, k, 240:256], sm.at[k + 1]) for k in range(3)]
    copies = [(w_in, w1.at[z]), (w_out, w2.at[z])]
    for n, (ra, rb) in enumerate(((s1a, s1b), (r2a, r2b), (c1a, c1b), (c2a, c2b))):
        for k in range(2):
            p = idx[6 + 2 * n + k]
            q, half = p // 2, p % 2
            for kz in range(3):
                zz = z ^ (kz + 1)
                at = pl.ds(pl.multiple_of(half * FB, 128), FB)
                first_copies.append((ra.at[k, kz, 192:240], wa.at[zz, pl.ds(pl.multiple_of(q * 48, 16), 48), at]))
                copies.append((ra.at[k, kz, 0:192], w1.at[zz, :, pl.ds(pl.multiple_of(p * FB, 128), FB)]))
                copies.append((rb.at[k, kz], w2.at[zz, pl.ds(pl.multiple_of(half * FB + q * 96, 16), 96)]))
    many = len(first_copies)
    first_copies = [pltpu.make_async_copy(a, b, sem.at[i]) for i, (a, b) in enumerate(first_copies)]
    copies = [pltpu.make_async_copy(a, b, sem.at[many + i]) for i, (a, b) in enumerate(copies)]
    for cp in first_copies + copies:
        cp.start()

    sums[...] = jnp.zeros_like(sums)
    extra[...] = jnp.zeros_like(extra)

    lower = lax.broadcasted_iota(jnp.int32, (T, 128), 1) < 64
    for s in range(2):
        for g in range(0, 4, 2):
            tiles = []
            for n in (g, g + 1):
                third = attn[n, :, 256:384].astype(F32)
                tiles.append((
                    attn[n, :, s * 128 : (s + 1) * 128].astype(F32),
                    third if s == 0 else pltpu.roll(third, 64, 1),
                ))
            for j, tile in enumerate(gather_heads(tiles)):
                at = g * 192 + j * 128
                att[s * T : (s + 1) * T, at : at + 128] = tile.astype(BF)

    for cp in first_copies:
        cp.wait()

    def whole(i):
        return jnp.concatenate([sm[k ^ z, i : i + 1, 0:192].astype(F32) for k in range(4)], axis=1)

    b_attn, g1v, s1v, b_out, g2v, s2v = (whole(i) for i in range(2, 8))
    for k in range(4):
        row = jnp.concatenate([sm[k ^ z, i : i + 1, 0:192].astype(F32) for i in range(8, 12)], axis=1)
        for half in range(2):
            b1[2 * k + half, 0:1, :] = row[:, half * FB : (half + 1) * FB]

    acc[...] = mm(att[...], wa[...].reshape(D, D))

    def first(r, _):
        rows = pl.ds(pl.multiple_of(r * TR, TR), TR)
        v = acc[rows, :] + tok[rows, :].astype(F32) + b_attn
        mean = jnp.mean(v, axis=-1, keepdims=True)
        v = v - mean
        rs = lax.rsqrt(jnp.mean(v * v, axis=-1, keepdims=True) + EPS)
        xh = v * rs
        xhat[rows, :] = xh
        rstd[rows, :] = jnp.broadcast_to(rs, (TR, 128))
        hid = xh * g1v + s1v
        hlow[rows, :] = hid.astype(BF)
        acc[rows, :] = hid + b_out
        return 0

    lax.fori_loop(0, R // TR, first, 0)
    for cp in copies:
        cp.wait()

    def keep(src, i, cc, at):
        to = pl.ds(pl.multiple_of(i * FB, 128), FB)

        @pl.when(c == cc)
        def _():
            pltpu.make_async_copy(src, kept.at[:, to], osem.at[at]).start()

        @pl.when(c != cc)
        def _():
            pltpu.make_async_copy(src, sent.at[:, to], osem.at[at]).start()

    def kept_all(first, count):
        for i in range(first, first + count):
            pltpu.make_async_copy(act.at[:, 0:FB], kept.at[:, 0:FB], osem.at[i]).wait()

    def forward(zz, _):
        cols = pl.ds(pl.multiple_of(zz * D, 128), D)
        u = mm(hlow[...], w1[:, :, cols].reshape(D, D)) + jnp.concatenate([b1[2 * zz, 0:1, :], b1[2 * zz + 1, 0:1, :]], axis=1)
        for r in range(R // TR):
            rows = slice(r * TR, (r + 1) * TR)
            a, d = gelu_parts(u[rows])
            act[rows, cols] = a.astype(BF)
            gp[rows, cols] = d.astype(BF)
        acc[...] += mm(act[:, cols], w2[zz])
        for half in range(2):
            src = act.at[:, pl.ds(pl.multiple_of(zz * D + half * FB, 128), FB)]
            keep(src, zz, half, 2 * zz + half)
        return 0

    lax.fori_loop(0, 4, forward, 0)

    def second(r, _):
        rows = pl.ds(pl.multiple_of(r * TR, TR), TR)
        s = r // (T // TR)
        v = acc[rows, :]
        mean = jnp.mean(v, axis=-1, keepdims=True)
        v = v - mean
        rs = lax.rsqrt(jnp.mean(v * v, axis=-1, keepdims=True) + EPS)
        xh = v * rs
        out[rows, :] = (xh * g2v + s2v).astype(BF)
        place = (mine * 4 + h) * T + r * TR - s * T
        pos = lax.broadcasted_iota(jnp.int32, (TR, D), 0) + place
        dy = jnp.where(pos < limits(lengths, s, 0)[4], cot[rows, :].astype(F32), 0.0)
        sums[4] += fold8(dy * xh)
        sums[5] += fold8(dy)
        dx = dy * g2v
        m1 = jnp.mean(dx, axis=-1, keepdims=True)
        m2 = jnp.mean(dx * xh, axis=-1, keepdims=True)
        ds = rs * (dx - m1 - xh * m2)
        low = ds.astype(BF)
        dlow[rows, :] = low
        sums[3] += fold8(low.astype(F32))
        acc[rows, :] = ds
        return 0

    lax.fori_loop(0, R // TR, second, 0)

    kept_all(0, 8)
    shared = [(att, 9), (hlow, 11), (dlow, 13)]
    shared = [pltpu.make_async_copy(v, sent.at[:, i * FB : (i + 2) * FB], osem.at[n + 16]) for n, (v, i) in enumerate(shared)]
    for cp in shared:
        cp.start()

    def backward(zz, _):
        cols = pl.ds(pl.multiple_of(zz * D, 128), D)
        da = mm_nt(dlow[...], w2[zz])
        gsum = jnp.zeros((8, D), F32)
        for r in range(R // TR):
            rows = slice(r * TR, (r + 1) * TR)
            di = (da[rows] * gp[rows, cols].astype(F32)).astype(BF)
            act[rows, cols] = di
            gsum = gsum + fold8(di.astype(F32))
        acc[...] += mm_nt(act[:, cols], w1[:, :, cols].reshape(D, D))
        for half in range(2):
            src = act.at[:, pl.ds(pl.multiple_of(zz * D + half * FB, 128), FB)]
            keep(src, 4 + zz, half, 8 + 2 * zz + half)
        gsum = jnp.sum(gsum, axis=0, keepdims=True)
        extra[zz, 3:4, :] = gsum[:, 0:576]
        extra[zz, 4:5, 0:192] = gsum[:, 576:768]
        return 0

    lax.fori_loop(0, 4, backward, 0)
    for cp in shared:
        cp.wait()

    def last(r, _):
        rows = pl.ds(pl.multiple_of(r * TR, TR), TR)
        dy = acc[rows, :]
        xh = xhat[rows, :]
        sums[1] += fold8(dy * xh)
        sums[2] += fold8(dy)
        dx = dy * g1v
        m1 = jnp.mean(dx, axis=-1, keepdims=True)
        m2 = jnp.mean(dx * xh, axis=-1, keepdims=True)
        df = rstd[rows, :1] * (dx - m1 - xh * m2)
        dfirst[rows, :] = df
        low = df.astype(BF)
        dlow[rows, :] = low
        sums[0] += fold8(low.astype(F32))
        return 0

    lax.fori_loop(0, R // TR, last, 0)
    acc[...] = mm_nt(dlow[...], wa[...].reshape(D, D))
    for g in range(0, 4, 2):
        thirds = []
        for s in range(2):
            t0, t1, t2 = (acc[s * T : (s + 1) * T, g * 192 + j * 128 : g * 192 + (j + 1) * 128] for j in range(3))
            t1r, t2r = pltpu.roll(t1, 64, 1), pltpu.roll(t2, 64, 1)
            dattn[g, :, s * 128 : (s + 1) * 128] = t0.astype(BF)
            dattn[g + 1, :, s * 128 : (s + 1) * 128] = jnp.where(lower, t1r, t2r).astype(BF)
            thirds.append((t1, t1r, t2, t2r))
        (a1, _, _, a2r), (_, b1r, b2, _) = thirds
        dattn[g, :, 256:384] = jnp.where(lower, a1, b1r).astype(BF)
        dattn[g + 1, :, 256:384] = jnp.where(lower, a2r, b2).astype(BF)
    for half in range(2):
        keep(dlow.at[:, half * FB : (half + 1) * FB], 8, half, 19 + half)
    for i in range(6):
        row = jnp.sum(sums[i], axis=0, keepdims=True)
        for k in range(4):
            at = (i % 3) * 192
            extra[k, 1 + i // 3 : 2 + i // 3, at : at + 192] = row[:, k * 192 : (k + 1) * 192]
    kept_all(8, 8)
    kept_all(19, 2)


def weight_kernel(idx, kept, mate, sent, plane, mine, *rest):
    outs, (units, shared, units2, shared2, sem) = rest[:6], rest[6:]
    z = idx[1]
    D = shared.shape[1] // 3
    FB = D // 2
    wide = 4 * FB
    copies = []
    for refs, us, sh in (((kept, sent), units, shared), ((mate, mate), units2, shared2)):
        for at, size in ((wide, wide), (0, wide), (2 * wide, FB)):
            copies.append((refs[0].at[:, at : at + size], us.at[:, at : at + size]))
        for at in (D, 2 * D, 0):
            copies.append((refs[1].at[:, 9 * FB + at : 9 * FB + at + D], sh.at[:, at : at + D]))
    order = (0, 3, 6, 9, 1, 4, 7, 10, 2, 5, 8, 11)
    copies = [pltpu.make_async_copy(*copies[n], sem.at[n]) for n in order]
    for cp in copies:
        cp.start()
    for cp in copies[:4]:
        cp.wait()
    for n in range(2):
        cols = slice(wide + n * D, wide + (n + 1) * D)
        v = mm_tn(shared[:, D : 2 * D], units[:, cols]) + mm_tn(shared2[:, D : 2 * D], units2[:, cols])
        v = v.astype(BF)
        for i in range(2):
            for zz in range(4):
                plane[2 * n + i, zz, 0:192, :] = v[zz * 192 : (zz + 1) * 192, i * FB : (i + 1) * FB]
    for cp in copies[4:8]:
        cp.wait()
    for k in range(4):
        cols = pl.ds(pl.multiple_of((z ^ k) * FB, 128), FB)
        v = mm_tn(units[:, cols], shared[:, 2 * D : 3 * D]) + mm_tn(units2[:, cols], shared2[:, 2 * D : 3 * D])
        for q in range(4):
            if k == 0:
                mine[q] = v[q * 96 : (q + 1) * 96]
            else:
                outs[(q // 2) * 3 + k - 1][q % 2] = v[q * 96 : (q + 1) * 96].astype(BF)
    for cp in copies[8:]:
        cp.wait()
    v = mm_tn(shared[:, 0:D], units[:, 2 * wide : 2 * wide + FB]) + mm_tn(shared2[:, 0:D], units2[:, 2 * wide : 2 * wide + FB])
    v = v.astype(BF)
    for zz in range(4):
        for q in range(4):
            plane[q, zz, 192:240, :] = v[zz * 192 + q * 48 : zz * 192 + (q + 1) * 48]


def products_kernel(s, idx, *refs):
    products(s, idx, *(refs if s == 1 else refs[:-1]))


def chunkq_kernel(own, got, *outs):
    for k, ref in enumerate(outs):
        ref[...] = (own[k].astype(F32) + got[k].astype(F32)).astype(ref.dtype)


def chunk_kernel(idx, terms, *outs):
    z = idx[1]
    for k, ref in enumerate(outs):
        ref[...] = sum(terms[q, z ^ k].astype(F32) for q in range(4)).astype(ref.dtype)


def sum2_kernel(mine, *refs):
    parts, out = refs[:-1], refs[-1]
    for q in range(4):
        v = mine[q]
        for k in range(3):
            v = v + parts[(q // 2) * 3 + k][q % 2].astype(F32)
        out[q] = v.astype(out.dtype)


def sum_kernel(a0, a1, a2, a3, b, q0, q1, q2, q3, out):
    A, B = a0.shape
    C, E = b.shape[1], q0.shape[0]
    out[0:A, :] = (a0[...] + sum(a[...].astype(F32) for a in (a1, a2, a3))).astype(BF)
    v = sum(b[k].astype(F32) for k in range(4)).astype(BF)
    out[A : A + C, :] = v[:, :B]
    out[A + C : A + 2 * C, :] = v[:, B:]
    v = (q0[...] + sum(q[...].astype(F32) for q in (q1, q2, q3))).astype(BF)
    at = A + 2 * C
    out[at : at + E, :] = v[:, :B]
    out[at + E : at + 2 * E, :] = jnp.zeros((E, B), BF)
    out[at + E : at + 2 * E, 0 : 576 - B] = v[:, B:]


def out_kernel(idx, s1, r2, c1, c2, g_wq, g_wk, g_wv, g_wi, g_wa, g_wo, g_bq, g_bv, g_bi, *six):
    FB = s1.shape[2]
    c, z = idx[0], idx[1]
    refs = (s1, r2, c1, c2)
    for n, ref in enumerate(refs):
        for k in range(2):
            p = idx[6 + 2 * n + k]
            g_wi[:, pl.ds(pl.multiple_of(p * FB, 128), FB)] = ref[k, 0:192, :].astype(F32)
            rows = pl.ds(pl.multiple_of((p // 2) * 48, 16), 48)
            g_wa[rows, pl.ds(pl.multiple_of((p % 2) * FB, 128), FB)] = ref[k, 192:240, :].astype(F32)
            rows = pl.ds(pl.multiple_of((p % 2) * FB + (p // 2) * 96, 16), 96)
            g_wo[rows, 0:FB] = ref[k, 240:336, :].astype(F32)
            g_wo[rows, FB : 2 * FB] = ref[k, 336:432, :].astype(F32)
    lower = lax.broadcasted_iota(jnp.int32, (96, 128), 1) < 64
    left, right = jnp.zeros((8, FB), F32), jnp.zeros((8, FB), F32)
    top = lax.broadcasted_iota(jnp.int32, (8, FB), 0) == 0
    for (n, k), (m, j) in (((0, 0), (2, 0)), ((0, 1), (3, 0)), ((1, 0), (2, 1)), ((1, 1), (3, 1))):
        p = idx[6 + 2 * n + k]
        yy, xx = p // 4, (p // 2) % 2
        own, other = refs[n].at[k], refs[m].at[j]

        def tile(i, swap):
            at = slice(432, 528) if i < 3 else slice(536, 632)
            cols = slice((i % 3) * 128, (i % 3 + 1) * 128)
            u, v = own[at, cols].astype(F32), other[at, cols].astype(F32)
            return jnp.where((c == 0) != swap, u, v)

        rows = pl.ds(pl.multiple_of(yy * 96, 8), 96)
        for ref, i, third, low in ((g_wq, 0, 3, True), (g_wk, 1, 4, True), (g_wv, 2, 3, False)):
            ta, tb = tile(third, False), tile(third, True)
            turned = pltpu.roll(tile(i, True), 64, 1)
            if not low:
                ta = pltpu.roll(ta, 64, 1)
            else:
                tb = pltpu.roll(tb, 64, 1)
            base = xx * 384
            ref[rows, pl.ds(pl.multiple_of(base, 128), 128)] = tile(i, False)
            ref[rows, pl.ds(pl.multiple_of(base + 128, 128), 128)] = jnp.where(lower, ta, turned)
            ref[rows, pl.ds(pl.multiple_of(base + 256, 128), 128)] = jnp.where(lower, turned, tb)
        for ref, cc in ((own, c), (other, 1 - c)):
            here = (yy == 0) & (~top | (xx * 2 + cc == z))
            left = left + jnp.where(here, ref[528:536, :].astype(F32), 0.0)
            right = right + jnp.where(here, ref[632:640, :].astype(F32), 0.0)
    g_bq[...] = jnp.concatenate([left[0:1, 0:128], right[0:1, 0:64]], axis=1).reshape(192)
    g_bv[...] = jnp.concatenate([left[0:1, 256:384], right[0:1, 64:128]], axis=1).reshape(192)
    for i, ref in enumerate(six):
        row = 1 + i // 3
        ref[...] = (left[row : row + 1, 0:192], left[row : row + 1, 192:384], right[row : row + 1, 0:192])[i % 3].reshape(192)
    g_bi[...] = jnp.concatenate([left[3:4, :], right[3:4, 0:192], left[4:5, 0:192]], axis=1).reshape(768)


def tie(*values):
    return lax.optimization_barrier(values)


def block(shape, *at):
    return pl.BlockSpec(shape, lambda i: at)


def call(kernel, outs, in_specs, out_specs, scratch=(), name=None, grid=()):
    return pl.pallas_call(
        kernel,
        out_shape=outs,
        grid=grid,
        in_specs=in_specs,
        out_specs=out_specs,
        scratch_shapes=list(scratch),
        compiler_params=pltpu.CompilerParams(vmem_limit_bytes=VMEM_LIMIT),
        cost_estimate=pl.CostEstimate(flops=1, bytes_accessed=1, transcendentals=0),
        name=name,
    )


def make_body(sizes):
    pg = sizes["pg"]
    order = [sizes[a] for a in AX]

    def send(fn, a):
        pairs = []
        for flat in range(math.prod(order)):
            at, rest = [], flat
            for n in reversed(order):
                at.append(rest % n)
                rest //= n
            dest = 0
            for n, v in zip(order, fn(*reversed(at))):
                dest = dest * n + v
            pairs.append((flat, dest))
        return lax.ppermute(a, AX, pairs)

    to_x = functools.partial(send, lambda s, g, x, c, z: (s, g, 1 - x, c, z))
    to_y = functools.partial(send, lambda s, g, x, c, z: (1 - s, g, x, c, z))
    to_core = functools.partial(send, lambda s, g, x, c, z: (s, g, x, 1 - c, z))
    to_z = [functools.partial(send, lambda s, g, x, c, z, k=k: (s, g, x, c, z ^ k)) for k in (1, 2, 3)]
    mix_a = functools.partial(send, lambda s, g, x, c, z: (s, g, 1 - x, c, z) if c == 0 else (1 - s, g, x, c, z))
    mix_b = functools.partial(send, lambda s, g, x, c, z: (1 - s, g, x, c, z) if c == 0 else (s, g, 1 - x, c, z))

    to_d = functools.partial(send, lambda s, g, x, c, z: (1 - s, g, 1 - x, c, z))

    def over_plane(sent):
        return [f(v) for f, v in zip((to_x, to_y, to_d), sent)]

    def over_z(sent):
        return [f(v) for f, v in zip(to_z, sent if isinstance(sent, list) else [sent] * 3)]

    def body(
        tokens, cotangent, segment_ids, lengths, w_query, b_query, w_key, w_value, b_value, w_attn, b_attn,
        ln1_gain, ln1_shift, w_inner, b_inner, w_outer, b_outer, ln2_gain, ln2_shift,
    ):
        S, T, D = tokens.shape
        R = S * T
        y, x, c = (lax.axis_index(a) for a in ("seq", "x", "core"))
        mine, z = lax.axis_index("pg"), lax.axis_index("wt")
        h = x * 2 + c
        p = y * 4 + h
        L = 4 * pg * T
        FB = w_inner.shape[1] // 8

        a_of = jnp.where(c == 0, 2, 4)
        other = p ^ 1
        mates = [p, p ^ a_of, p ^ (6 - a_of), p ^ 6, other, other ^ (6 - a_of), other ^ a_of, other ^ 6]
        idx = jnp.stack([c, z, h, y, x, mine] + mates).astype(jnp.int32)

        vecs = (b_query, b_value, b_attn, ln1_gain, ln1_shift, b_outer, ln2_gain, ln2_shift, b_inner)
        w_own, pack, piece1, piece2 = call(
            prep_kernel,
            (
                jax.ShapeDtypeStruct((200, 576), BF), jax.ShapeDtypeStruct((104, 576), BF),
                jax.ShapeDtypeStruct((256, FB), BF), jax.ShapeDtypeStruct((96, D), BF),
            ),
            [SM] + [VM] * 15, (VM,) * 4, name="prep",
        )(idx, w_query, w_key, w_value, w_attn, w_inner, w_outer, *vecs)
        w_z = over_z(pack)
        tok_x, tok_c = to_x(tokens), to_core(tokens)
        w_z, tok_x, tok_c, piece1 = tie(w_z, tok_x, tok_c, piece1)
        w_y, tok_xc = to_y(jnp.stack(w_z)), to_core(tok_x)
        z1 = over_z(piece1)
        w_y, tok_xc, z1, piece2 = tie(w_y, tok_xc, z1, piece2)
        z2 = over_z(piece2)
        one = jnp.stack(z1)
        tok_xc, one = tie(tok_xc, one)
        one_a = mix_a(one)

        toks = [t[None] for t in (tokens, tok_x, tok_c, tok_xc)]
        if pg > 1:
            toks = [lax.all_gather(t, "pg", axis=0, tiled=True) for t in toks]
        head = jax.ShapeDtypeStruct((S, 3, L, 128), BF)
        own_head = jax.ShapeDtypeStruct((S, 3, 4 * T, 128), BF)
        q_aug, k_aug, v_aug, w_qkv = call(
            functools.partial(qkv_kernel, pg),
            (own_head, head, head, jax.ShapeDtypeStruct((4, 192, 576), BF)),
            [SM, SM] + [VM] * 4 + [ANY] * 5,
            (VM,) * 4,
            [pltpu.VMEM((4, 8, 576), BF), pltpu.SemaphoreType.DMA((11,))],
            name="qkv",
        )(lengths, idx, *toks, w_own, *w_z, w_y)
        w_qkv = w_qkv.reshape(D, 576)
        q_aug, one_a, z2 = tie(q_aug, one_a, z2)
        one, two = jnp.stack([one, one_a]), jnp.stack(z2)
        q_aug, one, two = tie(q_aug, one, two)
        one_b, two_a = mix_b(one), mix_a(two)
        o, q_aug = call(
            functools.partial(attn_fwd_kernel, 1024),
            (jax.ShapeDtypeStruct((4, T, 384), BF), own_head),
            [SM, SM] + [VM] * 3,
            (VM,) * 2,
            [pltpu.VMEM((3, T, 128), F32), pltpu.VMEM((3, T, 128), F32)],
            name="attn_fwd",
        )(lengths, idx, q_aug, k_aug, v_aug)
        o, one_b, two_a = tie(o, one_b, two_a)
        attn = lax.all_to_all(o, ("x", "core"), 0, 0, tiled=True)
        two = jnp.stack([two, two_a])
        two_b = mix_b(two)
        one = (one, one_b, to_core(one), to_core(one_b))
        attn, two_b = tie(attn, two_b)
        two = (two, two_b, to_core(two), to_core(two_b))

        layer_out, d_first, d_attn, sent, kept, extra = call(
            ffn_kernel,
            (
                jax.ShapeDtypeStruct((R, D), BF), jax.ShapeDtypeStruct((R, D), F32), jax.ShapeDtypeStruct((4, T, 384), BF),
                jax.ShapeDtypeStruct((R, 15 * FB), BF), jax.ShapeDtypeStruct((R, 9 * FB), BF), jax.ShapeDtypeStruct((4, 8, 576), F32),
            ),
            [SM, SM] + [VM] * 3 + [ANY] * 12,
            (VM, VM, VM, ANY, ANY, VM),
            [
                pltpu.VMEM((4, 192, 8 * FB), BF),
                pltpu.VMEM((4, 2 * FB, D), BF),
                pltpu.VMEM((4, 192, D), BF),
                pltpu.VMEM((4, 16, FB), BF),
                pltpu.VMEM((8, 8, FB), F32),
                pltpu.VMEM((R, D), BF),
                pltpu.VMEM((R, D), BF),
                pltpu.VMEM((R, D), F32),
                pltpu.VMEM((R, 128), F32),
                pltpu.VMEM((R, D), F32),
                pltpu.VMEM((R, 8 * FB), BF),
                pltpu.VMEM((R, 8 * FB), BF),
                pltpu.VMEM((R, D), BF),
                pltpu.VMEM((8, 8, D), F32),
                pltpu.SemaphoreType.DMA((79,)),
                pltpu.SemaphoreType.DMA((21,)),
            ],
            name="ffn",
        )(
            idx, lengths, attn, tokens.reshape(R, D), cotangent.reshape(R, D), piece1, w_inner, w_attn, w_outer, *one, *two
        )

        d_o = lax.all_to_all(d_attn, ("x", "core"), 0, 0, tiled=True)

        def add(*parts):
            return sum(v.astype(F32) for v in parts)

        def shares(n, m):
            return jax.ShapeDtypeStruct((*n, m), F32), *(jax.ShapeDtypeStruct((*n, m), BF),) * 3

        mat = jax.ShapeDtypeStruct((T, D), F32)
        toks = (tokens, tok_x, tok_c, tok_xc)

        def products_specs(s):
            first = (jax.ShapeDtypeStruct((D + 8, 576), F32),) if s == 0 else (jax.ShapeDtypeStruct((4, 104, 576), BF),) * 2
            return (
                (*first, mat, mat, jax.ShapeDtypeStruct((2, T, D), BF)),
                [VM, block((T, D), s, 0)] + [block((1, T, D), s, 0, 0)] * 4 + [VM] * (2 * s),
                (VM,) * (4 + s),
            )

        def attn_bwd(s, d_o, prev):
            args = (lengths, idx, q_aug, k_aug, v_aug, o, d_o)
            outs, ins, out_specs = products_specs(s)
            d_shape = jax.ShapeDtypeStruct((pg, 4, T, 576), BF)
            more = (w_qkv, d_first, *toks, *prev)
            if pg > 1:
                outs, ins, out_specs, more = d_shape, [], VM, ()
            res = call(
                functools.partial(attn_bwd_kernel, pg, 512, s), outs,
                [SM, SM, block((1, 3, 4 * T, 128), s, 0, 0, 0)] + [block((1, 3, L, 128), s, 0, 0, 0)] * 2 + [VM] * 2 + ins,
                out_specs,
                [
                    pltpu.VMEM((3, 4 * T, 128), F32), pltpu.VMEM((3, L, 128), F32), pltpu.VMEM((3, L, 128), F32),
                    pltpu.VMEM((3, T, 128), BF), pltpu.VMEM((1, 4, T, 576), BF), pltpu.VMEM((D + 8, 576), F32),
                ],
                name="attn_bwd", grid=(1,),
            )(*args, *more)
            if pg > 1:
                d = lax.psum_scatter(res, "pg", scatter_dimension=0, tiled=True)
                outs, ins, out_specs = products_specs(s)
                res = call(
                    functools.partial(products_kernel, s), outs, [SM, VM] + ins, out_specs, [pltpu.VMEM((D + 8, 576), F32)],
                    name="products", grid=(1,),
                )(idx, d, w_qkv, d_first, *toks, *prev)
            return res

        half = jax.ShapeDtypeStruct((2, 96, D), BF)
        q1, c2, *sent2 = call(
            weight_kernel,
            (jax.ShapeDtypeStruct((4, 4, 240, FB), BF), jax.ShapeDtypeStruct((4, 96, D), F32)) + (half,) * 6,
            [SM] + [ANY] * 3, (VM,) * 8,
            [
                pltpu.VMEM((R, 9 * FB), BF), pltpu.VMEM((R, 3 * D), BF), pltpu.VMEM((R, 9 * FB), BF), pltpu.VMEM((R, 3 * D), BF),
                pltpu.SemaphoreType.DMA((12,)),
            ],
            name="weights",
        )(idx, kept, to_core(sent), sent)
        n, m = q1.shape[2:]
        d_o, sent2, q1 = tie(d_o, sent2, q1)
        got_a, q1 = over_z(sent2[:3]), lax.all_to_all(q1, ("seq", "x"), 0, 0, tiled=True)
        gq, own0, x0, core0 = attn_bwd(0, d_o, ())
        gq, d_o, core0, got_a, sent2 = tie(gq, d_o, core0, got_a, sent2[3:])
        got_b, core0 = over_z(sent2), to_core(core0)
        gq_own, gq_other, own1, x1, core1 = attn_bwd(1, d_o, (gq, extra))
        gq_own, core0, core1, got_b = tie(gq_own, core0, core1, got_b)
        gq_y, core1 = to_y(gq_other), to_core(core1)
        x0 = add(x0, core0[1]).astype(BF)
        c1, *sent1 = call(chunk_kernel, shares((n,), m), [SM, VM], (VM,) * 4, name="chunks1")(idx, q1)
        sent1, x0 = tie(sent1, x0)
        got_z1 = over_z(sent1)
        q2 = call(sum2_kernel, jax.ShapeDtypeStruct((4, 96, D), BF), [VM] * 7, VM, name="sums2")(c2, *got_a, *got_b)
        q2 = lax.all_to_all(q2, ("seq", "x"), 0, 0, tiled=True)
        x0 = to_x(x0)
        cq, *sentq = call(chunkq_kernel, shares((104,), 576), [VM] * 2, (VM,) * 4, name="chunksq")(gq_own, gq_y)
        x1 = add(x1, core1[1]).astype(BF)
        sentq, got_z1, x0, x1 = tie(sentq, got_z1, x0, x1)
        got_zq, x1 = over_z(sentq), to_x(x1)
        q2, got_z1, got_zq, x1 = tie(q2, got_z1, got_zq, x1)
        total = call(sum_kernel, jax.ShapeDtypeStruct((640, FB), BF), [VM] * 9, VM, name="sums")(
            c1, *got_z1, q2, cq, *got_zq
        )
        if pg > 1:
            total = lax.psum(total.astype(F32), "pg").astype(BF)
        s1 = mix_a(total)
        total, s1, x0, x1 = tie(total, s1, x0, x1)
        s1 = jnp.stack([total, s1])
        r2, s1_core = mix_b(s1), to_core(s1)
        grad_input = jnp.stack([add(own0, core0[0], x0), add(own1, core1[0], x1)]).astype(BF)
        r2, s1_core, grad_input = tie(r2, s1_core, grad_input)
        mat, wide = jax.ShapeDtypeStruct((192, D), F32), jax.ShapeDtypeStruct((192, 8 * FB), F32)
        vec, long_vec = jax.ShapeDtypeStruct((192,), F32), jax.ShapeDtypeStruct((2 * FB,), F32)
        g_wq, g_wk, g_wv, g_wi, g_wa, g_wo, g_bq, g_bv, g_bi, *six = call(
            out_kernel, (mat, mat, mat, wide, mat, jax.ShapeDtypeStruct((D, D), F32), vec, vec, long_vec) + (vec,) * 6,
            [SM] + [VM] * 4, (VM,) * 15, name="outputs",
        )(idx, s1, r2, s1_core, to_core(r2))
        return (
            layer_out.reshape(tokens.shape), grad_input,
            g_wq, g_bq, g_wk, g_wv, g_bv, g_wa, six[0], six[1], six[2], g_wi, g_bi, g_wo, six[3], six[4], six[5],
        )

    return body


def solution(mesh):
    sizes = dict(mesh.shape)
    pg = sizes["ctx"] // 4
    fine = dict(zip(AX, (sizes["seq"], pg, 2, 2, sizes["wt"])))
    split = Mesh(mesh.devices.reshape(tuple(fine.values())), AX)
    rows = P(("seq", "wt"), ("pg", "x", "core"), None)
    mat, vec = P("wt", None), P("wt")
    in_specs = (
        rows, rows, P(("seq", "wt"), ("pg", "x", "core")), P(("seq", "wt"), None),
        mat, vec, mat, mat, vec, mat, vec, vec, vec, mat, vec, mat, vec, vec, vec,
    )
    out_specs = (rows, rows, mat, vec, mat, mat, vec, mat, vec, vec, vec, mat, vec, mat, vec, vec, vec)
    return jax.shard_map(make_body(fine), mesh=split, in_specs=in_specs, out_specs=out_specs, check_vma=False)
```

```python
import functools
import math

import jax
import jax.numpy as jnp
from jax import lax
from jax.experimental import pallas as pl
from jax.experimental.pallas import tpu as pltpu
from jax.sharding import Mesh
from jax.sharding import PartitionSpec as P

NEG = -1000000000.0
EPS = 1e-05
BF = jnp.bfloat16
F32 = jnp.float32
AX = ("seq", "pg", "x", "core", "wt")
VM = pl.BlockSpec(memory_space=pltpu.VMEM)
SM = pl.BlockSpec(memory_space=pltpu.SMEM)
ANY = pl.BlockSpec(memory_space=pl.ANY)
OFFS = (0, 2, 1, 3)
VMEM_LIMIT = 60 * 2**20


def mm(a, b):
    return jnp.dot(a, b, preferred_element_type=F32)


def mm_nt(a, b):
    return lax.dot_general(a, b, (((1,), (1,)), ((), ())), preferred_element_type=F32)


def mm_tn(a, b):
    return lax.dot_general(a, b, (((0,), (0,)), ((), ())), preferred_element_type=F32)


def fold8(v):
    return jnp.sum(v.reshape(v.shape[0] // 8, 8, v.shape[1]), axis=0)


def limits(lengths, s, length):
    out = [jnp.int32(0)]
    for d in range(4):
        out.append(out[-1] + lengths[s, d])
    return out + [jnp.int32(length)]


def span(bounds, first, last):
    low, high = bounds[0], bounds[5]
    for d in range(1, 5):
        low = jnp.where(bounds[d] <= first, bounds[d], low)
        high = jnp.where(bounds[5 - d] > last, bounds[5 - d], high)
    return low, high


def prep_kernel(idx, wq, wk, wv, w_at, w_in, w_out, *rest):
    vecs, (w_own, pack, piece1, piece2) = rest[:9], rest[9:]
    c, h, y = idx[0], idx[2], idx[3]
    p = y * 4 + h
    FB = piece1.shape[1]
    for head in range(4):

        @pl.when(h == head)
        def _():
            a = head * 192
            for i, w in enumerate((wq, wk, wv)):
                w_own[0:192, i * 128 : (i + 1) * 128] = w[:, a : a + 128]
            w_own[0:192, 384:448] = wq[:, a + 128 : a + 192]
            w_own[0:192, 448:512] = wv[:, a + 128 : a + 192]
            w_own[0:192, 512:576] = wk[:, a + 128 : a + 192]

    bq, bv = (v[...].reshape(1, 192) for v in vecs[:2])
    w_own[192:200, :] = jnp.zeros((8, 576), BF)
    w_own[192:193, 0:128] = bq[:, 0:128]
    w_own[192:193, 256:384] = bv[:, 0:128]
    w_own[192:193, 384:448] = bq[:, 128:192]
    w_own[192:193, 448:512] = bv[:, 128:192]
    pack[0:96, :] = w_own[pl.ds(pl.multiple_of(y * 96, 16), 96), :]
    pack[96:104, :] = w_own[192:200, :]
    piece1[0:192, :] = w_in[:, pl.ds(pl.multiple_of(p * FB, 128), FB)]
    piece1[192:240, :] = w_at[pl.ds(pl.multiple_of((p // 2) * 48, 16), 48), pl.ds(pl.multiple_of(c * FB, 128), FB)]
    piece1[240:256, :] = jnp.zeros((16, FB), BF)
    for i, v in enumerate(vecs[:8]):
        piece1[240 + i : 241 + i, 0:192] = v[...].reshape(1, 192)
    for i in range(4):
        piece1[248 + i : 249 + i, 0:192] = vecs[8][i * 192 : (i + 1) * 192].reshape(1, 192)
    piece2[...] = w_out[pl.ds(pl.multiple_of(c * FB + (p // 2) * 96, 16), 96), :]


def qkv_kernel(pg, lengths, idx, *refs):
    toks, (w_own, w_z1, w_z2, w_z3, w_y, q_out, k_out, v_out, w, bs, sem) = refs[:4], refs[4:]
    z, c, y, mine = idx[1], idx[2], idx[3], idx[5]
    T, D = toks[0].shape[2:]
    copies = [(w_own.at[0:192], w.at[z]), (w_own.at[192:200], bs.at[0])]
    for k, ref in enumerate((w_z1, w_z2, w_z3)):
        copies.append((ref.at[0:96], w.at[z ^ (k + 1), pl.ds(pl.multiple_of(y * 96, 16), 96)]))
        copies.append((ref.at[96:104], bs.at[k + 1]))
        copies.append((w_y.at[k, 0:96], w.at[z ^ (k + 1), pl.ds(pl.multiple_of((1 - y) * 96, 16), 96)]))
    copies = [pltpu.make_async_copy(a, b, sem.at[i]) for i, (a, b) in enumerate(copies)]
    for cp in copies:
        cp.start()
    for cp in copies:
        cp.wait()
    lane = lax.broadcasted_iota(jnp.int32, (T, 128), 1)
    row = lax.broadcasted_iota(jnp.int32, (T, 128), 0)
    lower = lane < 64
    rel = lane & 63
    zero64 = jnp.zeros((T, 64), F32)

    bias = bs[c ^ z, 0:1, :].astype(F32)
    for g in range(pg):
        for n, off in enumerate(OFFS):
            place = pl.multiple_of((g * 4 + (c ^ off)) * T, T)
            own = pl.multiple_of((c ^ off) * T, T)
            pos = row + place
            for s in range(2):
                qkv = mm(toks[n][g, s], w[...].reshape(D, 576)) + bias
                qkv = qkv.astype(BF).astype(F32)
                seg = jnp.zeros((T, 128), jnp.int32)
                for start in limits(lengths, s, 0)[1:5]:
                    seg = seg + (pos >= start).astype(jnp.int32)
                hot = rel == seg
                q_aug = jnp.where(hot, 1.0, 0.0)
                k_aug = jnp.where(rel < 5, jnp.where(hot, 0.0, NEG), jnp.where(rel < 11, 1.0, 0.0))
                q01, k01, v01, q2v2 = (qkv[:, j * 128 : (j + 1) * 128] for j in range(4))
                k2 = jnp.concatenate([qkv[:, 512:576], zero64], axis=1)
                for h, (k, v) in enumerate(((k01, v01), (k01, v01), (k2, q2v2))):
                    half = ~lower if h == 1 else lower
                    k_out[s, h, pl.ds(place, T)] = jnp.where(half, k, k_aug).astype(BF)
                    half = lower if h == 0 else ~lower
                    v_out[s, h, pl.ds(place, T)] = jnp.where(half, v, 1.0).astype(BF)

                def store_q():
                    for h, q in enumerate((q01, q01, q2v2)):
                        half = ~lower if h == 1 else lower
                        q_out[s, h, pl.ds(own, T)] = jnp.where(half, q * 0.125, q_aug).astype(BF)

                if pg == 1:
                    store_q()
                else:
                    pl.when(mine == g)(store_q)


def attn_fwd_kernel(KC, lengths, idx, q_ref, k_ref, v_ref, o_ref, q_out, m_s, acc_s):
    mine = idx[5]
    T, L = o_ref.shape[1], k_ref.shape[2]
    lane = lax.broadcasted_iota(jnp.int32, (T, 128), 1)
    lower = lane < 64

    def per_tile(si, _):
        s, i = si // 4, si % 4
        here = pl.multiple_of(i * T, T)
        first = (mine * 4 + i) * T
        low, high = span(limits(lengths, s, L), first, first + T - 1)
        for h in range(3):
            m_s[h] = jnp.full((T, 128), -jnp.inf, F32)
            acc_s[h] = jnp.zeros((T, 128), F32)

        def step(kt, _):
            at = pl.multiple_of(kt * KC, KC)
            for h in range(3):
                sc = mm_nt(q_ref[s, h, pl.ds(here, T)], k_ref[s, h, pl.ds(at, KC)])
                old = m_s[h]
                parts = [sc[:, j * 128 : (j + 1) * 128] for j in range(KC // 128)]
                top = functools.reduce(jnp.maximum, parts)
                new = jnp.maximum(old, jnp.broadcast_to(jnp.max(top, axis=1, keepdims=True), (T, 128)))
                p = jnp.concatenate([jnp.exp(v - new).astype(BF) for v in parts], axis=1)
                acc_s[h] = acc_s[h] * jnp.exp(old - new) + mm(p, v_ref[s, h, pl.ds(at, KC)])
                m_s[h] = new
            return 0

        lax.fori_loop(low // KC, (high + KC - 1) // KC, step, 0)
        outs = []
        for h in range(3):
            acc = acc_s[h]
            turned = pltpu.roll(acc, 64, 1)
            data = lower if h == 0 else ~lower
            total = jnp.where(data, turned, acc)
            outs.append(acc / total)
            lse = m_s[h] + jnp.log(total)
            l1 = lse.astype(BF).astype(F32)
            l2 = (lse - l1).astype(BF).astype(F32)
            l3 = lse - l1 - l2
            at = lane if h == 1 else lane - 64
            q = q_ref[s, h, pl.ds(here, T)].astype(F32)
            q = jnp.where(at == 8, -l1, jnp.where(at == 9, -l2, jnp.where(at == 10, -l3, q)))
            q_out[s, h, pl.ds(here, T)] = q.astype(BF)
        o_ref[i, :, pl.ds(pl.multiple_of(s * 128, 128), 128)] = jnp.where(lower, outs[0], outs[1]).astype(BF)

        @pl.when(s == 0)
        def _():
            o_ref[i, :, 256:384] = pltpu.roll(outs[2], 64, 1).astype(BF)

        @pl.when(s == 1)
        def _():
            o_ref[i, :, 256:384] = jnp.where(lower, o_ref[i, :, 256:384].astype(F32), outs[2]).astype(BF)

        return 0

    lax.fori_loop(0, 8, per_tile, 0)


def attn_bwd_kernel(pg, KC, lengths, idx, *refs):
    ins, (w, t0, t1, t2, t3, extra), outs, scratch = refs[:5], refs[5:11], refs[11:-6], refs[-6:]
    gq_s = scratch[-1]
    for s in range(2):
        attn_bwd(pg, KC, s, lengths, idx, *ins, *scratch[:4], outs[0].at[s] if pg > 1 else scratch[4])
        if pg == 1:
            products(s, idx, scratch[4], w, (t0, t1, t2, t3), extra, gq_s, *outs)


def attn_bwd(pg, KC, s, lengths, idx, q_ref, k_ref, v_ref, o_ref, do_ref, dq_s, dk_s, dv_s, do_s, d_ref):
    c, mine = idx[2], idx[5]
    T, L = o_ref.shape[1], k_ref.shape[2]
    bounds = limits(lengths, s, L)
    lane = lax.broadcasted_iota(jnp.int32, (T, 128), 1)
    lower = lane < 64
    zero = jnp.zeros((T, 128), F32)

    dk_s[...] = jnp.zeros_like(dk_s)
    dv_s[...] = jnp.zeros_like(dv_s)
    live = bounds[4]
    cols = slice(s * 128, (s + 1) * 128)

    def per_tile(i, _):
        here = pl.multiple_of(i * T, T)
        first = (mine * 4 + i) * T
        low, high = span(bounds, first, first + T - 1)
        high = jnp.minimum(high, live)
        pair = do_ref[i, :, cols].astype(F32)
        third = do_ref[i, :, 256:384].astype(F32)
        if s == 0:
            third = pltpu.roll(third, 64, 1)
        o_third = o_ref[i, :, 256:384].astype(F32)
        if s == 0:
            o_third = pltpu.roll(o_third, 64, 1)
        prod = pair * o_ref[i, :, cols].astype(F32)
        for h in range(3):
            data = lower if h == 0 else ~lower
            full = prod if h < 2 else third * o_third
            delta = jnp.sum(jnp.where(data, full, zero), axis=1, keepdims=True)
            d1 = delta.astype(BF).astype(F32)
            d2 = (delta - d1).astype(BF).astype(F32)
            d3 = delta - d1 - d2
            at = lane - 64 if h == 0 else lane
            aug = jnp.where(at == 8, -d1, jnp.where(at == 9, -d2, jnp.where(at == 10, -d3, zero)))
            do_s[h] = jnp.where(data, pair if h < 2 else third, aug).astype(BF)
            dq_s[h, pl.ds(here, T)] = zero

        def step(kt, _):
            at = pl.multiple_of(kt * KC, KC)
            for h in range(3):
                q = q_ref[s, h, pl.ds(here, T)]
                k = k_ref[s, h, pl.ds(at, KC)]
                d = do_s[h]
                pt = jnp.exp(mm_nt(k, q))
                ds = (pt * mm_nt(v_ref[s, h, pl.ds(at, KC)], d)).astype(BF)
                dv_s[h, pl.ds(at, KC)] += mm(pt.astype(BF), d)
                dk_s[h, pl.ds(at, KC)] += mm(ds, q)
                dq_s[h, pl.ds(here, T)] += mm_tn(ds, k)
            return 0

        lax.fori_loop(low // KC, (high + KC - 1) // KC, step, 0)
        return 0

    lax.fori_loop(0, 4, per_tile, 0)
    for g in range(pg):
        for n, off in enumerate(OFFS):
            at = pl.multiple_of((g * 4 + (c ^ off)) * T, T)
            own = pl.multiple_of((c ^ off) * T, T)
            keep = 0.125 if pg == 1 else jnp.where(mine == g, 0.125, 0.0)
            dq = [dq_s[h, pl.ds(own, T)] * keep for h in range(3)]
            dk = [dk_s[h, pl.ds(at, T)] for h in range(3)]
            dv = [dv_s[h, pl.ds(at, T)] for h in range(3)]
            d_ref[g, n, :, 0:128] = jnp.where(lower, dq[0], dq[1]).astype(BF)
            d_ref[g, n, :, 128:256] = jnp.where(lower, dk[0], dk[1]).astype(BF)
            d_ref[g, n, :, 256:384] = jnp.where(lower, dv[0], dv[1]).astype(BF)
            d_ref[g, n, :, 384:512] = jnp.where(lower, dq[2], dv[2]).astype(BF)
            d_ref[g, n, :, 512:576] = dk[2][:, 0:64].astype(BF)


def products(s, idx, d, w, toks, extra, acc, gq_own, gq_other, gi):
    zw, h, y = idx[1], idx[2], idx[3]
    D = w.shape[0]
    T = d.shape[2]
    rows = slice(s * T, (s + 1) * T)
    for n, off in enumerate(OFFS):
        gi[h ^ off, rows, :] = mm_nt(d[0, n], w[...]).astype(BF)
    v = sum(mm_tn(t[s], d[0, n]) for n, t in enumerate(toks))
    col = sum(fold8(d[0, n].astype(F32)) for n in range(4))
    if s == 0:
        acc[0:D, :] = v
        acc[D : D + 8, :] = col
        return
    acc[0:D, :] += v
    col = jnp.sum(col + acc[D : D + 8, :], axis=0, keepdims=True)
    top = lax.broadcasted_iota(jnp.int32, (8, 576), 0) == 0
    for k in range(4):
        z = zw ^ k
        tail = jnp.where(top & (h == z), col, extra[z]).astype(BF)
        for ref, yy in ((gq_own, y), (gq_other, 1 - y)):
            ref[k, 0:96, :] = acc[pl.ds(pl.multiple_of(z * 192 + yy * 96, 8), 96), :].astype(BF)
            ref[k, 96:104, :] = tail


def gelu_parts(u):
    t = 1.0 / (1.0 + (0.3275911 * 0.7071067811865476) * jnp.abs(u))
    e = jnp.exp(-0.5 * u * u)
    poly = t * (
        0.127414796
        + t * (-0.142248368 + t * (0.7107068705 + t * (-0.7265760135 + t * 0.5307027145)))
    )
    tail = poly * e
    cdf = jnp.where(u >= 0, 1.0 - tail, tail)
    return u * cdf, cdf + u * e * 0.3989422804014327


def gather_heads(tiles):
    (pair0, third0), (pair1, third1) = tiles
    lower = lax.broadcasted_iota(jnp.int32, pair0.shape, 1) < 64
    turned = pltpu.roll(pair1, 64, 1)
    return pair0, jnp.where(lower, third0, turned), jnp.where(lower, turned, pltpu.roll(third1, 64, 1))


def ffn_kernel(
    idx, lengths, attn, tok, cot, sm_own, w_in, w_at, w_out,
    s1a, r2a, c1a, c2a, s1b, r2b, c1b, c2b,
    out, dfirst, dattn, sent, kept, extra,
    w1, w2, wa, sm, b1, att, hlow, xhat, rstd, acc, act, gp, dlow, sums, sem, osem,
):
    c, z, h, y, x, mine = (idx[i] for i in range(6))
    R, D = tok.shape
    T = attn.shape[1]
    FB = w_in.shape[1] // 8
    TR = 128
    first_copies = [(w_at, wa.at[z]), (sm_own.at[240:256], sm.at[0])]
    first_copies += [(s1a.at[0, k, 240:256], sm.at[k + 1]) for k in range(3)]
    copies = [(w_in, w1.at[z]), (w_out, w2.at[z])]
    for n, (ra, rb) in enumerate(((s1a, s1b), (r2a, r2b), (c1a, c1b), (c2a, c2b))):
        for k in range(2):
            p = idx[6 + 2 * n + k]
            q, half = p // 2, p % 2
            for kz in range(3):
                zz = z ^ (kz + 1)
                at = pl.ds(pl.multiple_of(half * FB, 128), FB)
                first_copies.append((ra.at[k, kz, 192:240], wa.at[zz, pl.ds(pl.multiple_of(q * 48, 16), 48), at]))
                copies.append((ra.at[k, kz, 0:192], w1.at[zz, :, pl.ds(pl.multiple_of(p * FB, 128), FB)]))
                copies.append((rb.at[k, kz], w2.at[zz, pl.ds(pl.multiple_of(half * FB + q * 96, 16), 96)]))
    many = len(first_copies)
    first_copies = [pltpu.make_async_copy(a, b, sem.at[i]) for i, (a, b) in enumerate(first_copies)]
    copies = [pltpu.make_async_copy(a, b, sem.at[many + i]) for i, (a, b) in enumerate(copies)]
    for cp in first_copies + copies:
        cp.start()

    sums[...] = jnp.zeros_like(sums)
    extra[...] = jnp.zeros_like(extra)

    lower = lax.broadcasted_iota(jnp.int32, (T, 128), 1) < 64
    for s in range(2):
        for g in range(0, 4, 2):
            tiles = []
            for n in (g, g + 1):
                third = attn[n, :, 256:384].astype(F32)
                tiles.append((
                    attn[n, :, s * 128 : (s + 1) * 128].astype(F32),
                    third if s == 0 else pltpu.roll(third, 64, 1),
                ))
            for j, tile in enumerate(gather_heads(tiles)):
                at = g * 192 + j * 128
                att[s * T : (s + 1) * T, at : at + 128] = tile.astype(BF)

    for cp in first_copies:
        cp.wait()

    def whole(i):
        return jnp.concatenate([sm[k ^ z, i : i + 1, 0:192].astype(F32) for k in range(4)], axis=1)

    b_attn, g1v, s1v, b_out, g2v, s2v = (whole(i) for i in range(2, 8))
    for k in range(4):
        row = jnp.concatenate([sm[k ^ z, i : i + 1, 0:192].astype(F32) for i in range(8, 12)], axis=1)
        for half in range(2):
            b1[2 * k + half, 0:1, :] = row[:, half * FB : (half + 1) * FB]

    acc[...] = mm(att[...], wa[...].reshape(D, D))

    def first(r, _):
        rows = pl.ds(pl.multiple_of(r * TR, TR), TR)
        v = acc[rows, :] + tok[rows, :].astype(F32) + b_attn
        mean = jnp.mean(v, axis=-1, keepdims=True)
        v = v - mean
        rs = lax.rsqrt(jnp.mean(v * v, axis=-1, keepdims=True) + EPS)
        xh = v * rs
        xhat[rows, :] = xh
        rstd[rows, :] = jnp.broadcast_to(rs, (TR, 128))
        hid = xh * g1v + s1v
        hlow[rows, :] = hid.astype(BF)
        acc[rows, :] = hid + b_out
        return 0

    lax.fori_loop(0, R // TR, first, 0)
    for cp in copies:
        cp.wait()

    def keep(src, i, cc, at):
        to = pl.ds(pl.multiple_of(i * FB, 128), FB)

        @pl.when(c == cc)
        def _():
            pltpu.make_async_copy(src, kept.at[:, to], osem.at[at]).start()

        @pl.when(c != cc)
        def _():
            pltpu.make_async_copy(src, sent.at[:, to], osem.at[at]).start()

    def kept_all(first, count):
        for i in range(first, first + count):
            pltpu.make_async_copy(act.at[:, 0:FB], kept.at[:, 0:FB], osem.at[i]).wait()

    def forward(zz, _):
        cols = pl.ds(pl.multiple_of(zz * D, 128), D)
        u = mm(hlow[...], w1[:, :, cols].reshape(D, D)) + jnp.concatenate([b1[2 * zz, 0:1, :], b1[2 * zz + 1, 0:1, :]], axis=1)
        for r in range(R // TR):
            rows = slice(r * TR, (r + 1) * TR)
            a, d = gelu_parts(u[rows])
            act[rows, cols] = a.astype(BF)
            gp[rows, cols] = d.astype(BF)
        acc[...] += mm(act[:, cols], w2[zz])
        for half in range(2):
            src = act.at[:, pl.ds(pl.multiple_of(zz * D + half * FB, 128), FB)]
            keep(src, zz, half, 2 * zz + half)
        return 0

    lax.fori_loop(0, 4, forward, 0)

    def second(r, _):
        rows = pl.ds(pl.multiple_of(r * TR, TR), TR)
        s = r // (T // TR)
        v = acc[rows, :]
        mean = jnp.mean(v, axis=-1, keepdims=True)
        v = v - mean
        rs = lax.rsqrt(jnp.mean(v * v, axis=-1, keepdims=True) + EPS)
        xh = v * rs
        out[rows, :] = (xh * g2v + s2v).astype(BF)
        place = (mine * 4 + h) * T + r * TR - s * T
        pos = lax.broadcasted_iota(jnp.int32, (TR, D), 0) + place
        dy = jnp.where(pos < limits(lengths, s, 0)[4], cot[rows, :].astype(F32), 0.0)
        sums[4] += fold8(dy * xh)
        sums[5] += fold8(dy)
        dx = dy * g2v
        m1 = jnp.mean(dx, axis=-1, keepdims=True)
        m2 = jnp.mean(dx * xh, axis=-1, keepdims=True)
        ds = rs * (dx - m1 - xh * m2)
        low = ds.astype(BF)
        dlow[rows, :] = low
        sums[3] += fold8(low.astype(F32))
        acc[rows, :] = ds
        return 0

    lax.fori_loop(0, R // TR, second, 0)

    kept_all(0, 8)
    shared = [(att, 9), (hlow, 11), (dlow, 13)]
    shared = [pltpu.make_async_copy(v, sent.at[:, i * FB : (i + 2) * FB], osem.at[n + 16]) for n, (v, i) in enumerate(shared)]
    for cp in shared:
        cp.start()

    def backward(zz, _):
        cols = pl.ds(pl.multiple_of(zz * D, 128), D)
        da = mm_nt(dlow[...], w2[zz])
        gsum = jnp.zeros((8, D), F32)
        for r in range(R // TR):
            rows = slice(r * TR, (r + 1) * TR)
            di = (da[rows] * gp[rows, cols].astype(F32)).astype(BF)
            act[rows, cols] = di
            gsum = gsum + fold8(di.astype(F32))
        acc[...] += mm_nt(act[:, cols], w1[:, :, cols].reshape(D, D))
        for half in range(2):
            src = act.at[:, pl.ds(pl.multiple_of(zz * D + half * FB, 128), FB)]
            keep(src, 4 + zz, half, 8 + 2 * zz + half)
        gsum = jnp.sum(gsum, axis=0, keepdims=True)
        extra[zz, 3:4, :] = gsum[:, 0:576]
        extra[zz, 4:5, 0:192] = gsum[:, 576:768]
        return 0

    lax.fori_loop(0, 4, backward, 0)
    for cp in shared:
        cp.wait()

    def last(r, _):
        rows = pl.ds(pl.multiple_of(r * TR, TR), TR)
        dy = acc[rows, :]
        xh = xhat[rows, :]
        sums[1] += fold8(dy * xh)
        sums[2] += fold8(dy)
        dx = dy * g1v
        m1 = jnp.mean(dx, axis=-1, keepdims=True)
        m2 = jnp.mean(dx * xh, axis=-1, keepdims=True)
        df = rstd[rows, :1] * (dx - m1 - xh * m2)
        dfirst[rows, :] = df
        low = df.astype(BF)
        dlow[rows, :] = low
        sums[0] += fold8(low.astype(F32))
        return 0

    lax.fori_loop(0, R // TR, last, 0)
    acc[...] = mm_nt(dlow[...], wa[...].reshape(D, D))
    for g in range(0, 4, 2):
        thirds = []
        for s in range(2):
            t0, t1, t2 = (acc[s * T : (s + 1) * T, g * 192 + j * 128 : g * 192 + (j + 1) * 128] for j in range(3))
            t1r, t2r = pltpu.roll(t1, 64, 1), pltpu.roll(t2, 64, 1)
            dattn[g, :, s * 128 : (s + 1) * 128] = t0.astype(BF)
            dattn[g + 1, :, s * 128 : (s + 1) * 128] = jnp.where(lower, t1r, t2r).astype(BF)
            thirds.append((t1, t1r, t2, t2r))
        (a1, _, _, a2r), (_, b1r, b2, _) = thirds
        dattn[g, :, 256:384] = jnp.where(lower, a1, b1r).astype(BF)
        dattn[g + 1, :, 256:384] = jnp.where(lower, a2r, b2).astype(BF)
    for half in range(2):
        keep(dlow.at[:, half * FB : (half + 1) * FB], 8, half, 19 + half)
    for i in range(6):
        row = jnp.sum(sums[i], axis=0, keepdims=True)
        for k in range(4):
            at = (i % 3) * 192
            extra[k, 1 + i // 3 : 2 + i // 3, at : at + 192] = row[:, k * 192 : (k + 1) * 192]
    kept_all(8, 8)
    kept_all(19, 2)


def weight_kernel(idx, kept, mate, sent, plane, mine, *rest):
    outs, (units, shared, units2, shared2, sem) = rest[:3], rest[3:]
    z = idx[1]
    D = shared.shape[1] // 3
    FB = D // 2
    wide = 4 * FB
    copies = []
    for refs, us, sh in (((kept, sent), units, shared), ((mate, mate), units2, shared2)):
        for at, size in ((wide, wide), (0, wide), (2 * wide, FB)):
            copies.append((refs[0].at[:, at : at + size], us.at[:, at : at + size]))
        for at in (D, 2 * D, 0):
            copies.append((refs[1].at[:, 9 * FB + at : 9 * FB + at + D], sh.at[:, at : at + D]))
    order = (0, 3, 6, 9, 1, 4, 7, 10, 2, 5, 8, 11)
    copies = [pltpu.make_async_copy(*copies[n], sem.at[n]) for n in order]
    for cp in copies:
        cp.start()
    for cp in copies[:4]:
        cp.wait()
    for n in range(2):
        cols = slice(wide + n * D, wide + (n + 1) * D)
        v = mm_tn(shared[:, D : 2 * D], units[:, cols]) + mm_tn(shared2[:, D : 2 * D], units2[:, cols])
        v = v.astype(BF)
        for i in range(2):
            for zz in range(4):
                plane[2 * n + i, zz, 0:192, :] = v[zz * 192 : (zz + 1) * 192, i * FB : (i + 1) * FB]
    for cp in copies[4:8]:
        cp.wait()
    for k in range(4):
        cols = pl.ds(pl.multiple_of((z ^ k) * FB, 128), FB)
        v = mm_tn(units[:, cols], shared[:, 2 * D : 3 * D]) + mm_tn(units2[:, cols], shared2[:, 2 * D : 3 * D])
        for q in range(4):
            if k == 0:
                mine[q] = v[q * 96 : (q + 1) * 96]
            else:
                outs[k - 1][q] = v[q * 96 : (q + 1) * 96].astype(BF)
    for cp in copies[8:]:
        cp.wait()
    v = mm_tn(shared[:, 0:D], units[:, 2 * wide : 2 * wide + FB]) + mm_tn(shared2[:, 0:D], units2[:, 2 * wide : 2 * wide + FB])
    v = v.astype(BF)
    for zz in range(4):
        for q in range(4):
            plane[q, zz, 192:240, :] = v[zz * 192 + q * 48 : zz * 192 + (q + 1) * 48]


def products_kernel(idx, d, w, t0, t1, t2, t3, extra, *outs):
    for s in range(2):
        products(s, idx, d.at[s], w, (t0, t1, t2, t3), extra, outs[-1], *outs[:-1])


def chunkq_kernel(own, got, *outs):
    for k, ref in enumerate(outs):
        ref[...] = (own[k].astype(F32) + got[k].astype(F32)).astype(ref.dtype)


def chunk_kernel(idx, terms, *outs):
    z = idx[1]
    for k, ref in enumerate(outs):
        ref[...] = sum(terms[q, z ^ k].astype(F32) for q in range(4)).astype(ref.dtype)


def sum2_kernel(idx, a0, a1, a2, a3, *outs):
    here = idx[3] * 2 + idx[4]
    for k, ref in enumerate(outs):
        q = here ^ k
        ref[...] = (a0[q] + sum(a[q].astype(F32) for a in (a1, a2, a3))).astype(ref.dtype)


def sum_kernel(a0, a1, a2, a3, b0, b1, b2, b3, out):
    A, B = a0.shape
    C = b0.shape[0]
    out[0:A, :] = (a0[...] + sum(a[...].astype(F32) for a in (a1, a2, a3))).astype(BF)
    v = (b0[...] + sum(b[...].astype(F32) for b in (b1, b2, b3))).astype(BF)
    out[A : A + C, :] = v[:, :B]
    out[A + C : A + 2 * C, :] = v[:, B:]


def sumq_kernel(q0, q1, q2, q3, out):
    E, W = q0.shape
    B = out.shape[1]
    v = (q0[...] + sum(q[...].astype(F32) for q in (q1, q2, q3))).astype(BF)
    out[0:E, :] = v[:, :B]
    out[E : 2 * E, :] = jnp.zeros((E, B), BF)
    out[E : 2 * E, 0 : W - B] = v[:, B:]


def out_ffn_kernel(idx, s1, r2, c1, c2, g_wi, g_wa, g_wo):
    FB = s1.shape[2]
    refs = (s1, r2, c1, c2)
    for n, ref in enumerate(refs):
        for k in range(2):
            p = idx[6 + 2 * n + k]
            g_wi[:, pl.ds(pl.multiple_of(p * FB, 128), FB)] = ref[k, 0:192, :].astype(F32)
            rows = pl.ds(pl.multiple_of((p // 2) * 48, 16), 48)
            g_wa[rows, pl.ds(pl.multiple_of((p % 2) * FB, 128), FB)] = ref[k, 192:240, :].astype(F32)
            rows = pl.ds(pl.multiple_of((p % 2) * FB + (p // 2) * 96, 16), 96)
            g_wo[rows, 0:FB] = ref[k, 240:336, :].astype(F32)
            g_wo[rows, FB : 2 * FB] = ref[k, 336:432, :].astype(F32)


def out_qkv_kernel(idx, s1, r2, c1, c2, g_wq, g_wk, g_wv, g_bq, g_bv, g_bi, *six):
    FB = s1.shape[2]
    c, z = idx[0], idx[1]
    refs = (s1, r2, c1, c2)
    lower = lax.broadcasted_iota(jnp.int32, (96, 128), 1) < 64
    left, right = jnp.zeros((8, FB), F32), jnp.zeros((8, FB), F32)
    top = lax.broadcasted_iota(jnp.int32, (8, FB), 0) == 0
    for (n, k), (m, j) in (((0, 0), (2, 0)), ((0, 1), (3, 0)), ((1, 0), (2, 1)), ((1, 1), (3, 1))):
        p = idx[6 + 2 * n + k]
        yy, xx = p // 4, (p // 2) % 2
        own, other = refs[n].at[k], refs[m].at[j]

        def tile(i, swap):
            at = slice(0, 96) if i < 3 else slice(104, 200)
            cols = slice((i % 3) * 128, (i % 3 + 1) * 128)
            u, v = own[at, cols].astype(F32), other[at, cols].astype(F32)
            return jnp.where((c == 0) != swap, u, v)

        rows = pl.ds(pl.multiple_of(yy * 96, 8), 96)
        for ref, i, third, low in ((g_wq, 0, 3, True), (g_wk, 1, 4, True), (g_wv, 2, 3, False)):
            ta, tb = tile(third, False), tile(third, True)
            turned = pltpu.roll(tile(i, True), 64, 1)
            if not low:
                ta = pltpu.roll(ta, 64, 1)
            else:
                tb = pltpu.roll(tb, 64, 1)
            base = xx * 384
            ref[rows, pl.ds(pl.multiple_of(base, 128), 128)] = tile(i, False)
            ref[rows, pl.ds(pl.multiple_of(base + 128, 128), 128)] = jnp.where(lower, ta, turned)
            ref[rows, pl.ds(pl.multiple_of(base + 256, 128), 128)] = jnp.where(lower, turned, tb)
        for ref, cc in ((own, c), (other, 1 - c)):
            here = (yy == 0) & (~top | (xx * 2 + cc == z))
            left = left + jnp.where(here, ref[96:104, :].astype(F32), 0.0)
            right = right + jnp.where(here, ref[200:208, :].astype(F32), 0.0)
    g_bq[...] = jnp.concatenate([left[0:1, 0:128], right[0:1, 0:64]], axis=1).reshape(192)
    g_bv[...] = jnp.concatenate([left[0:1, 256:384], right[0:1, 64:128]], axis=1).reshape(192)
    for i, ref in enumerate(six):
        row = 1 + i // 3
        ref[...] = (left[row : row + 1, 0:192], left[row : row + 1, 192:384], right[row : row + 1, 0:192])[i % 3].reshape(192)
    g_bi[...] = jnp.concatenate([left[3:4, :], right[3:4, 0:192], left[4:5, 0:192]], axis=1).reshape(768)


def tie(*values):
    return lax.optimization_barrier(values)


def block(shape, *at):
    return pl.BlockSpec(shape, lambda i: at)


def call(kernel, outs, in_specs, out_specs, scratch=(), name=None, grid=()):
    return pl.pallas_call(
        kernel,
        out_shape=outs,
        grid=grid,
        in_specs=in_specs,
        out_specs=out_specs,
        scratch_shapes=list(scratch),
        compiler_params=pltpu.CompilerParams(vmem_limit_bytes=VMEM_LIMIT),
        cost_estimate=pl.CostEstimate(flops=1, bytes_accessed=1, transcendentals=0),
        name=name,
    )


def make_body(sizes):
    pg = sizes["pg"]
    order = [sizes[a] for a in AX]

    def send(fn, a):
        pairs = []
        for flat in range(math.prod(order)):
            at, rest = [], flat
            for n in reversed(order):
                at.append(rest % n)
                rest //= n
            dest = 0
            for n, v in zip(order, fn(*reversed(at))):
                dest = dest * n + v
            pairs.append((flat, dest))
        return lax.ppermute(a, AX, pairs)

    to_x = functools.partial(send, lambda s, g, x, c, z: (s, g, 1 - x, c, z))
    to_y = functools.partial(send, lambda s, g, x, c, z: (1 - s, g, x, c, z))
    to_core = functools.partial(send, lambda s, g, x, c, z: (s, g, x, 1 - c, z))
    to_z = [functools.partial(send, lambda s, g, x, c, z, k=k: (s, g, x, c, z ^ k)) for k in (1, 2, 3)]
    mix_a = functools.partial(send, lambda s, g, x, c, z: (s, g, 1 - x, c, z) if c == 0 else (1 - s, g, x, c, z))
    mix_b = functools.partial(send, lambda s, g, x, c, z: (1 - s, g, x, c, z) if c == 0 else (s, g, 1 - x, c, z))

    to_d = functools.partial(send, lambda s, g, x, c, z: (1 - s, g, 1 - x, c, z))

    def over_z(sent):
        return [f(v) for f, v in zip(to_z, sent if isinstance(sent, list) else [sent] * 3)]

    def body(
        tokens, cotangent, segment_ids, lengths, w_query, b_query, w_key, w_value, b_value, w_attn, b_attn,
        ln1_gain, ln1_shift, w_inner, b_inner, w_outer, b_outer, ln2_gain, ln2_shift,
    ):
        S, T, D = tokens.shape
        R = S * T
        y, x, c = (lax.axis_index(a) for a in ("seq", "x", "core"))
        mine, z = lax.axis_index("pg"), lax.axis_index("wt")
        h = x * 2 + c
        p = y * 4 + h
        L = 4 * pg * T
        FB = w_inner.shape[1] // 8

        a_of = jnp.where(c == 0, 2, 4)
        other = p ^ 1
        mates = [p, p ^ a_of, p ^ (6 - a_of), p ^ 6, other, other ^ (6 - a_of), other ^ a_of, other ^ 6]
        idx = jnp.stack([c, z, h, y, x, mine] + mates).astype(jnp.int32)

        vecs = (b_query, b_value, b_attn, ln1_gain, ln1_shift, b_outer, ln2_gain, ln2_shift, b_inner)
        w_own, pack, piece1, piece2 = call(
            prep_kernel,
            (
                jax.ShapeDtypeStruct((200, 576), BF), jax.ShapeDtypeStruct((104, 576), BF),
                jax.ShapeDtypeStruct((256, FB), BF), jax.ShapeDtypeStruct((96, D), BF),
            ),
            [SM] + [VM] * 15, (VM,) * 4, name="prep",
        )(idx, w_query, w_key, w_value, w_attn, w_inner, w_outer, *vecs)
        w_z = over_z(pack)
        tok_x, tok_c = to_x(tokens), to_core(tokens)
        w_z, tok_x, tok_c, piece1 = tie(w_z, tok_x, tok_c, piece1)
        w_y, tok_xc = to_y(jnp.stack(w_z)), to_core(tok_x)
        z1 = over_z(piece1)
        w_y, tok_xc, z1, piece2 = tie(w_y, tok_xc, z1, piece2)
        z2 = over_z(piece2)
        one = jnp.stack(z1)
        tok_xc, one = tie(tok_xc, one)
        one_a = mix_a(one)

        toks = [t[None] for t in (tokens, tok_x, tok_c, tok_xc)]
        if pg > 1:
            toks = [lax.all_gather(t, "pg", axis=0, tiled=True) for t in toks]
        head = jax.ShapeDtypeStruct((S, 3, L, 128), BF)
        own_head = jax.ShapeDtypeStruct((S, 3, 4 * T, 128), BF)
        q_aug, k_aug, v_aug, w_qkv = call(
            functools.partial(qkv_kernel, pg),
            (own_head, head, head, jax.ShapeDtypeStruct((4, 192, 576), BF)),
            [SM, SM] + [VM] * 4 + [ANY] * 5,
            (VM,) * 4,
            [pltpu.VMEM((4, 8, 576), BF), pltpu.SemaphoreType.DMA((11,))],
            name="qkv",
        )(lengths, idx, *toks, w_own, *w_z, w_y)
        w_qkv = w_qkv.reshape(D, 576)
        q_aug, one_a, z2 = tie(q_aug, one_a, z2)
        one, two = jnp.stack([one, one_a]), jnp.stack(z2)
        q_aug, one, two = tie(q_aug, one, two)
        one_b, two_a = mix_b(one), mix_a(two)
        o, q_aug = call(
            functools.partial(attn_fwd_kernel, 1024),
            (jax.ShapeDtypeStruct((4, T, 384), BF), own_head),
            [SM, SM] + [VM] * 3,
            (VM,) * 2,
            [pltpu.VMEM((3, T, 128), F32), pltpu.VMEM((3, T, 128), F32)],
            name="attn_fwd",
        )(lengths, idx, q_aug, k_aug, v_aug)
        o, one_b, two_a = tie(o, one_b, two_a)
        attn = lax.all_to_all(o, ("x", "core"), 0, 0, tiled=True)
        two = jnp.stack([two, two_a])
        two_b = mix_b(two)
        one = (one, one_b, to_core(one), to_core(one_b))
        attn, two_b = tie(attn, two_b)
        two = (two, two_b, to_core(two), to_core(two_b))

        layer_out, d_first, d_attn, sent, kept, extra = call(
            ffn_kernel,
            (
                jax.ShapeDtypeStruct((R, D), BF), jax.ShapeDtypeStruct((R, D), F32), jax.ShapeDtypeStruct((4, T, 384), BF),
                jax.ShapeDtypeStruct((R, 15 * FB), BF), jax.ShapeDtypeStruct((R, 9 * FB), BF), jax.ShapeDtypeStruct((4, 8, 576), F32),
            ),
            [SM, SM] + [VM] * 3 + [ANY] * 12,
            (VM, VM, VM, ANY, ANY, VM),
            [
                pltpu.VMEM((4, 192, 8 * FB), BF),
                pltpu.VMEM((4, 2 * FB, D), BF),
                pltpu.VMEM((4, 192, D), BF),
                pltpu.VMEM((4, 16, FB), BF),
                pltpu.VMEM((8, 8, FB), F32),
                pltpu.VMEM((R, D), BF),
                pltpu.VMEM((R, D), BF),
                pltpu.VMEM((R, D), F32),
                pltpu.VMEM((R, 128), F32),
                pltpu.VMEM((R, D), F32),
                pltpu.VMEM((R, 8 * FB), BF),
                pltpu.VMEM((R, 8 * FB), BF),
                pltpu.VMEM((R, D), BF),
                pltpu.VMEM((8, 8, D), F32),
                pltpu.SemaphoreType.DMA((79,)),
                pltpu.SemaphoreType.DMA((21,)),
            ],
            name="ffn",
        )(
            idx, lengths, attn, tokens.reshape(R, D), cotangent.reshape(R, D), piece1, w_inner, w_attn, w_outer, *one, *two
        )

        d_o = lax.all_to_all(d_attn, ("x", "core"), 0, 0, tiled=True)

        def add(*parts):
            return sum(v.astype(F32) for v in parts)

        def shares(n, m):
            return jax.ShapeDtypeStruct((*n, m), F32), *(jax.ShapeDtypeStruct((*n, m), BF),) * 3

        def attn_back(d_o):
            part = jax.ShapeDtypeStruct((4, 104, 576), BF)
            outs = (part, part, jax.ShapeDtypeStruct((4, R, D), BF))
            more = (w_qkv, tokens, tok_x, tok_c, tok_xc, extra)
            total = pltpu.VMEM((D + 8, 576), F32)
            res = call(
                functools.partial(attn_bwd_kernel, pg, 512),
                outs if pg == 1 else (jax.ShapeDtypeStruct((S, pg, 4, T, 576), BF),),
                [SM, SM] + [VM] * 5 + [VM if pg == 1 else ANY] * 6,
                (VM,) * (3 if pg == 1 else 1),
                [
                    pltpu.VMEM((3, 4 * T, 128), F32), pltpu.VMEM((3, L, 128), F32), pltpu.VMEM((3, L, 128), F32),
                    pltpu.VMEM((3, T, 128), BF), pltpu.VMEM((1, 4, T, 576), BF), total,
                ],
                name="attn_bwd",
            )(lengths, idx, q_aug, k_aug, v_aug, o, d_o, *more)
            if pg > 1:
                d = lax.psum_scatter(res[0], "pg", scatter_dimension=1, tiled=True)
                res = call(products_kernel, outs, [SM] + [VM] * 7, (VM,) * 3, [total], name="products")(idx, d, *more)
            return res

        part = jax.ShapeDtypeStruct((4, 96, D), BF)
        q1, c2, *sent2 = call(
            weight_kernel,
            (jax.ShapeDtypeStruct((4, 4, 240, FB), BF), jax.ShapeDtypeStruct((4, 96, D), F32)) + (part,) * 3,
            [SM] + [ANY] * 3, (VM,) * 5,
            [
                pltpu.VMEM((R, 9 * FB), BF), pltpu.VMEM((R, 3 * D), BF), pltpu.VMEM((R, 9 * FB), BF), pltpu.VMEM((R, 3 * D), BF),
                pltpu.SemaphoreType.DMA((12,)),
            ],
            name="weights",
        )(idx, kept, to_core(sent), sent)
        n, m = q1.shape[2:]
        d_o, sent2, q1 = tie(d_o, sent2, q1)
        got_z2, q1 = over_z(sent2), lax.all_to_all(q1, ("seq", "x"), 0, 0, tiled=True)
        gq_own, gq_other, gi = attn_back(d_o)
        gq_y = to_y(gq_other)
        c1, *sent1 = call(chunk_kernel, shares((n,), m), [SM, VM], (VM,) * 4, name="chunks1")(idx, q1)
        sent1, got_z2 = tie(sent1, got_z2)
        got_z1 = over_z(sent1)
        gi = lax.all_to_all(gi, ("x", "core"), 0, 0, tiled=True)
        cq, *sentq = call(chunkq_kernel, shares((104,), 576), [VM] * 2, (VM,) * 4, name="chunksq")(gq_own, gq_y)
        p2, *sent2 = call(sum2_kernel, shares((96,), D), [SM] + [VM] * 4, (VM,) * 4, name="sums2")(idx, c2, *got_z2)
        sent2, got_z1, sentq = tie(sent2, got_z1, sentq)
        got_zq = over_z(sentq)
        got_p2 = [f(v) for f, v in zip((to_x, to_y, to_d), sent2)]

        total = call(sum_kernel, jax.ShapeDtypeStruct((432, FB), BF), [VM] * 8, VM, name="sums")(c1, *got_z1, p2, *got_p2)
        total, got_zq = tie(total, got_zq)
        total_q = call(sumq_kernel, jax.ShapeDtypeStruct((208, FB), BF), [VM] * 4, VM, name="sumsq")(cq, *got_zq)
        if pg > 1:
            total, total_q = (lax.psum(v.astype(F32), "pg").astype(BF) for v in (total, total_q))

        mate, mate_q = mix_a(total), mix_a(total_q)
        s1 = jnp.stack([total, mate])
        r2, s1_core = mix_b(s1), to_core(s1)
        r2, s1_core, mate_q = tie(r2, s1_core, mate_q)
        s1_q = jnp.stack([total_q, mate_q])
        r2_q = mix_b(s1_q)
        grad_input = add(d_first, *(gi[k] for k in range(4))).astype(BF).reshape(tokens.shape)
        mat, wide = jax.ShapeDtypeStruct((192, D), F32), jax.ShapeDtypeStruct((192, 8 * FB), F32)
        vec, long_vec = jax.ShapeDtypeStruct((192,), F32), jax.ShapeDtypeStruct((2 * FB,), F32)
        g_wi, g_wa, g_wo = call(
            out_ffn_kernel, (wide, mat, jax.ShapeDtypeStruct((D, D), F32)), [SM] + [VM] * 4, (VM,) * 3, name="out_ffn"
        )(idx, s1, r2, s1_core, to_core(r2))
        g_wi, g_wa, g_wo, r2_q, grad_input = tie(g_wi, g_wa, g_wo, r2_q, grad_input)
        g_wq, g_wk, g_wv, g_bq, g_bv, g_bi, *six = call(
            out_qkv_kernel, (mat, mat, mat, vec, vec, long_vec) + (vec,) * 6, [SM] + [VM] * 4, (VM,) * 12, name="out_qkv"
        )(idx, s1_q, r2_q, to_core(s1_q), to_core(r2_q))
        return (
            layer_out.reshape(tokens.shape), grad_input,
            g_wq, g_bq, g_wk, g_wv, g_bv, g_wa, six[0], six[1], six[2], g_wi, g_bi, g_wo, six[3], six[4], six[5],
        )

    return body


def solution(mesh):
    sizes = dict(mesh.shape)
    pg = sizes["ctx"] // 4
    fine = dict(zip(AX, (sizes["seq"], pg, 2, 2, sizes["wt"])))
    split = Mesh(mesh.devices.reshape(tuple(fine.values())), AX)
    rows = P(("seq", "wt"), ("pg", "x", "core"), None)
    mat, vec = P("wt", None), P("wt")
    in_specs = (
        rows, rows, P(("seq", "wt"), ("pg", "x", "core")), P(("seq", "wt"), None),
        mat, vec, mat, mat, vec, mat, vec, vec, vec, mat, vec, mat, vec, vec, vec,
    )
    out_specs = (rows, rows, mat, vec, mat, mat, vec, mat, vec, vec, vec, mat, vec, mat, vec, vec, vec)
    return jax.shard_map(make_body(fine), mesh=split, in_specs=in_specs, out_specs=out_specs, check_vma=False)
```

```python
import functools
import math

import jax
import jax.numpy as jnp
from jax import lax
from jax.experimental import pallas as pl
from jax.experimental.pallas import tpu as pltpu
from jax.sharding import Mesh
from jax.sharding import PartitionSpec as P

NEG = -1000000000.0
EPS = 1e-05
BF = jnp.bfloat16
F32 = jnp.float32
AX = ("seq", "pg", "x", "core", "wt")
VM = pl.BlockSpec(memory_space=pltpu.VMEM)
SM = pl.BlockSpec(memory_space=pltpu.SMEM)
ANY = pl.BlockSpec(memory_space=pl.ANY)
OFFS = (0, 2, 1, 3)
VMEM_LIMIT = 60 * 2**20


def mm(a, b):
    return jnp.dot(a, b, preferred_element_type=F32)


def mm_nt(a, b):
    return lax.dot_general(a, b, (((1,), (1,)), ((), ())), preferred_element_type=F32)


def mm_tn(a, b):
    return lax.dot_general(a, b, (((0,), (0,)), ((), ())), preferred_element_type=F32)


def fold8(v):
    return jnp.sum(v.reshape(v.shape[0] // 8, 8, v.shape[1]), axis=0)


def limits(lengths, s, length):
    out = [jnp.int32(0)]
    for d in range(4):
        out.append(out[-1] + lengths[s, d])
    return out + [jnp.int32(length)]


def span(bounds, first, last):
    low, high = bounds[0], bounds[5]
    for d in range(1, 5):
        low = jnp.where(bounds[d] <= first, bounds[d], low)
        high = jnp.where(bounds[5 - d] > last, bounds[5 - d], high)
    return low, high


def prep_kernel(idx, wq, wk, wv, w_at, w_in, w_out, *rest):
    vecs, (w_own, pack, piece1, piece2) = rest[:9], rest[9:]
    c, h, y = idx[0], idx[2], idx[3]
    p = y * 4 + h
    FB = piece1.shape[1]
    for head in range(4):

        @pl.when(h == head)
        def _():
            a = head * 192
            for i, w in enumerate((wq, wk, wv)):
                w_own[0:192, i * 128 : (i + 1) * 128] = w[:, a : a + 128]
            w_own[0:192, 384:448] = wq[:, a + 128 : a + 192]
            w_own[0:192, 448:512] = wv[:, a + 128 : a + 192]
            w_own[0:192, 512:576] = wk[:, a + 128 : a + 192]

    bq, bv = (v[...].reshape(1, 192) for v in vecs[:2])
    w_own[192:200, :] = jnp.zeros((8, 576), BF)
    w_own[192:193, 0:128] = bq[:, 0:128]
    w_own[192:193, 256:384] = bv[:, 0:128]
    w_own[192:193, 384:448] = bq[:, 128:192]
    w_own[192:193, 448:512] = bv[:, 128:192]
    pack[0:96, :] = w_own[pl.ds(pl.multiple_of(y * 96, 16), 96), :]
    pack[96:104, :] = w_own[192:200, :]
    piece1[0:192, :] = w_in[:, pl.ds(pl.multiple_of(p * FB, 128), FB)]
    piece1[192:240, :] = w_at[pl.ds(pl.multiple_of((p // 2) * 48, 16), 48), pl.ds(pl.multiple_of(c * FB, 128), FB)]
    piece1[240:256, :] = jnp.zeros((16, FB), BF)
    for i, v in enumerate(vecs[:8]):
        piece1[240 + i : 241 + i, 0:192] = v[...].reshape(1, 192)
    for i in range(4):
        piece1[248 + i : 249 + i, 0:192] = vecs[8][i * 192 : (i + 1) * 192].reshape(1, 192)
    piece2[...] = w_out[pl.ds(pl.multiple_of(c * FB + (p // 2) * 96, 16), 96), :]


def qkv_kernel(pg, lengths, idx, *refs):
    toks, (w_own, w_z1, w_z2, w_z3, w_y, q_out, k_out, v_out, w, bs, sem) = refs[:4], refs[4:]
    z, c, y, mine = idx[1], idx[2], idx[3], idx[5]
    T, D = toks[0].shape[2:]
    copies = [(w_own.at[0:192], w.at[z]), (w_own.at[192:200], bs.at[0])]
    for k, ref in enumerate((w_z1, w_z2, w_z3)):
        copies.append((ref.at[0:96], w.at[z ^ (k + 1), pl.ds(pl.multiple_of(y * 96, 16), 96)]))
        copies.append((ref.at[96:104], bs.at[k + 1]))
        copies.append((w_y.at[k, 0:96], w.at[z ^ (k + 1), pl.ds(pl.multiple_of((1 - y) * 96, 16), 96)]))
    copies = [pltpu.make_async_copy(a, b, sem.at[i]) for i, (a, b) in enumerate(copies)]
    for cp in copies:
        cp.start()
    for cp in copies:
        cp.wait()
    lane = lax.broadcasted_iota(jnp.int32, (T, 128), 1)
    row = lax.broadcasted_iota(jnp.int32, (T, 128), 0)
    lower = lane < 64
    rel = lane & 63
    zero64 = jnp.zeros((T, 64), F32)

    bias = bs[c ^ z, 0:1, :].astype(F32)
    for g in range(pg):
        for n, off in enumerate(OFFS):
            place = pl.multiple_of((g * 4 + (c ^ off)) * T, T)
            own = pl.multiple_of((c ^ off) * T, T)
            pos = row + place
            for s in range(2):
                qkv = mm(toks[n][g, s], w[...].reshape(D, 576)) + bias
                qkv = qkv.astype(BF).astype(F32)
                seg = jnp.zeros((T, 128), jnp.int32)
                for start in limits(lengths, s, 0)[1:5]:
                    seg = seg + (pos >= start).astype(jnp.int32)
                hot = rel == seg
                q_aug = jnp.where(hot, 1.0, 0.0)
                k_aug = jnp.where(rel < 5, jnp.where(hot, 0.0, NEG), jnp.where(rel < 11, 1.0, 0.0))
                q01, k01, v01, q2v2 = (qkv[:, j * 128 : (j + 1) * 128] for j in range(4))
                k2 = jnp.concatenate([qkv[:, 512:576], zero64], axis=1)
                for h, (k, v) in enumerate(((k01, v01), (k01, v01), (k2, q2v2))):
                    half = ~lower if h == 1 else lower
                    k_out[s, h, pl.ds(place, T)] = jnp.where(half, k, k_aug).astype(BF)
                    half = lower if h == 0 else ~lower
                    v_out[s, h, pl.ds(place, T)] = jnp.where(half, v, 1.0).astype(BF)

                def store_q():
                    for h, q in enumerate((q01, q01, q2v2)):
                        half = ~lower if h == 1 else lower
                        q_out[s, h, pl.ds(own, T)] = jnp.where(half, q * 0.125, q_aug).astype(BF)

                if pg == 1:
                    store_q()
                else:
                    pl.when(mine == g)(store_q)


def attn_fwd_kernel(KC, lengths, idx, q_ref, k_ref, v_ref, o_ref, q_out, m_s, acc_s):
    mine = idx[5]
    T, L = o_ref.shape[1], k_ref.shape[2]
    lane = lax.broadcasted_iota(jnp.int32, (T, 128), 1)
    lower = lane < 64

    def per_tile(si, _):
        s, i = si // 4, si % 4
        here = pl.multiple_of(i * T, T)
        first = (mine * 4 + i) * T
        low, high = span(limits(lengths, s, L), first, first + T - 1)
        def whole(width):
            at = pl.multiple_of(jnp.minimum(low // T * T, L - width), T)
            for h in range(3):
                sc = mm_nt(q_ref[s, h, pl.ds(here, T)], k_ref[s, h, pl.ds(at, width)])
                parts = [sc[:, j * 128 : (j + 1) * 128] for j in range(width // 128)]
                top = jnp.max(functools.reduce(jnp.maximum, parts), axis=1, keepdims=True)
                top = jnp.broadcast_to(top, (T, 128))
                p = jnp.concatenate([jnp.exp(v - top).astype(BF) for v in parts], axis=1)
                acc_s[h] = mm(p, v_ref[s, h, pl.ds(at, width)])
                m_s[h] = top

        def running():
            for h in range(3):
                m_s[h] = jnp.full((T, 128), -jnp.inf, F32)
                acc_s[h] = jnp.zeros((T, 128), F32)

            def step(kt, _):
                at = pl.multiple_of(kt * KC, KC)
                for h in range(3):
                    sc = mm_nt(q_ref[s, h, pl.ds(here, T)], k_ref[s, h, pl.ds(at, KC)])
                    old = m_s[h]
                    parts = [sc[:, j * 128 : (j + 1) * 128] for j in range(KC // 128)]
                    top = functools.reduce(jnp.maximum, parts)
                    new = jnp.maximum(old, jnp.broadcast_to(jnp.max(top, axis=1, keepdims=True), (T, 128)))
                    p = jnp.concatenate([jnp.exp(v - new).astype(BF) for v in parts], axis=1)
                    acc_s[h] = acc_s[h] * jnp.exp(old - new) + mm(p, v_ref[s, h, pl.ds(at, KC)])
                    m_s[h] = new
                return 0

            lax.fori_loop(low // KC, (high + KC - 1) // KC, step, 0)

        tiles = (high + T - 1) // T - low // T
        pl.when(tiles <= 2)(functools.partial(whole, 2 * T))
        pl.when(tiles == 3)(functools.partial(whole, 3 * T))
        if L == 4 * T:
            pl.when(tiles == 4)(functools.partial(whole, 4 * T))
        else:
            pl.when(tiles > 3)(running)
        outs = []
        for h in range(3):
            acc = acc_s[h]
            turned = pltpu.roll(acc, 64, 1)
            data = lower if h == 0 else ~lower
            total = jnp.where(data, turned, acc)
            outs.append(acc / total)
            lse = m_s[h] + jnp.log(total)
            l1 = lse.astype(BF).astype(F32)
            l2 = (lse - l1).astype(BF).astype(F32)
            l3 = lse - l1 - l2
            at = lane if h == 1 else lane - 64
            q = q_ref[s, h, pl.ds(here, T)].astype(F32)
            q = jnp.where(at == 8, -l1, jnp.where(at == 9, -l2, jnp.where(at == 10, -l3, q)))
            q_out[s, h, pl.ds(here, T)] = q.astype(BF)
        o_ref[i, :, pl.ds(pl.multiple_of(s * 128, 128), 128)] = jnp.where(lower, outs[0], outs[1]).astype(BF)

        @pl.when(s == 0)
        def _():
            o_ref[i, :, 256:384] = pltpu.roll(outs[2], 64, 1).astype(BF)

        @pl.when(s == 1)
        def _():
            o_ref[i, :, 256:384] = jnp.where(lower, o_ref[i, :, 256:384].astype(F32), outs[2]).astype(BF)

        return 0

    lax.fori_loop(0, 8, per_tile, 0)


def attn_bwd_kernel(pg, KC, lengths, idx, *refs):
    ins, (w, t0, t1, t2, t3, extra), outs, scratch = refs[:5], refs[5:11], refs[11:-6], refs[-6:]
    gq_s = scratch[-1]
    for s in range(2):
        attn_bwd(pg, KC, s, lengths, idx, *ins, *scratch[:4], outs[0].at[s] if pg > 1 else scratch[4])
        if pg == 1:
            products(s, idx, scratch[4], w, (t0, t1, t2, t3), extra, gq_s, *outs)


def attn_bwd(pg, KC, s, lengths, idx, q_ref, k_ref, v_ref, o_ref, do_ref, dq_s, dk_s, dv_s, do_s, d_ref):
    c, mine = idx[2], idx[5]
    T, L = o_ref.shape[1], k_ref.shape[2]
    bounds = limits(lengths, s, L)
    lane = lax.broadcasted_iota(jnp.int32, (T, 128), 1)
    lower = lane < 64
    zero = jnp.zeros((T, 128), F32)

    dk_s[...] = jnp.zeros_like(dk_s)
    dv_s[...] = jnp.zeros_like(dv_s)
    live = bounds[4]
    cols = slice(s * 128, (s + 1) * 128)

    def per_tile(i, _):
        here = pl.multiple_of(i * T, T)
        first = (mine * 4 + i) * T
        low, high = span(bounds, first, first + T - 1)
        high = jnp.minimum(high, live)
        pair = do_ref[i, :, cols].astype(F32)
        third = do_ref[i, :, 256:384].astype(F32)
        if s == 0:
            third = pltpu.roll(third, 64, 1)
        o_third = o_ref[i, :, 256:384].astype(F32)
        if s == 0:
            o_third = pltpu.roll(o_third, 64, 1)
        prod = pair * o_ref[i, :, cols].astype(F32)
        for h in range(3):
            data = lower if h == 0 else ~lower
            full = prod if h < 2 else third * o_third
            delta = jnp.sum(jnp.where(data, full, zero), axis=1, keepdims=True)
            d1 = delta.astype(BF).astype(F32)
            d2 = (delta - d1).astype(BF).astype(F32)
            d3 = delta - d1 - d2
            at = lane - 64 if h == 0 else lane
            aug = jnp.where(at == 8, -d1, jnp.where(at == 9, -d2, jnp.where(at == 10, -d3, zero)))
            do_s[h] = jnp.where(data, pair if h < 2 else third, aug).astype(BF)
            dq_s[h, pl.ds(here, T)] = zero

        def step(kt, _):
            at = pl.multiple_of(kt * KC, KC)
            for h in range(3):
                q = q_ref[s, h, pl.ds(here, T)]
                k = k_ref[s, h, pl.ds(at, KC)]
                d = do_s[h]
                pt = jnp.exp(mm_nt(k, q))
                ds = (pt * mm_nt(v_ref[s, h, pl.ds(at, KC)], d)).astype(BF)
                dv_s[h, pl.ds(at, KC)] += mm(pt.astype(BF), d)
                dk_s[h, pl.ds(at, KC)] += mm(ds, q)
                dq_s[h, pl.ds(here, T)] += mm_tn(ds, k)
            return 0

        lax.fori_loop(low // KC, (high + KC - 1) // KC, step, 0)
        return 0

    lax.fori_loop(0, 4, per_tile, 0)
    for g in range(pg):
        for n, off in enumerate(OFFS):
            at = pl.multiple_of((g * 4 + (c ^ off)) * T, T)
            own = pl.multiple_of((c ^ off) * T, T)
            keep = 0.125 if pg == 1 else jnp.where(mine == g, 0.125, 0.0)
            dq = [dq_s[h, pl.ds(own, T)] * keep for h in range(3)]
            dk = [dk_s[h, pl.ds(at, T)] for h in range(3)]
            dv = [dv_s[h, pl.ds(at, T)] for h in range(3)]
            d_ref[g, n, :, 0:128] = jnp.where(lower, dq[0], dq[1]).astype(BF)
            d_ref[g, n, :, 128:256] = jnp.where(lower, dk[0], dk[1]).astype(BF)
            d_ref[g, n, :, 256:384] = jnp.where(lower, dv[0], dv[1]).astype(BF)
            d_ref[g, n, :, 384:512] = jnp.where(lower, dq[2], dv[2]).astype(BF)
            d_ref[g, n, :, 512:576] = dk[2][:, 0:64].astype(BF)


def products(s, idx, d, w, toks, extra, acc, gq_own, gq_other, gi):
    zw, h, y = idx[1], idx[2], idx[3]
    D = w.shape[0]
    T = d.shape[2]
    rows = slice(s * T, (s + 1) * T)
    for n, off in enumerate(OFFS):
        gi[h ^ off, rows, :] = mm_nt(d[0, n], w[...]).astype(BF)
    v = sum(mm_tn(t[s], d[0, n]) for n, t in enumerate(toks))
    col = sum(fold8(d[0, n].astype(F32)) for n in range(4))
    if s == 0:
        acc[0:D, :] = v
        acc[D : D + 8, :] = col
        return
    acc[0:D, :] += v
    col = jnp.sum(col + acc[D : D + 8, :], axis=0, keepdims=True)
    top = lax.broadcasted_iota(jnp.int32, (8, 576), 0) == 0
    for k in range(4):
        z = zw ^ k
        tail = jnp.where(top & (h == z), col, extra[z]).astype(BF)
        for ref, yy in ((gq_own, y), (gq_other, 1 - y)):
            ref[k, 0:96, :] = acc[pl.ds(pl.multiple_of(z * 192 + yy * 96, 8), 96), :].astype(BF)
            ref[k, 96:104, :] = tail


def gelu_parts(u):
    t = 1.0 / (1.0 + (0.3275911 * 0.7071067811865476) * jnp.abs(u))
    e = jnp.exp(-0.5 * u * u)
    poly = t * (
        0.127414796
        + t * (-0.142248368 + t * (0.7107068705 + t * (-0.7265760135 + t * 0.5307027145)))
    )
    tail = poly * e
    cdf = jnp.where(u >= 0, 1.0 - tail, tail)
    return u * cdf, cdf + u * e * 0.3989422804014327


def gather_heads(tiles):
    (pair0, third0), (pair1, third1) = tiles
    lower = lax.broadcasted_iota(jnp.int32, pair0.shape, 1) < 64
    turned = pltpu.roll(pair1, 64, 1)
    return pair0, jnp.where(lower, third0, turned), jnp.where(lower, turned, pltpu.roll(third1, 64, 1))


def ffn_kernel(
    idx, lengths, attn, tok, cot, sm_own, w_in, w_at, w_out,
    s1a, r2a, c1a, c2a, s1b, r2b, c1b, c2b,
    out, dfirst, dattn, sent, kept, extra,
    w1, w2, wa, sm, b1, att, hlow, xhat, rstd, acc, act, gp, dlow, sums, sem, osem,
):
    c, z, h, y, x, mine = (idx[i] for i in range(6))
    R, D = tok.shape
    T = attn.shape[1]
    FB = w_in.shape[1] // 8
    TR, GR = 256, 128
    first_copies = [(w_at, wa.at[z]), (sm_own.at[240:256], sm.at[0])]
    first_copies += [(s1a.at[0, k, 240:256], sm.at[k + 1]) for k in range(3)]
    copies = [(w_in, w1.at[z]), (w_out, w2.at[z])]
    for n, (ra, rb) in enumerate(((s1a, s1b), (r2a, r2b), (c1a, c1b), (c2a, c2b))):
        for k in range(2):
            p = idx[6 + 2 * n + k]
            q, half = p // 2, p % 2
            for kz in range(3):
                zz = z ^ (kz + 1)
                at = pl.ds(pl.multiple_of(half * FB, 128), FB)
                first_copies.append((ra.at[k, kz, 192:240], wa.at[zz, pl.ds(pl.multiple_of(q * 48, 16), 48), at]))
                copies.append((ra.at[k, kz, 0:192], w1.at[zz, :, pl.ds(pl.multiple_of(p * FB, 128), FB)]))
                copies.append((rb.at[k, kz], w2.at[zz, pl.ds(pl.multiple_of(half * FB + q * 96, 16), 96)]))
    many = len(first_copies)
    first_copies = [pltpu.make_async_copy(a, b, sem.at[i]) for i, (a, b) in enumerate(first_copies)]
    copies = [pltpu.make_async_copy(a, b, sem.at[many + i]) for i, (a, b) in enumerate(copies)]
    for cp in first_copies + copies:
        cp.start()

    sums[...] = jnp.zeros_like(sums)
    extra[...] = jnp.zeros_like(extra)

    lower = lax.broadcasted_iota(jnp.int32, (T, 128), 1) < 64
    for s in range(2):
        for g in range(0, 4, 2):
            tiles = []
            for n in (g, g + 1):
                third = attn[n, :, 256:384].astype(F32)
                tiles.append((
                    attn[n, :, s * 128 : (s + 1) * 128].astype(F32),
                    third if s == 0 else pltpu.roll(third, 64, 1),
                ))
            for j, tile in enumerate(gather_heads(tiles)):
                at = g * 192 + j * 128
                att[s * T : (s + 1) * T, at : at + 128] = tile.astype(BF)

    for cp in first_copies:
        cp.wait()

    def whole(i):
        return jnp.concatenate([sm[k ^ z, i : i + 1, 0:192].astype(F32) for k in range(4)], axis=1)

    b_attn, g1v, s1v, b_out, g2v, s2v = (whole(i) for i in range(2, 8))
    for k in range(4):
        row = jnp.concatenate([sm[k ^ z, i : i + 1, 0:192].astype(F32) for i in range(8, 12)], axis=1)
        for half in range(2):
            b1[2 * k + half, 0:1, :] = row[:, half * FB : (half + 1) * FB]

    acc[...] = mm(att[...], wa[...].reshape(D, D))

    def first(r, _):
        rows = pl.ds(pl.multiple_of(r * TR, TR), TR)
        v = acc[rows, :] + tok[rows, :].astype(F32) + b_attn
        mean = jnp.mean(v, axis=-1, keepdims=True)
        v = v - mean
        rs = lax.rsqrt(jnp.mean(v * v, axis=-1, keepdims=True) + EPS)
        xh = v * rs
        xhat[rows, :] = xh
        rstd[rows, :] = jnp.broadcast_to(rs, (TR, 128))
        hid = xh * g1v + s1v
        hlow[rows, :] = hid.astype(BF)
        acc[rows, :] = hid + b_out
        return 0

    lax.fori_loop(0, R // TR, first, 0)
    for cp in copies:
        cp.wait()

    def keep(src, i, cc, at):
        to = pl.ds(pl.multiple_of(i * FB, 128), FB)

        @pl.when(c == cc)
        def _():
            pltpu.make_async_copy(src, kept.at[:, to], osem.at[at]).start()

        @pl.when(c != cc)
        def _():
            pltpu.make_async_copy(src, sent.at[:, to], osem.at[at]).start()

    def kept_all(first, count):
        for i in range(first, first + count):
            pltpu.make_async_copy(act.at[:, 0:FB], kept.at[:, 0:FB], osem.at[i]).wait()

    def forward(zz, _):
        cols = pl.ds(pl.multiple_of(zz * D, 128), D)
        u = mm(hlow[...], w1[:, :, cols].reshape(D, D)) + jnp.concatenate([b1[2 * zz, 0:1, :], b1[2 * zz + 1, 0:1, :]], axis=1)
        for r in range(R // GR):
            rows = slice(r * GR, (r + 1) * GR)
            a, d = gelu_parts(u[rows])
            act[rows, cols] = a.astype(BF)
            gp[rows, cols] = d.astype(BF)
        acc[...] += mm(act[:, cols], w2[zz])
        for half in range(2):
            src = act.at[:, pl.ds(pl.multiple_of(zz * D + half * FB, 128), FB)]
            keep(src, zz, half, 2 * zz + half)
        return 0

    lax.fori_loop(0, 4, forward, 0)

    def second(r, _):
        rows = pl.ds(pl.multiple_of(r * TR, TR), TR)
        s = r // (T // TR)
        v = acc[rows, :]
        mean = jnp.mean(v, axis=-1, keepdims=True)
        v = v - mean
        rs = lax.rsqrt(jnp.mean(v * v, axis=-1, keepdims=True) + EPS)
        xh = v * rs
        out[rows, :] = (xh * g2v + s2v).astype(BF)
        place = (mine * 4 + h) * T + r * TR - s * T
        pos = lax.broadcasted_iota(jnp.int32, (TR, D), 0) + place
        dy = jnp.where(pos < limits(lengths, s, 0)[4], cot[rows, :].astype(F32), 0.0)
        sums[4] += fold8(dy * xh)
        sums[5] += fold8(dy)
        dx = dy * g2v
        m1 = jnp.mean(dx, axis=-1, keepdims=True)
        m2 = jnp.mean(dx * xh, axis=-1, keepdims=True)
        ds = rs * (dx - m1 - xh * m2)
        low = ds.astype(BF)
        dlow[rows, :] = low
        sums[3] += fold8(low.astype(F32))
        acc[rows, :] = ds
        return 0

    lax.fori_loop(0, R // TR, second, 0)

    kept_all(0, 8)
    shared = [(att, 9), (hlow, 11), (dlow, 13)]
    shared = [pltpu.make_async_copy(v, sent.at[:, i * FB : (i + 2) * FB], osem.at[n + 16]) for n, (v, i) in enumerate(shared)]
    for cp in shared:
        cp.start()

    def backward(zz, _):
        cols = pl.ds(pl.multiple_of(zz * D, 128), D)
        da = mm_nt(dlow[...], w2[zz])
        gsum = jnp.zeros((8, D), F32)
        for r in range(R // GR):
            rows = slice(r * GR, (r + 1) * GR)
            di = (da[rows] * gp[rows, cols].astype(F32)).astype(BF)
            act[rows, cols] = di
            gsum = gsum + fold8(di.astype(F32))
        acc[...] += mm_nt(act[:, cols], w1[:, :, cols].reshape(D, D))
        for half in range(2):
            src = act.at[:, pl.ds(pl.multiple_of(zz * D + half * FB, 128), FB)]
            keep(src, 4 + zz, half, 8 + 2 * zz + half)
        gsum = jnp.sum(gsum, axis=0, keepdims=True)
        extra[zz, 3:4, :] = gsum[:, 0:576]
        extra[zz, 4:5, 0:192] = gsum[:, 576:768]
        return 0

    lax.fori_loop(0, 4, backward, 0)
    for cp in shared:
        cp.wait()

    def last(r, _):
        rows = pl.ds(pl.multiple_of(r * TR, TR), TR)
        dy = acc[rows, :]
        xh = xhat[rows, :]
        sums[1] += fold8(dy * xh)
        sums[2] += fold8(dy)
        dx = dy * g1v
        m1 = jnp.mean(dx, axis=-1, keepdims=True)
        m2 = jnp.mean(dx * xh, axis=-1, keepdims=True)
        df = rstd[rows, :1] * (dx - m1 - xh * m2)
        dfirst[rows, :] = df
        low = df.astype(BF)
        dlow[rows, :] = low
        sums[0] += fold8(low.astype(F32))
        return 0

    lax.fori_loop(0, R // TR, last, 0)
    acc[...] = mm_nt(dlow[...], wa[...].reshape(D, D))
    for g in range(0, 4, 2):
        thirds = []
        for s in range(2):
            t0, t1, t2 = (acc[s * T : (s + 1) * T, g * 192 + j * 128 : g * 192 + (j + 1) * 128] for j in range(3))
            t1r, t2r = pltpu.roll(t1, 64, 1), pltpu.roll(t2, 64, 1)
            dattn[g, :, s * 128 : (s + 1) * 128] = t0.astype(BF)
            dattn[g + 1, :, s * 128 : (s + 1) * 128] = jnp.where(lower, t1r, t2r).astype(BF)
            thirds.append((t1, t1r, t2, t2r))
        (a1, _, _, a2r), (_, b1r, b2, _) = thirds
        dattn[g, :, 256:384] = jnp.where(lower, a1, b1r).astype(BF)
        dattn[g + 1, :, 256:384] = jnp.where(lower, a2r, b2).astype(BF)
    for half in range(2):
        keep(dlow.at[:, half * FB : (half + 1) * FB], 8, half, 19 + half)
    for i in range(6):
        row = jnp.sum(sums[i], axis=0, keepdims=True)
        for k in range(4):
            at = (i % 3) * 192
            extra[k, 1 + i // 3 : 2 + i // 3, at : at + 192] = row[:, k * 192 : (k + 1) * 192]
    kept_all(8, 8)
    kept_all(19, 2)


def weight_kernel(idx, kept, mate, sent, plane, mine, s1, s2, s3, units, shared, units2, shared2, plane_s, mine_s, sent_s, sem, osem):
    z = idx[1]
    D = shared.shape[1] // 3
    FB = D // 2
    wide = 4 * FB
    copies = []
    for refs, us, sh in (((kept, sent), units, shared), ((mate, mate), units2, shared2)):
        for at, size in ((wide, wide), (0, wide), (2 * wide, FB)):
            copies.append((refs[0].at[:, at : at + size], us.at[:, at : at + size]))
        for at in (D, 2 * D, 0):
            copies.append((refs[1].at[:, 9 * FB + at : 9 * FB + at + D], sh.at[:, at : at + D]))
    order = (1, 4, 7, 10, 0, 3, 6, 9, 2, 5, 8, 11)
    copies = [pltpu.make_async_copy(*copies[n], sem.at[n]) for n in order]
    for cp in copies:
        cp.start()
    for cp in copies[:4]:
        cp.wait()
    outs = []

    def emit(src, to):
        cp = pltpu.make_async_copy(src, to, osem.at[len(outs)])
        cp.start()
        outs.append(cp)

    for k in (1, 2, 3, 0):
        cols = pl.ds(pl.multiple_of((z ^ k) * FB, 128), FB)
        v = mm_tn(units[:, cols], shared[:, 2 * D : 3 * D]) + mm_tn(units2[:, cols], shared2[:, 2 * D : 3 * D])
        for q in range(4):
            if k == 0:
                mine_s[q] = v[q * 96 : (q + 1) * 96]
            else:
                sent_s[k - 1, q] = v[q * 96 : (q + 1) * 96].astype(BF)
        if k == 0:
            emit(mine_s, mine)
        else:
            emit(sent_s.at[k - 1], (s1, s2, s3)[k - 1])
    for cp in copies[4:]:
        cp.wait()
    v = mm_tn(shared[:, 0:D], units[:, 2 * wide : 2 * wide + FB]) + mm_tn(shared2[:, 0:D], units2[:, 2 * wide : 2 * wide + FB])
    v = v.astype(BF)
    for zz in range(4):
        for q in range(4):
            plane_s[q, zz, 192:240, :] = v[zz * 192 + q * 48 : zz * 192 + (q + 1) * 48]
    for n in range(2):
        cols = slice(wide + n * D, wide + (n + 1) * D)
        v = mm_tn(shared[:, D : 2 * D], units[:, cols]) + mm_tn(shared2[:, D : 2 * D], units2[:, cols])
        v = v.astype(BF)
        for i in range(2):
            for zz in range(4):
                plane_s[2 * n + i, zz, 0:192, :] = v[zz * 192 : (zz + 1) * 192, i * FB : (i + 1) * FB]
        emit(plane_s.at[2 * n : 2 * n + 2], plane.at[2 * n : 2 * n + 2])
    for cp in outs:
        cp.wait()


def products_kernel(idx, d, w, t0, t1, t2, t3, extra, *outs):
    for s in range(2):
        products(s, idx, d.at[s], w, (t0, t1, t2, t3), extra, outs[-1], *outs[:-1])


def chunkq_kernel(own, got, *outs):
    for k, ref in enumerate(outs):
        ref[...] = (own[k].astype(F32) + got[k].astype(F32)).astype(ref.dtype)


def chunk_kernel(idx, terms, *outs):
    z = idx[1]
    for k, ref in enumerate(outs):
        ref[...] = sum(terms[q, z ^ k].astype(F32) for q in range(4)).astype(ref.dtype)


def sum2_kernel(idx, a0, a1, a2, a3, *outs):
    here = idx[3] * 2 + idx[4]
    for k, ref in enumerate(outs):
        q = here ^ k
        ref[...] = (a0[q] + sum(a[q].astype(F32) for a in (a1, a2, a3))).astype(ref.dtype)


def sum_kernel(a0, a1, a2, a3, b0, b1, b2, b3, out):
    A, B = a0.shape
    C = b0.shape[0]
    out[0:A, :] = (a0[...] + sum(a[...].astype(F32) for a in (a1, a2, a3))).astype(BF)
    v = (b0[...] + sum(b[...].astype(F32) for b in (b1, b2, b3))).astype(BF)
    out[A : A + C, :] = v[:, :B]
    out[A + C : A + 2 * C, :] = v[:, B:]


def sumq_kernel(q0, q1, q2, q3, out):
    E, W = q0.shape
    B = out.shape[1]
    v = (q0[...] + sum(q[...].astype(F32) for q in (q1, q2, q3))).astype(BF)
    out[0:E, :] = v[:, :B]
    out[E : 2 * E, :] = jnp.zeros((E, B), BF)
    out[E : 2 * E, 0 : W - B] = v[:, B:]


def out_ffn_kernel(idx, s1, r2, c1, c2, g_wi, g_wa, g_wo):
    FB = s1.shape[2]
    refs = (s1, r2, c1, c2)
    for n, ref in enumerate(refs):
        for k in range(2):
            p = idx[6 + 2 * n + k]
            g_wi[:, pl.ds(pl.multiple_of(p * FB, 128), FB)] = ref[k, 0:192, :].astype(F32)
            rows = pl.ds(pl.multiple_of((p // 2) * 48, 16), 48)
            g_wa[rows, pl.ds(pl.multiple_of((p % 2) * FB, 128), FB)] = ref[k, 192:240, :].astype(F32)
            rows = pl.ds(pl.multiple_of((p % 2) * FB + (p // 2) * 96, 16), 96)
            g_wo[rows, 0:FB] = ref[k, 240:336, :].astype(F32)
            g_wo[rows, FB : 2 * FB] = ref[k, 336:432, :].astype(F32)


def out_qkv_kernel(idx, s1, r2, c1, c2, g_wq, g_wk, g_wv, g_bq, g_bv, g_bi, *six):
    FB = s1.shape[2]
    c, z = idx[0], idx[1]
    refs = (s1, r2, c1, c2)
    lower = lax.broadcasted_iota(jnp.int32, (96, 128), 1) < 64
    left, right = jnp.zeros((8, FB), F32), jnp.zeros((8, FB), F32)
    top = lax.broadcasted_iota(jnp.int32, (8, FB), 0) == 0
    for (n, k), (m, j) in (((0, 0), (2, 0)), ((0, 1), (3, 0)), ((1, 0), (2, 1)), ((1, 1), (3, 1))):
        p = idx[6 + 2 * n + k]
        yy, xx = p // 4, (p // 2) % 2
        own, other = refs[n].at[k], refs[m].at[j]

        def tile(i, swap):
            at = slice(0, 96) if i < 3 else slice(104, 200)
            cols = slice((i % 3) * 128, (i % 3 + 1) * 128)
            u, v = own[at, cols].astype(F32), other[at, cols].astype(F32)
            return jnp.where((c == 0) != swap, u, v)

        rows = pl.ds(pl.multiple_of(yy * 96, 8), 96)
        for ref, i, third, low in ((g_wq, 0, 3, True), (g_wk, 1, 4, True), (g_wv, 2, 3, False)):
            ta, tb = tile(third, False), tile(third, True)
            turned = pltpu.roll(tile(i, True), 64, 1)
            if not low:
                ta = pltpu.roll(ta, 64, 1)
            else:
                tb = pltpu.roll(tb, 64, 1)
            base = xx * 384
            ref[rows, pl.ds(pl.multiple_of(base, 128), 128)] = tile(i, False)
            ref[rows, pl.ds(pl.multiple_of(base + 128, 128), 128)] = jnp.where(lower, ta, turned)
            ref[rows, pl.ds(pl.multiple_of(base + 256, 128), 128)] = jnp.where(lower, turned, tb)
        for ref, cc in ((own, c), (other, 1 - c)):
            here = (yy == 0) & (~top | (xx * 2 + cc == z))
            left = left + jnp.where(here, ref[96:104, :].astype(F32), 0.0)
            right = right + jnp.where(here, ref[200:208, :].astype(F32), 0.0)
    g_bq[...] = jnp.concatenate([left[0:1, 0:128], right[0:1, 0:64]], axis=1).reshape(192)
    g_bv[...] = jnp.concatenate([left[0:1, 256:384], right[0:1, 64:128]], axis=1).reshape(192)
    for i, ref in enumerate(six):
        row = 1 + i // 3
        ref[...] = (left[row : row + 1, 0:192], left[row : row + 1, 192:384], right[row : row + 1, 0:192])[i % 3].reshape(192)
    g_bi[...] = jnp.concatenate([left[3:4, :], right[3:4, 0:192], left[4:5, 0:192]], axis=1).reshape(768)


def tie(*values):
    return lax.optimization_barrier(values)


def block(shape, *at):
    return pl.BlockSpec(shape, lambda i: at)


def call(kernel, outs, in_specs, out_specs, scratch=(), name=None, grid=()):
    return pl.pallas_call(
        kernel,
        out_shape=outs,
        grid=grid,
        in_specs=in_specs,
        out_specs=out_specs,
        scratch_shapes=list(scratch),
        compiler_params=pltpu.CompilerParams(vmem_limit_bytes=VMEM_LIMIT),
        cost_estimate=pl.CostEstimate(flops=1, bytes_accessed=1, transcendentals=0),
        name=name,
    )


def make_body(sizes):
    pg = sizes["pg"]
    order = [sizes[a] for a in AX]

    def send(fn, a):
        pairs = []
        for flat in range(math.prod(order)):
            at, rest = [], flat
            for n in reversed(order):
                at.append(rest % n)
                rest //= n
            dest = 0
            for n, v in zip(order, fn(*reversed(at))):
                dest = dest * n + v
            pairs.append((flat, dest))
        return lax.ppermute(a, AX, pairs)

    to_x = functools.partial(send, lambda s, g, x, c, z: (s, g, 1 - x, c, z))
    to_y = functools.partial(send, lambda s, g, x, c, z: (1 - s, g, x, c, z))
    to_core = functools.partial(send, lambda s, g, x, c, z: (s, g, x, 1 - c, z))
    to_z = [functools.partial(send, lambda s, g, x, c, z, k=k: (s, g, x, c, z ^ k)) for k in (1, 2, 3)]
    mix_a = functools.partial(send, lambda s, g, x, c, z: (s, g, 1 - x, c, z) if c == 0 else (1 - s, g, x, c, z))
    mix_b = functools.partial(send, lambda s, g, x, c, z: (1 - s, g, x, c, z) if c == 0 else (s, g, 1 - x, c, z))

    to_d = functools.partial(send, lambda s, g, x, c, z: (1 - s, g, 1 - x, c, z))

    def over_z(sent):
        return [f(v) for f, v in zip(to_z, sent if isinstance(sent, list) else [sent] * 3)]

    def body(
        tokens, cotangent, segment_ids, lengths, w_query, b_query, w_key, w_value, b_value, w_attn, b_attn,
        ln1_gain, ln1_shift, w_inner, b_inner, w_outer, b_outer, ln2_gain, ln2_shift,
    ):
        S, T, D = tokens.shape
        R = S * T
        y, x, c = (lax.axis_index(a) for a in ("seq", "x", "core"))
        mine, z = lax.axis_index("pg"), lax.axis_index("wt")
        h = x * 2 + c
        p = y * 4 + h
        L = 4 * pg * T
        FB = w_inner.shape[1] // 8

        a_of = jnp.where(c == 0, 2, 4)
        other = p ^ 1
        mates = [p, p ^ a_of, p ^ (6 - a_of), p ^ 6, other, other ^ (6 - a_of), other ^ a_of, other ^ 6]
        idx = jnp.stack([c, z, h, y, x, mine] + mates).astype(jnp.int32)

        vecs = (b_query, b_value, b_attn, ln1_gain, ln1_shift, b_outer, ln2_gain, ln2_shift, b_inner)
        w_own, pack, piece1, piece2 = call(
            prep_kernel,
            (
                jax.ShapeDtypeStruct((200, 576), BF), jax.ShapeDtypeStruct((104, 576), BF),
                jax.ShapeDtypeStruct((256, FB), BF), jax.ShapeDtypeStruct((96, D), BF),
            ),
            [SM] + [VM] * 15, (VM,) * 4, name="prep",
        )(idx, w_query, w_key, w_value, w_attn, w_inner, w_outer, *vecs)
        w_z = over_z(pack)
        tok_x, tok_c = to_x(tokens), to_core(tokens)
        w_z, tok_x, tok_c, piece1 = tie(w_z, tok_x, tok_c, piece1)
        w_y, tok_xc = to_y(jnp.stack(w_z)), to_core(tok_x)
        z1 = over_z(piece1)
        w_y, tok_xc, z1, piece2 = tie(w_y, tok_xc, z1, piece2)
        z2 = over_z(piece2)
        one = jnp.stack(z1)
        tok_xc, one = tie(tok_xc, one)
        one_a = mix_a(one)

        toks = [t[None] for t in (tokens, tok_x, tok_c, tok_xc)]
        if pg > 1:
            toks = [lax.all_gather(t, "pg", axis=0, tiled=True) for t in toks]
        head = jax.ShapeDtypeStruct((S, 3, L, 128), BF)
        own_head = jax.ShapeDtypeStruct((S, 3, 4 * T, 128), BF)
        q_aug, k_aug, v_aug, w_qkv = call(
            functools.partial(qkv_kernel, pg),
            (own_head, head, head, jax.ShapeDtypeStruct((4, 192, 576), BF)),
            [SM, SM] + [VM] * 4 + [ANY] * 5,
            (VM,) * 4,
            [pltpu.VMEM((4, 8, 576), BF), pltpu.SemaphoreType.DMA((11,))],
            name="qkv",
        )(lengths, idx, *toks, w_own, *w_z, w_y)
        w_qkv = w_qkv.reshape(D, 576)
        q_aug, one_a, z2 = tie(q_aug, one_a, z2)
        one, two = jnp.stack([one, one_a]), jnp.stack(z2)
        q_aug, one, two = tie(q_aug, one, two)
        one_b, two_a = mix_b(one), mix_a(two)
        o, q_aug = call(
            functools.partial(attn_fwd_kernel, 1024),
            (jax.ShapeDtypeStruct((4, T, 384), BF), own_head),
            [SM, SM] + [VM] * 3,
            (VM,) * 2,
            [pltpu.VMEM((3, T, 128), F32), pltpu.VMEM((3, T, 128), F32)],
            name="attn_fwd",
        )(lengths, idx, q_aug, k_aug, v_aug)
        o, one_b, two_a = tie(o, one_b, two_a)
        attn = lax.all_to_all(o, ("x", "core"), 0, 0, tiled=True)
        two = jnp.stack([two, two_a])
        two_b = mix_b(two)
        one = (one, one_b, to_core(one), to_core(one_b))
        attn, two_b = tie(attn, two_b)
        two = (two, two_b, to_core(two), to_core(two_b))

        layer_out, d_first, d_attn, sent, kept, extra = call(
            ffn_kernel,
            (
                jax.ShapeDtypeStruct((R, D), BF), jax.ShapeDtypeStruct((R, D), F32), jax.ShapeDtypeStruct((4, T, 384), BF),
                jax.ShapeDtypeStruct((R, 15 * FB), BF), jax.ShapeDtypeStruct((R, 9 * FB), BF), jax.ShapeDtypeStruct((4, 8, 576), F32),
            ),
            [SM, SM] + [VM] * 3 + [ANY] * 12,
            (VM, VM, VM, ANY, ANY, VM),
            [
                pltpu.VMEM((4, 192, 8 * FB), BF),
                pltpu.VMEM((4, 2 * FB, D), BF),
                pltpu.VMEM((4, 192, D), BF),
                pltpu.VMEM((4, 16, FB), BF),
                pltpu.VMEM((8, 8, FB), F32),
                pltpu.VMEM((R, D), BF),
                pltpu.VMEM((R, D), BF),
                pltpu.VMEM((R, D), F32),
                pltpu.VMEM((R, 128), F32),
                pltpu.VMEM((R, D), F32),
                pltpu.VMEM((R, 8 * FB), BF),
                pltpu.VMEM((R, 8 * FB), BF),
                pltpu.VMEM((R, D), BF),
                pltpu.VMEM((8, 8, D), F32),
                pltpu.SemaphoreType.DMA((79,)),
                pltpu.SemaphoreType.DMA((21,)),
            ],
            name="ffn",
        )(
            idx, lengths, attn, tokens.reshape(R, D), cotangent.reshape(R, D), piece1, w_inner, w_attn, w_outer, *one, *two
        )

        d_o = lax.all_to_all(d_attn, ("x", "core"), 0, 0, tiled=True)

        def add(*parts):
            return sum(v.astype(F32) for v in parts)

        def shares(n, m):
            return jax.ShapeDtypeStruct((*n, m), F32), *(jax.ShapeDtypeStruct((*n, m), BF),) * 3

        def attn_back(d_o):
            part = jax.ShapeDtypeStruct((4, 104, 576), BF)
            outs = (part, part, jax.ShapeDtypeStruct((4, R, D), BF))
            more = (w_qkv, tokens, tok_x, tok_c, tok_xc, extra)
            total = pltpu.VMEM((D + 8, 576), F32)
            res = call(
                functools.partial(attn_bwd_kernel, pg, 512),
                outs if pg == 1 else (jax.ShapeDtypeStruct((S, pg, 4, T, 576), BF),),
                [SM, SM] + [VM] * 5 + [VM if pg == 1 else ANY] * 6,
                (VM,) * (3 if pg == 1 else 1),
                [
                    pltpu.VMEM((3, 4 * T, 128), F32), pltpu.VMEM((3, L, 128), F32), pltpu.VMEM((3, L, 128), F32),
                    pltpu.VMEM((3, T, 128), BF), pltpu.VMEM((1, 4, T, 576), BF), total,
                ],
                name="attn_bwd",
            )(lengths, idx, q_aug, k_aug, v_aug, o, d_o, *more)
            if pg > 1:
                d = lax.psum_scatter(res[0], "pg", scatter_dimension=1, tiled=True)
                res = call(products_kernel, outs, [SM] + [VM] * 7, (VM,) * 3, [total], name="products")(idx, d, *more)
            return res

        part = jax.ShapeDtypeStruct((4, 96, D), BF)
        q1, c2, *sent2 = call(
            weight_kernel,
            (jax.ShapeDtypeStruct((4, 4, 240, FB), BF), jax.ShapeDtypeStruct((4, 96, D), F32)) + (part,) * 3,
            [SM] + [ANY] * 3, (ANY,) * 5,
            [
                pltpu.VMEM((R, 9 * FB), BF), pltpu.VMEM((R, 3 * D), BF), pltpu.VMEM((R, 9 * FB), BF), pltpu.VMEM((R, 3 * D), BF),
                pltpu.VMEM((4, 4, 240, FB), BF), pltpu.VMEM((4, 96, D), F32),
                pltpu.VMEM((3, 4, 96, D), BF), pltpu.SemaphoreType.DMA((12,)), pltpu.SemaphoreType.DMA((6,)),
            ],
            name="weights",
        )(idx, kept, to_core(sent), sent)
        n, m = q1.shape[2:]
        d_o, sent2, q1 = tie(d_o, sent2, q1)
        got_z2, q1 = over_z(sent2), lax.all_to_all(q1, ("seq", "x"), 0, 0, tiled=True)
        gq_own, gq_other, gi = attn_back(d_o)
        gq_y = to_y(gq_other)
        c1, *sent1 = call(chunk_kernel, shares((n,), m), [SM, VM], (VM,) * 4, name="chunks1")(idx, q1)
        sent1, got_z2 = tie(sent1, got_z2)
        got_z1 = over_z(sent1)
        gi = lax.all_to_all(gi, ("x", "core"), 0, 0, tiled=True)
        cq, *sentq = call(chunkq_kernel, shares((104,), 576), [VM] * 2, (VM,) * 4, name="chunksq")(gq_own, gq_y)
        p2, *sent2 = call(sum2_kernel, shares((96,), D), [SM] + [VM] * 4, (VM,) * 4, name="sums2")(idx, c2, *got_z2)
        sent2, got_z1, sentq = tie(sent2, got_z1, sentq)
        got_zq = over_z(sentq)
        got_p2 = [f(v) for f, v in zip((to_x, to_y, to_d), sent2)]

        total = call(sum_kernel, jax.ShapeDtypeStruct((432, FB), BF), [VM] * 8, VM, name="sums")(c1, *got_z1, p2, *got_p2)
        total, got_zq = tie(total, got_zq)
        total_q = call(sumq_kernel, jax.ShapeDtypeStruct((208, FB), BF), [VM] * 4, VM, name="sumsq")(cq, *got_zq)
        if pg > 1:
            total, total_q = (lax.psum(v.astype(F32), "pg").astype(BF) for v in (total, total_q))

        mate, mate_q = mix_a(total), mix_a(total_q)
        s1 = jnp.stack([total, mate])
        r2, s1_core = mix_b(s1), to_core(s1)
        r2, s1_core, mate_q = tie(r2, s1_core, mate_q)
        s1_q = jnp.stack([total_q, mate_q])
        r2_q = mix_b(s1_q)
        grad_input = add(d_first, *(gi[k] for k in range(4))).astype(BF).reshape(tokens.shape)
        mat, wide = jax.ShapeDtypeStruct((192, D), F32), jax.ShapeDtypeStruct((192, 8 * FB), F32)
        vec, long_vec = jax.ShapeDtypeStruct((192,), F32), jax.ShapeDtypeStruct((2 * FB,), F32)
        g_wi, g_wa, g_wo = call(
            out_ffn_kernel, (wide, mat, jax.ShapeDtypeStruct((D, D), F32)), [SM] + [VM] * 4, (VM,) * 3, name="out_ffn"
        )(idx, s1, r2, s1_core, to_core(r2))
        g_wi, g_wa, g_wo, r2_q, grad_input = tie(g_wi, g_wa, g_wo, r2_q, grad_input)
        g_wq, g_wk, g_wv, g_bq, g_bv, g_bi, *six = call(
            out_qkv_kernel, (mat, mat, mat, vec, vec, long_vec) + (vec,) * 6, [SM] + [VM] * 4, (VM,) * 12, name="out_qkv"
        )(idx, s1_q, r2_q, to_core(s1_q), to_core(r2_q))
        return (
            layer_out.reshape(tokens.shape), grad_input,
            g_wq, g_bq, g_wk, g_wv, g_bv, g_wa, six[0], six[1], six[2], g_wi, g_bi, g_wo, six[3], six[4], six[5],
        )

    return body


def solution(mesh):
    sizes = dict(mesh.shape)
    pg = sizes["ctx"] // 4
    fine = dict(zip(AX, (sizes["seq"], pg, 2, 2, sizes["wt"])))
    split = Mesh(mesh.devices.reshape(tuple(fine.values())), AX)
    rows = P(("seq", "wt"), ("pg", "x", "core"), None)
    mat, vec = P("wt", None), P("wt")
    in_specs = (
        rows, rows, P(("seq", "wt"), ("pg", "x", "core")), P(("seq", "wt"), None),
        mat, vec, mat, mat, vec, mat, vec, vec, vec, mat, vec, mat, vec, vec, vec,
    )
    out_specs = (rows, rows, mat, vec, mat, mat, vec, mat, vec, vec, vec, mat, vec, mat, vec, vec, vec)
    return jax.shard_map(make_body(fine), mesh=split, in_specs=in_specs, out_specs=out_specs, check_vma=False)
```

```python
import functools
import math

import jax
import jax.numpy as jnp
from jax import lax
from jax.experimental import pallas as pl
from jax.experimental.pallas import tpu as pltpu
from jax.sharding import Mesh
from jax.sharding import PartitionSpec as P

NEG = -1000000000.0
EPS = 1e-05
BF = jnp.bfloat16
F32 = jnp.float32
AX = ("seq", "pg", "x", "core", "wt")
VM = pl.BlockSpec(memory_space=pltpu.VMEM)
SM = pl.BlockSpec(memory_space=pltpu.SMEM)
ANY = pl.BlockSpec(memory_space=pl.ANY)
OFFS = (0, 2, 1, 3)
VMEM_LIMIT = 60 * 2**20
GQ = 112


def mm(a, b):
    return jnp.dot(a, b, preferred_element_type=F32)


def mm_nt(a, b):
    return lax.dot_general(a, b, (((1,), (1,)), ((), ())), preferred_element_type=F32)


def mm_tn(a, b):
    return lax.dot_general(a, b, (((0,), (0,)), ((), ())), preferred_element_type=F32)


def fold8(v):
    return jnp.sum(v.reshape(v.shape[0] // 8, 8, v.shape[1]), axis=0)


def limits(lengths, s, length):
    out = [jnp.int32(0)]
    for d in range(4):
        out.append(out[-1] + lengths[s, d])
    return out + [jnp.int32(length)]


def span(bounds, first, last):
    low, high = bounds[0], bounds[5]
    for d in range(1, 5):
        low = jnp.where(bounds[d] <= first, bounds[d], low)
        high = jnp.where(bounds[5 - d] > last, bounds[5 - d], high)
    return low, high


def prep_kernel(idx, wq, wk, wv, w_at, w_in, w_out, *rest):
    vecs, (w_own, pack, piece1, piece2) = rest[:9], rest[9:]
    c, h, y = idx[0], idx[2], idx[3]
    p = y * 4 + h
    FB = piece1.shape[1]
    for head in range(4):

        @pl.when(h == head)
        def _():
            a = head * 192
            for i, w in enumerate((wq, wk, wv)):
                w_own[0:192, i * 128 : (i + 1) * 128] = w[:, a : a + 128]
            w_own[0:192, 384:448] = wq[:, a + 128 : a + 192]
            w_own[0:192, 448:512] = wv[:, a + 128 : a + 192]
            w_own[0:192, 512:576] = wk[:, a + 128 : a + 192]

    row = lax.broadcasted_iota(jnp.int32, (16, 576), 0)
    bq, bv = (v[...].astype(F32).reshape(1, 192) for v in vecs[:2])
    none = jnp.zeros((1, 128), F32)
    bias = jnp.concatenate([bq[:, :128], none, bv[:, :128], bq[:, 128:], bv[:, 128:], none[:, :64]], axis=1)
    w_own[192:208, :] = jnp.where(row == 0, jnp.broadcast_to(bias, (16, 576)), 0.0).astype(BF)
    pack[0:96, :] = w_own[pl.ds(pl.multiple_of(y * 96, 16), 96), :]
    pack[96:112, :] = w_own[192:208, :]
    piece1[0:192, :] = w_in[:, pl.ds(pl.multiple_of(p * FB, 128), FB)]
    piece1[192:240, :] = w_at[pl.ds(pl.multiple_of((p // 2) * 48, 16), 48), pl.ds(pl.multiple_of(c * FB, 128), FB)]
    row = lax.broadcasted_iota(jnp.int32, (16, FB), 0)
    long = vecs[8][...].astype(F32).reshape(1, 768)
    small = [v[...].astype(F32).reshape(1, 192) for v in vecs[:8]] + [long[:, i * 192 : (i + 1) * 192] for i in range(4)]
    tall = jnp.zeros((16, FB), F32)
    for i, v in enumerate(small):
        v = jnp.concatenate([v, jnp.zeros((1, FB - 192), F32)], axis=1)
        tall = jnp.where(row == i, jnp.broadcast_to(v, (16, FB)), tall)
    piece1[240:256, :] = tall.astype(BF)
    piece2[...] = w_out[pl.ds(pl.multiple_of(c * FB + (p // 2) * 96, 16), 96), :]


def qkv_kernel(pg, lengths, idx, *refs):
    toks, (w_own, w_z1, w_z2, w_z3, w_y, q_out, k_out, v_out, w, bs, sem) = refs[:4], refs[4:]
    z, c, y, mine = idx[1], idx[2], idx[3], idx[5]
    T, D = toks[0].shape[2:]
    copies = [(w_own.at[0:192], w.at[z]), (w_own.at[192:208], bs.at[0])]
    for k, ref in enumerate((w_z1, w_z2, w_z3)):
        copies.append((ref.at[0:96], w.at[z ^ (k + 1), pl.ds(pl.multiple_of(y * 96, 16), 96)]))
        copies.append((ref.at[96:112], bs.at[k + 1]))
        copies.append((w_y.at[k, 0:96], w.at[z ^ (k + 1), pl.ds(pl.multiple_of((1 - y) * 96, 16), 96)]))
    copies = [pltpu.make_async_copy(a, b, sem.at[i]) for i, (a, b) in enumerate(copies)]
    for cp in copies:
        cp.start()
    for cp in copies:
        cp.wait()
    lane = lax.broadcasted_iota(jnp.int32, (T, 128), 1)
    row = lax.broadcasted_iota(jnp.int32, (T, 128), 0)
    lower = lane < 64
    rel = lane & 63
    zero64 = jnp.zeros((T, 64), F32)

    bias = bs[c ^ z].astype(F32)[0:1]
    for g in range(pg):
        for n, off in enumerate(OFFS):
            place = pl.multiple_of((g * 4 + (c ^ off)) * T, T)
            own = pl.multiple_of((c ^ off) * T, T)
            pos = row + place
            for s in range(2):
                qkv = mm(toks[n][g, s], w[...].reshape(D, 576)) + bias
                qkv = qkv.astype(BF).astype(F32)
                seg = jnp.zeros((T, 128), jnp.int32)
                for start in limits(lengths, s, 0)[1:5]:
                    seg = seg + (pos >= start).astype(jnp.int32)
                hot = rel == seg
                q_aug = jnp.where(hot, 1.0, 0.0)
                k_aug = jnp.where(rel < 5, jnp.where(hot, 0.0, NEG), jnp.where(rel < 11, 1.0, 0.0))
                q01, k01, v01, q2v2 = (qkv[:, j * 128 : (j + 1) * 128] for j in range(4))
                k2 = jnp.concatenate([qkv[:, 512:576], zero64], axis=1)
                for h, (k, v) in enumerate(((k01, v01), (k01, v01), (k2, q2v2))):
                    half = ~lower if h == 1 else lower
                    k_out[s, h, pl.ds(place, T)] = jnp.where(half, k, k_aug).astype(BF)
                    half = lower if h == 0 else ~lower
                    v_out[s, h, pl.ds(place, T)] = jnp.where(half, v, 1.0).astype(BF)

                def store_q():
                    for h, q in enumerate((q01, q01, q2v2)):
                        half = ~lower if h == 1 else lower
                        q_out[s, h, pl.ds(own, T)] = jnp.where(half, q * 0.125, q_aug).astype(BF)

                if pg == 1:
                    store_q()
                else:
                    pl.when(mine == g)(store_q)


def attn_fwd_kernel(KC, lengths, idx, q_ref, k_ref, v_ref, o_ref, q_out, m_s, acc_s):
    mine = idx[5]
    T, L = o_ref.shape[1], k_ref.shape[2]
    lane = lax.broadcasted_iota(jnp.int32, (T, 128), 1)
    lower = lane < 64

    def per_tile(si, _):
        s, i = si // 4, si % 4
        here = pl.multiple_of(i * T, T)
        first = (mine * 4 + i) * T
        low, high = span(limits(lengths, s, L), first, first + T - 1)
        def whole(width):
            at = pl.multiple_of(jnp.minimum(low // T * T, L - width), T)
            for h in range(3):
                sc = mm_nt(q_ref[s, h, pl.ds(here, T)], k_ref[s, h, pl.ds(at, width)])
                parts = [sc[:, j * 128 : (j + 1) * 128] for j in range(width // 128)]
                top = jnp.max(functools.reduce(jnp.maximum, parts), axis=1, keepdims=True)
                top = jnp.broadcast_to(top, (T, 128))
                p = jnp.concatenate([jnp.exp(v - top).astype(BF) for v in parts], axis=1)
                acc_s[h] = mm(p, v_ref[s, h, pl.ds(at, width)])
                m_s[h] = top

        def running():
            for h in range(3):
                m_s[h] = jnp.full((T, 128), -jnp.inf, F32)
                acc_s[h] = jnp.zeros((T, 128), F32)

            def step(kt, _):
                at = pl.multiple_of(kt * KC, KC)
                for h in range(3):
                    sc = mm_nt(q_ref[s, h, pl.ds(here, T)], k_ref[s, h, pl.ds(at, KC)])
                    old = m_s[h]
                    parts = [sc[:, j * 128 : (j + 1) * 128] for j in range(KC // 128)]
                    top = functools.reduce(jnp.maximum, parts)
                    new = jnp.maximum(old, jnp.broadcast_to(jnp.max(top, axis=1, keepdims=True), (T, 128)))
                    p = jnp.concatenate([jnp.exp(v - new).astype(BF) for v in parts], axis=1)
                    acc_s[h] = acc_s[h] * jnp.exp(old - new) + mm(p, v_ref[s, h, pl.ds(at, KC)])
                    m_s[h] = new
                return 0

            lax.fori_loop(low // KC, (high + KC - 1) // KC, step, 0)

        tiles = (high + T - 1) // T - low // T
        pl.when(tiles <= 2)(functools.partial(whole, 2 * T))
        pl.when(tiles == 3)(functools.partial(whole, 3 * T))
        if L == 4 * T:
            pl.when(tiles == 4)(functools.partial(whole, 4 * T))
        else:
            pl.when(tiles > 3)(running)
        outs = []
        for h in range(3):
            acc = acc_s[h]
            turned = pltpu.roll(acc, 64, 1)
            data = lower if h == 0 else ~lower
            total = jnp.where(data, turned, acc)
            outs.append(acc / total)
            lse = m_s[h] + jnp.log(total)
            l1 = lse.astype(BF).astype(F32)
            l2 = (lse - l1).astype(BF).astype(F32)
            l3 = lse - l1 - l2
            at = lane if h == 1 else lane - 64
            q = q_ref[s, h, pl.ds(here, T)].astype(F32)
            q = jnp.where(at == 8, -l1, jnp.where(at == 9, -l2, jnp.where(at == 10, -l3, q)))
            q_out[s, h, pl.ds(here, T)] = q.astype(BF)
        o_ref[i, :, pl.ds(pl.multiple_of(s * 128, 128), 128)] = jnp.where(lower, outs[0], outs[1]).astype(BF)

        @pl.when(s == 0)
        def _():
            o_ref[i, :, 256:384] = pltpu.roll(outs[2], 64, 1).astype(BF)

        @pl.when(s == 1)
        def _():
            o_ref[i, :, 256:384] = jnp.where(lower, o_ref[i, :, 256:384].astype(F32), outs[2]).astype(BF)

        return 0

    lax.fori_loop(0, 8, per_tile, 0)


def attn_bwd_kernel(pg, KC, lengths, idx, *refs):
    ins, (w, t0, t1, t2, t3, extra), outs, scratch = refs[:5], refs[5:11], refs[11:-6], refs[-6:]
    gq_s = scratch[-1]
    for s in range(2):
        attn_bwd(pg, KC, s, lengths, idx, *ins, *scratch[:4], outs[0].at[s] if pg > 1 else scratch[4])
        if pg == 1:
            products(s, idx, scratch[4], w, (t0, t1, t2, t3), extra, gq_s, *outs)


def attn_bwd(pg, KC, s, lengths, idx, q_ref, k_ref, v_ref, o_ref, do_ref, dq_s, dk_s, dv_s, do_s, d_ref):
    c, mine = idx[2], idx[5]
    T, L = o_ref.shape[1], k_ref.shape[2]
    bounds = limits(lengths, s, L)
    lane = lax.broadcasted_iota(jnp.int32, (T, 128), 1)
    lower = lane < 64
    zero = jnp.zeros((T, 128), F32)

    dk_s[...] = jnp.zeros_like(dk_s)
    dv_s[...] = jnp.zeros_like(dv_s)
    live = bounds[4]
    cols = slice(s * 128, (s + 1) * 128)

    def per_tile(i, _):
        here = pl.multiple_of(i * T, T)
        first = (mine * 4 + i) * T
        low, high = span(bounds, first, first + T - 1)
        high = jnp.minimum(high, live)
        pair = do_ref[i, :, cols].astype(F32)
        third = do_ref[i, :, 256:384].astype(F32)
        if s == 0:
            third = pltpu.roll(third, 64, 1)
        o_third = o_ref[i, :, 256:384].astype(F32)
        if s == 0:
            o_third = pltpu.roll(o_third, 64, 1)
        prod = pair * o_ref[i, :, cols].astype(F32)
        for h in range(3):
            data = lower if h == 0 else ~lower
            full = prod if h < 2 else third * o_third
            delta = jnp.sum(jnp.where(data, full, zero), axis=1, keepdims=True)
            d1 = delta.astype(BF).astype(F32)
            d2 = (delta - d1).astype(BF).astype(F32)
            d3 = delta - d1 - d2
            at = lane - 64 if h == 0 else lane
            aug = jnp.where(at == 8, -d1, jnp.where(at == 9, -d2, jnp.where(at == 10, -d3, zero)))
            do_s[h] = jnp.where(data, pair if h < 2 else third, aug).astype(BF)
            dq_s[h, pl.ds(here, T)] = zero

        def step(kt, _):
            at = pl.multiple_of(kt * KC, KC)
            for h in range(3):
                q = q_ref[s, h, pl.ds(here, T)]
                k = k_ref[s, h, pl.ds(at, KC)]
                d = do_s[h]
                pt = jnp.exp(mm_nt(k, q))
                ds = (pt * mm_nt(v_ref[s, h, pl.ds(at, KC)], d)).astype(BF)
                dv_s[h, pl.ds(at, KC)] += mm(pt.astype(BF), d)
                dk_s[h, pl.ds(at, KC)] += mm(ds, q)
                dq_s[h, pl.ds(here, T)] += mm_tn(ds, k)
            return 0

        lax.fori_loop(low // KC, (high + KC - 1) // KC, step, 0)
        return 0

    lax.fori_loop(0, 4, per_tile, 0)
    for g in range(pg):
        for n, off in enumerate(OFFS):
            at = pl.multiple_of((g * 4 + (c ^ off)) * T, T)
            own = pl.multiple_of((c ^ off) * T, T)
            keep = 0.125 if pg == 1 else jnp.where(mine == g, 0.125, 0.0)
            dq = [dq_s[h, pl.ds(own, T)] * keep for h in range(3)]
            dk = [dk_s[h, pl.ds(at, T)] for h in range(3)]
            dv = [dv_s[h, pl.ds(at, T)] for h in range(3)]
            d_ref[g, n, :, 0:128] = jnp.where(lower, dq[0], dq[1]).astype(BF)
            d_ref[g, n, :, 128:256] = jnp.where(lower, dk[0], dk[1]).astype(BF)
            d_ref[g, n, :, 256:384] = jnp.where(lower, dv[0], dv[1]).astype(BF)
            d_ref[g, n, :, 384:512] = jnp.where(lower, dq[2], dv[2]).astype(BF)
            d_ref[g, n, :, 512:576] = dk[2][:, 0:64].astype(BF)


def products(s, idx, d, w, toks, extra, acc, gq_own, gq_other, gi):
    zw, h, y = idx[1], idx[2], idx[3]
    D = w.shape[0]
    T = d.shape[2]
    rows = slice(s * T, (s + 1) * T)
    for n, off in enumerate(OFFS):
        gi[h ^ off, rows, :] = mm_nt(d[0, n], w[...]).astype(BF)
    v = sum(mm_tn(t[s], d[0, n]) for n, t in enumerate(toks))
    col = sum(fold8(d[0, n].astype(F32)) for n in range(4))
    if s == 0:
        acc[0:D, :] = v
        acc[D : D + 8, :] = col
        return
    acc[0:D, :] += v
    col = jnp.sum(col + acc[D : D + 8, :], axis=0, keepdims=True)
    top = lax.broadcasted_iota(jnp.int32, (8, 576), 0) == 0
    for k in range(4):
        z = zw ^ k
        tail = jnp.where(top & (h == z), col, extra[z])
        tail = jnp.concatenate([tail, jnp.zeros_like(tail)], axis=0).astype(BF)
        for ref, yy in ((gq_own, y), (gq_other, 1 - y)):
            ref[k, 0:96, :] = acc[pl.ds(pl.multiple_of(z * 192 + yy * 96, 8), 96), :].astype(BF)
            ref[k, 96:GQ, :] = tail


def gelu_parts(u):
    t = 1.0 / (1.0 + (0.3275911 * 0.7071067811865476) * jnp.abs(u))
    e = jnp.exp(-0.5 * u * u)
    poly = t * (
        0.127414796
        + t * (-0.142248368 + t * (0.7107068705 + t * (-0.7265760135 + t * 0.5307027145)))
    )
    tail = poly * e
    cdf = jnp.where(u >= 0, 1.0 - tail, tail)
    return u * cdf, cdf + u * e * 0.3989422804014327


def gather_heads(tiles):
    (pair0, third0), (pair1, third1) = tiles
    lower = lax.broadcasted_iota(jnp.int32, pair0.shape, 1) < 64
    turned = pltpu.roll(pair1, 64, 1)
    return pair0, jnp.where(lower, third0, turned), jnp.where(lower, turned, pltpu.roll(third1, 64, 1))


def ffn_kernel(
    idx, lengths, attn, tok, cot, sm_own, w_in, w_at, w_out,
    s1a, r2a, c1a, c2a, s1b, r2b, c1b, c2b,
    out, dfirst, dattn, sent, kept, extra,
    w1, w2, wa, sm, b1, att, hlow, xhat, rstd, acc, act, gp, dlow, sums, sem, osem,
):
    c, z, h, y, x, mine = (idx[i] for i in range(6))
    R, D = tok.shape
    T = attn.shape[1]
    FB = w_in.shape[1] // 8
    TR, GR = 256, 128
    first_copies = [(w_at, wa.at[z]), (sm_own.at[240:256], sm.at[0])]
    first_copies += [(s1a.at[0, k, 240:256], sm.at[k + 1]) for k in range(3)]
    copies = [(w_in, w1.at[z]), (w_out, w2.at[z])]
    for n, (ra, rb) in enumerate(((s1a, s1b), (r2a, r2b), (c1a, c1b), (c2a, c2b))):
        for k in range(2):
            p = idx[6 + 2 * n + k]
            q, half = p // 2, p % 2
            for kz in range(3):
                zz = z ^ (kz + 1)
                at = pl.ds(pl.multiple_of(half * FB, 128), FB)
                first_copies.append((ra.at[k, kz, 192:240], wa.at[zz, pl.ds(pl.multiple_of(q * 48, 16), 48), at]))
                copies.append((ra.at[k, kz, 0:192], w1.at[zz, :, pl.ds(pl.multiple_of(p * FB, 128), FB)]))
                copies.append((rb.at[k, kz], w2.at[zz, pl.ds(pl.multiple_of(half * FB + q * 96, 16), 96)]))
    many = len(first_copies)
    first_copies = [pltpu.make_async_copy(a, b, sem.at[i]) for i, (a, b) in enumerate(first_copies)]
    copies = [pltpu.make_async_copy(a, b, sem.at[many + i]) for i, (a, b) in enumerate(copies)]
    for cp in first_copies + copies:
        cp.start()

    sums[...] = jnp.zeros_like(sums)
    extra[...] = jnp.zeros_like(extra)

    lower = lax.broadcasted_iota(jnp.int32, (T, 128), 1) < 64
    for s in range(2):
        for g in range(0, 4, 2):
            tiles = []
            for n in (g, g + 1):
                third = attn[n, :, 256:384].astype(F32)
                tiles.append((
                    attn[n, :, s * 128 : (s + 1) * 128].astype(F32),
                    third if s == 0 else pltpu.roll(third, 64, 1),
                ))
            for j, tile in enumerate(gather_heads(tiles)):
                at = g * 192 + j * 128
                att[s * T : (s + 1) * T, at : at + 128] = tile.astype(BF)

    for cp in first_copies:
        cp.wait()

    small = [sm[k ^ z].astype(F32) for k in range(4)]

    def whole(i):
        return jnp.concatenate([v[i : i + 1, 0:192] for v in small], axis=1)

    b_attn, g1v, s1v, b_out, g2v, s2v = (whole(i) for i in range(2, 8))
    for k in range(4):
        row = jnp.concatenate([small[k][i : i + 1, 0:192] for i in range(8, 12)], axis=1)
        for half in range(2):
            b1[2 * k + half, 0:1, :] = row[:, half * FB : (half + 1) * FB]

    acc[...] = mm(att[...], wa[...].reshape(D, D))

    def first(r, _):
        rows = pl.ds(pl.multiple_of(r * TR, TR), TR)
        v = acc[rows, :] + tok[rows, :].astype(F32) + b_attn
        mean = jnp.mean(v, axis=-1, keepdims=True)
        v = v - mean
        rs = lax.rsqrt(jnp.mean(v * v, axis=-1, keepdims=True) + EPS)
        xh = v * rs
        xhat[rows, :] = xh
        rstd[rows, :] = jnp.broadcast_to(rs, (TR, 128))
        hid = xh * g1v + s1v
        hlow[rows, :] = hid.astype(BF)
        acc[rows, :] = hid + b_out
        return 0

    lax.fori_loop(0, R // TR, first, 0)
    for cp in copies:
        cp.wait()

    def keep(src, i, cc, at):
        to = pl.ds(pl.multiple_of(i * FB, 128), FB)

        @pl.when(c == cc)
        def _():
            pltpu.make_async_copy(src, kept.at[:, to], osem.at[at]).start()

        @pl.when(c != cc)
        def _():
            pltpu.make_async_copy(src, sent.at[:, to], osem.at[at]).start()

    def kept_all(first, count):
        for i in range(first, first + count):
            pltpu.make_async_copy(act.at[:, 0:FB], kept.at[:, 0:FB], osem.at[i]).wait()

    def forward(zz, _):
        cols = pl.ds(pl.multiple_of(zz * D, 128), D)
        u = mm(hlow[...], w1[:, :, cols].reshape(D, D)) + jnp.concatenate([b1[2 * zz, 0:1, :], b1[2 * zz + 1, 0:1, :]], axis=1)
        for r in range(R // GR):
            rows = slice(r * GR, (r + 1) * GR)
            a, d = gelu_parts(u[rows])
            act[rows, cols] = a.astype(BF)
            gp[rows, cols] = d.astype(BF)
        acc[...] += mm(act[:, cols], w2[zz])
        for half in range(2):
            src = act.at[:, pl.ds(pl.multiple_of(zz * D + half * FB, 128), FB)]
            keep(src, zz, half, 2 * zz + half)
        return 0

    lax.fori_loop(0, 4, forward, 0)

    def second(r, _):
        rows = pl.ds(pl.multiple_of(r * TR, TR), TR)
        s = r // (T // TR)
        v = acc[rows, :]
        mean = jnp.mean(v, axis=-1, keepdims=True)
        v = v - mean
        rs = lax.rsqrt(jnp.mean(v * v, axis=-1, keepdims=True) + EPS)
        xh = v * rs
        out[rows, :] = (xh * g2v + s2v).astype(BF)
        place = (mine * 4 + h) * T + r * TR - s * T
        pos = lax.broadcasted_iota(jnp.int32, (TR, D), 0) + place
        dy = jnp.where(pos < limits(lengths, s, 0)[4], cot[rows, :].astype(F32), 0.0)
        sums[4] += fold8(dy * xh)
        sums[5] += fold8(dy)
        dx = dy * g2v
        m1 = jnp.mean(dx, axis=-1, keepdims=True)
        m2 = jnp.mean(dx * xh, axis=-1, keepdims=True)
        ds = rs * (dx - m1 - xh * m2)
        low = ds.astype(BF)
        dlow[rows, :] = low
        sums[3] += fold8(low.astype(F32))
        acc[rows, :] = ds
        return 0

    lax.fori_loop(0, R // TR, second, 0)

    kept_all(0, 8)
    shared = [(att, 9), (hlow, 11), (dlow, 13)]
    shared = [pltpu.make_async_copy(v, sent.at[:, i * FB : (i + 2) * FB], osem.at[n + 16]) for n, (v, i) in enumerate(shared)]
    for cp in shared:
        cp.start()

    def backward(zz, _):
        cols = pl.ds(pl.multiple_of(zz * D, 128), D)
        da = mm_nt(dlow[...], w2[zz])
        gsum = jnp.zeros((8, D), F32)
        for r in range(R // GR):
            rows = slice(r * GR, (r + 1) * GR)
            di = (da[rows] * gp[rows, cols].astype(F32)).astype(BF)
            act[rows, cols] = di
            gsum = gsum + fold8(di.astype(F32))
        acc[...] += mm_nt(act[:, cols], w1[:, :, cols].reshape(D, D))
        for half in range(2):
            src = act.at[:, pl.ds(pl.multiple_of(zz * D + half * FB, 128), FB)]
            keep(src, 4 + zz, half, 8 + 2 * zz + half)
        gsum = jnp.sum(gsum, axis=0, keepdims=True)
        extra[zz, 3:4, :] = gsum[:, 0:576]
        extra[zz, 4:5, 0:192] = gsum[:, 576:768]
        return 0

    lax.fori_loop(0, 4, backward, 0)
    for cp in shared:
        cp.wait()

    def last(r, _):
        rows = pl.ds(pl.multiple_of(r * TR, TR), TR)
        dy = acc[rows, :]
        xh = xhat[rows, :]
        sums[1] += fold8(dy * xh)
        sums[2] += fold8(dy)
        dx = dy * g1v
        m1 = jnp.mean(dx, axis=-1, keepdims=True)
        m2 = jnp.mean(dx * xh, axis=-1, keepdims=True)
        df = rstd[rows, :1] * (dx - m1 - xh * m2)
        dfirst[rows, :] = df
        low = df.astype(BF)
        dlow[rows, :] = low
        sums[0] += fold8(low.astype(F32))
        return 0

    lax.fori_loop(0, R // TR, last, 0)
    acc[...] = mm_nt(dlow[...], wa[...].reshape(D, D))
    for g in range(0, 4, 2):
        thirds = []
        for s in range(2):
            t0, t1, t2 = (acc[s * T : (s + 1) * T, g * 192 + j * 128 : g * 192 + (j + 1) * 128] for j in range(3))
            t1r, t2r = pltpu.roll(t1, 64, 1), pltpu.roll(t2, 64, 1)
            dattn[g, :, s * 128 : (s + 1) * 128] = t0.astype(BF)
            dattn[g + 1, :, s * 128 : (s + 1) * 128] = jnp.where(lower, t1r, t2r).astype(BF)
            thirds.append((t1, t1r, t2, t2r))
        (a1, _, _, a2r), (_, b1r, b2, _) = thirds
        dattn[g, :, 256:384] = jnp.where(lower, a1, b1r).astype(BF)
        dattn[g + 1, :, 256:384] = jnp.where(lower, a2r, b2).astype(BF)
    for half in range(2):
        keep(dlow.at[:, half * FB : (half + 1) * FB], 8, half, 19 + half)
    for i in range(6):
        row = jnp.sum(sums[i], axis=0, keepdims=True)
        for k in range(4):
            at = (i % 3) * 192
            extra[k, 1 + i // 3 : 2 + i // 3, at : at + 192] = row[:, k * 192 : (k + 1) * 192]
    kept_all(8, 8)
    kept_all(19, 2)


def weight_kernel(idx, kept, mate, sent, plane, mine, s1, s2, s3, units, shared, units2, shared2, plane_s, mine_s, sent_s, sem, osem):
    z = idx[1]
    D = shared.shape[1] // 3
    FB = D // 2
    wide = 4 * FB
    copies = []
    for refs, us, sh in (((kept, sent), units, shared), ((mate, mate), units2, shared2)):
        for at, size in ((wide, wide), (0, wide), (2 * wide, FB)):
            copies.append((refs[0].at[:, at : at + size], us.at[:, at : at + size]))
        for at in (D, 2 * D, 0):
            copies.append((refs[1].at[:, 9 * FB + at : 9 * FB + at + D], sh.at[:, at : at + D]))
    order = (1, 4, 7, 10, 0, 3, 6, 9, 2, 5, 8, 11)
    copies = [pltpu.make_async_copy(*copies[n], sem.at[n]) for n in order]
    for cp in copies:
        cp.start()
    for cp in copies[:4]:
        cp.wait()
    outs = []

    def emit(src, to):
        cp = pltpu.make_async_copy(src, to, osem.at[len(outs)])
        cp.start()
        outs.append(cp)

    for k in (1, 2, 3, 0):
        cols = pl.ds(pl.multiple_of((z ^ k) * FB, 128), FB)
        v = mm_tn(units[:, cols], shared[:, 2 * D : 3 * D]) + mm_tn(units2[:, cols], shared2[:, 2 * D : 3 * D])
        for q in range(4):
            if k == 0:
                mine_s[q] = v[q * 96 : (q + 1) * 96]
            else:
                sent_s[k - 1, q] = v[q * 96 : (q + 1) * 96].astype(BF)
        if k == 0:
            emit(mine_s, mine)
        else:
            emit(sent_s.at[k - 1], (s1, s2, s3)[k - 1])
    for cp in copies[4:]:
        cp.wait()
    v = mm_tn(shared[:, 0:D], units[:, 2 * wide : 2 * wide + FB]) + mm_tn(shared2[:, 0:D], units2[:, 2 * wide : 2 * wide + FB])
    v = v.astype(BF)
    for zz in range(4):
        for q in range(4):
            plane_s[q, zz, 192:240, :] = v[zz * 192 + q * 48 : zz * 192 + (q + 1) * 48]
    for n in range(2):
        cols = slice(wide + n * D, wide + (n + 1) * D)
        v = mm_tn(shared[:, D : 2 * D], units[:, cols]) + mm_tn(shared2[:, D : 2 * D], units2[:, cols])
        v = v.astype(BF)
        for i in range(2):
            for zz in range(4):
                plane_s[2 * n + i, zz, 0:192, :] = v[zz * 192 : (zz + 1) * 192, i * FB : (i + 1) * FB]
        emit(plane_s.at[2 * n : 2 * n + 2], plane.at[2 * n : 2 * n + 2])
    for cp in outs:
        cp.wait()


def products_kernel(idx, d, w, t0, t1, t2, t3, extra, *outs):
    for s in range(2):
        products(s, idx, d.at[s], w, (t0, t1, t2, t3), extra, outs[-1], *outs[:-1])


def chunkq_kernel(own, got, *outs):
    for k, ref in enumerate(outs):
        ref[...] = (own[k].astype(F32) + got[k].astype(F32)).astype(ref.dtype)


def chunk_kernel(idx, terms, *outs):
    z = idx[1]
    for k, ref in enumerate(outs):
        ref[...] = sum(terms[q, z ^ k].astype(F32) for q in range(4)).astype(ref.dtype)


def sum2_kernel(idx, a0, a1, a2, a3, *outs):
    here = idx[3] * 2 + idx[4]
    for k, ref in enumerate(outs):
        q = here ^ k
        ref[...] = (a0[q] + sum(a[q].astype(F32) for a in (a1, a2, a3))).astype(ref.dtype)


def sum_kernel(a0, a1, a2, a3, b0, b1, b2, b3, out):
    A, B = a0.shape
    C = b0.shape[0]
    out[0:A, :] = (a0[...] + sum(a[...].astype(F32) for a in (a1, a2, a3))).astype(BF)
    v = (b0[...] + sum(b[...].astype(F32) for b in (b1, b2, b3))).astype(BF)
    out[A : A + C, :] = v[:, :B]
    out[A + C : A + 2 * C, :] = v[:, B:]


def sumq_kernel(q0, q1, q2, q3, out):
    E, W = q0.shape
    B = out.shape[1]
    v = (q0[...] + sum(q[...].astype(F32) for q in (q1, q2, q3))).astype(BF)
    out[0:E, :] = v[:, :B]
    out[E : 2 * E, :] = jnp.zeros((E, B), BF)
    out[E : 2 * E, 0 : W - B] = v[:, B:]


def out_ffn_kernel(idx, s1, r2, c1, c2, g_wi, g_wa, g_wo):
    FB = s1.shape[2]
    refs = (s1, r2, c1, c2)
    for n, ref in enumerate(refs):
        for k in range(2):
            p = idx[6 + 2 * n + k]
            g_wi[:, pl.ds(pl.multiple_of(p * FB, 128), FB)] = ref[k, 0:192, :].astype(F32)
            rows = pl.ds(pl.multiple_of((p // 2) * 48, 16), 48)
            g_wa[rows, pl.ds(pl.multiple_of((p % 2) * FB, 128), FB)] = ref[k, 192:240, :].astype(F32)
            rows = pl.ds(pl.multiple_of((p % 2) * FB + (p // 2) * 96, 16), 96)
            g_wo[rows, 0:FB] = ref[k, 240:336, :].astype(F32)
            g_wo[rows, FB : 2 * FB] = ref[k, 336:432, :].astype(F32)


def out_qkv_kernel(idx, s1, r2, c1, c2, g_wq, g_wk, g_wv, g_bq, g_bv, g_bi, *six):
    FB = s1.shape[2]
    c, z = idx[0], idx[1]
    refs = (s1, r2, c1, c2)
    lower = lax.broadcasted_iota(jnp.int32, (96, 128), 1) < 64
    left, right = jnp.zeros((16, FB), F32), jnp.zeros((16, FB), F32)
    top = lax.broadcasted_iota(jnp.int32, (16, FB), 0) == 0
    for (n, k), (m, j) in (((0, 0), (2, 0)), ((0, 1), (3, 0)), ((1, 0), (2, 1)), ((1, 1), (3, 1))):
        p = idx[6 + 2 * n + k]
        yy, xx = p // 4, (p // 2) % 2
        own, other = refs[n].at[k], refs[m].at[j]

        def tile(i, swap):
            at = slice(0, 96) if i < 3 else slice(GQ, GQ + 96)
            cols = slice((i % 3) * 128, (i % 3 + 1) * 128)
            u, v = own[at, cols].astype(F32), other[at, cols].astype(F32)
            return jnp.where((c == 0) != swap, u, v)

        rows = pl.ds(pl.multiple_of(yy * 96, 8), 96)
        for ref, i, third, low in ((g_wq, 0, 3, True), (g_wk, 1, 4, True), (g_wv, 2, 3, False)):
            ta, tb = tile(third, False), tile(third, True)
            turned = pltpu.roll(tile(i, True), 64, 1)
            if not low:
                ta = pltpu.roll(ta, 64, 1)
            else:
                tb = pltpu.roll(tb, 64, 1)
            base = xx * 384
            ref[rows, pl.ds(pl.multiple_of(base, 128), 128)] = tile(i, False)
            ref[rows, pl.ds(pl.multiple_of(base + 128, 128), 128)] = jnp.where(lower, ta, turned)
            ref[rows, pl.ds(pl.multiple_of(base + 256, 128), 128)] = jnp.where(lower, turned, tb)
        for ref, cc in ((own, c), (other, 1 - c)):
            here = (yy == 0) & (~top | (xx * 2 + cc == z))
            left = left + jnp.where(here, ref[96:GQ, :].astype(F32), 0.0)
            right = right + jnp.where(here, ref[GQ + 96 : 2 * GQ, :].astype(F32), 0.0)
    g_bq[...] = jnp.concatenate([left[0:1, 0:128], right[0:1, 0:64]], axis=1).reshape(192)
    g_bv[...] = jnp.concatenate([left[0:1, 256:384], right[0:1, 64:128]], axis=1).reshape(192)
    for i, ref in enumerate(six):
        row = 1 + i // 3
        ref[...] = (left[row : row + 1, 0:192], left[row : row + 1, 192:384], right[row : row + 1, 0:192])[i % 3].reshape(192)
    g_bi[...] = jnp.concatenate([left[3:4, :], right[3:4, 0:192], left[4:5, 0:192]], axis=1).reshape(768)


def tie(*values):
    return lax.optimization_barrier(values)


def block(shape, *at):
    return pl.BlockSpec(shape, lambda i: at)


def call(kernel, outs, in_specs, out_specs, scratch=(), name=None, grid=()):
    return pl.pallas_call(
        kernel,
        out_shape=outs,
        grid=grid,
        in_specs=in_specs,
        out_specs=out_specs,
        scratch_shapes=list(scratch),
        compiler_params=pltpu.CompilerParams(vmem_limit_bytes=VMEM_LIMIT),
        cost_estimate=pl.CostEstimate(flops=1, bytes_accessed=1, transcendentals=0),
        name=name,
    )


def make_body(sizes):
    pg = sizes["pg"]
    order = [sizes[a] for a in AX]

    def send(fn, a):
        pairs = []
        for flat in range(math.prod(order)):
            at, rest = [], flat
            for n in reversed(order):
                at.append(rest % n)
                rest //= n
            dest = 0
            for n, v in zip(order, fn(*reversed(at))):
                dest = dest * n + v
            pairs.append((flat, dest))
        return lax.ppermute(a, AX, pairs)

    to_x = functools.partial(send, lambda s, g, x, c, z: (s, g, 1 - x, c, z))
    to_y = functools.partial(send, lambda s, g, x, c, z: (1 - s, g, x, c, z))
    to_core = functools.partial(send, lambda s, g, x, c, z: (s, g, x, 1 - c, z))
    to_z = [functools.partial(send, lambda s, g, x, c, z, k=k: (s, g, x, c, z ^ k)) for k in (1, 2, 3)]
    mix_a = functools.partial(send, lambda s, g, x, c, z: (s, g, 1 - x, c, z) if c == 0 else (1 - s, g, x, c, z))
    mix_b = functools.partial(send, lambda s, g, x, c, z: (1 - s, g, x, c, z) if c == 0 else (s, g, 1 - x, c, z))

    to_d = functools.partial(send, lambda s, g, x, c, z: (1 - s, g, 1 - x, c, z))

    def over_z(sent):
        return [f(v) for f, v in zip(to_z, sent if isinstance(sent, list) else [sent] * 3)]

    def body(
        tokens, cotangent, segment_ids, lengths, w_query, b_query, w_key, w_value, b_value, w_attn, b_attn,
        ln1_gain, ln1_shift, w_inner, b_inner, w_outer, b_outer, ln2_gain, ln2_shift,
    ):
        S, T, D = tokens.shape
        R = S * T
        y, x, c = (lax.axis_index(a) for a in ("seq", "x", "core"))
        mine, z = lax.axis_index("pg"), lax.axis_index("wt")
        h = x * 2 + c
        p = y * 4 + h
        L = 4 * pg * T
        FB = w_inner.shape[1] // 8

        a_of = jnp.where(c == 0, 2, 4)
        other = p ^ 1
        mates = [p, p ^ a_of, p ^ (6 - a_of), p ^ 6, other, other ^ (6 - a_of), other ^ a_of, other ^ 6]
        idx = jnp.stack([c, z, h, y, x, mine] + mates).astype(jnp.int32)

        vecs = (b_query, b_value, b_attn, ln1_gain, ln1_shift, b_outer, ln2_gain, ln2_shift, b_inner)
        w_own, pack, piece1, piece2 = call(
            prep_kernel,
            (
                jax.ShapeDtypeStruct((208, 576), BF), jax.ShapeDtypeStruct((GQ, 576), BF),
                jax.ShapeDtypeStruct((256, FB), BF), jax.ShapeDtypeStruct((96, D), BF),
            ),
            [SM] + [VM] * 15, (VM,) * 4, name="prep",
        )(idx, w_query, w_key, w_value, w_attn, w_inner, w_outer, *vecs)
        w_z = over_z(pack)
        tok_x, tok_c = to_x(tokens), to_core(tokens)
        w_z, tok_x, tok_c, piece1 = tie(w_z, tok_x, tok_c, piece1)
        w_y, tok_xc = to_y(jnp.stack(w_z)), to_core(tok_x)
        z1 = over_z(piece1)
        w_y, tok_xc, z1, piece2 = tie(w_y, tok_xc, z1, piece2)
        z2 = over_z(piece2)
        one = jnp.stack(z1)
        tok_xc, one = tie(tok_xc, one)
        one_a = mix_a(one)

        toks = [t[None] for t in (tokens, tok_x, tok_c, tok_xc)]
        if pg > 1:
            toks = [lax.all_gather(t, "pg", axis=0, tiled=True) for t in toks]
        head = jax.ShapeDtypeStruct((S, 3, L, 128), BF)
        own_head = jax.ShapeDtypeStruct((S, 3, 4 * T, 128), BF)
        q_aug, k_aug, v_aug, w_qkv = call(
            functools.partial(qkv_kernel, pg),
            (own_head, head, head, jax.ShapeDtypeStruct((4, 192, 576), BF)),
            [SM, SM] + [VM] * 4 + [ANY] * 5,
            (VM,) * 4,
            [pltpu.VMEM((4, 16, 576), BF), pltpu.SemaphoreType.DMA((11,))],
            name="qkv",
        )(lengths, idx, *toks, w_own, *w_z, w_y)
        w_qkv = w_qkv.reshape(D, 576)
        q_aug, one_a, z2 = tie(q_aug, one_a, z2)
        one, two = jnp.stack([one, one_a]), jnp.stack(z2)
        q_aug, one, two = tie(q_aug, one, two)
        one_b, two_a = mix_b(one), mix_a(two)
        o, q_aug = call(
            functools.partial(attn_fwd_kernel, 1024),
            (jax.ShapeDtypeStruct((4, T, 384), BF), own_head),
            [SM, SM] + [VM] * 3,
            (VM,) * 2,
            [pltpu.VMEM((3, T, 128), F32), pltpu.VMEM((3, T, 128), F32)],
            name="attn_fwd",
        )(lengths, idx, q_aug, k_aug, v_aug)
        o, one_b, two_a = tie(o, one_b, two_a)
        attn = lax.all_to_all(o, ("x", "core"), 0, 0, tiled=True)
        two = jnp.stack([two, two_a])
        two_b = mix_b(two)
        one = (one, one_b, to_core(one), to_core(one_b))
        attn, two_b = tie(attn, two_b)
        two = (two, two_b, to_core(two), to_core(two_b))

        layer_out, d_first, d_attn, sent, kept, extra = call(
            ffn_kernel,
            (
                jax.ShapeDtypeStruct((R, D), BF), jax.ShapeDtypeStruct((R, D), F32), jax.ShapeDtypeStruct((4, T, 384), BF),
                jax.ShapeDtypeStruct((R, 15 * FB), BF), jax.ShapeDtypeStruct((R, 9 * FB), BF), jax.ShapeDtypeStruct((4, 8, 576), F32),
            ),
            [SM, SM] + [VM] * 3 + [ANY] * 12,
            (VM, VM, VM, ANY, ANY, VM),
            [
                pltpu.VMEM((4, 192, 8 * FB), BF),
                pltpu.VMEM((4, 2 * FB, D), BF),
                pltpu.VMEM((4, 192, D), BF),
                pltpu.VMEM((4, 16, FB), BF),
                pltpu.VMEM((8, 8, FB), F32),
                pltpu.VMEM((R, D), BF),
                pltpu.VMEM((R, D), BF),
                pltpu.VMEM((R, D), F32),
                pltpu.VMEM((R, 128), F32),
                pltpu.VMEM((R, D), F32),
                pltpu.VMEM((R, 8 * FB), BF),
                pltpu.VMEM((R, 8 * FB), BF),
                pltpu.VMEM((R, D), BF),
                pltpu.VMEM((8, 8, D), F32),
                pltpu.SemaphoreType.DMA((79,)),
                pltpu.SemaphoreType.DMA((21,)),
            ],
            name="ffn",
        )(
            idx, lengths, attn, tokens.reshape(R, D), cotangent.reshape(R, D), piece1, w_inner, w_attn, w_outer, *one, *two
        )

        d_o = lax.all_to_all(d_attn, ("x", "core"), 0, 0, tiled=True)

        def add(*parts):
            return sum(v.astype(F32) for v in parts)

        def shares(n, m):
            return jax.ShapeDtypeStruct((*n, m), F32), *(jax.ShapeDtypeStruct((*n, m), BF),) * 3

        def attn_back(d_o):
            part = jax.ShapeDtypeStruct((4, GQ, 576), BF)
            outs = (part, part, jax.ShapeDtypeStruct((4, R, D), BF))
            more = (w_qkv, tokens, tok_x, tok_c, tok_xc, extra)
            total = pltpu.VMEM((D + 8, 576), F32)
            res = call(
                functools.partial(attn_bwd_kernel, pg, 512),
                outs if pg == 1 else (jax.ShapeDtypeStruct((S, pg, 4, T, 576), BF),),
                [SM, SM] + [VM] * 5 + [VM if pg == 1 else ANY] * 6,
                (VM,) * (3 if pg == 1 else 1),
                [
                    pltpu.VMEM((3, 4 * T, 128), F32), pltpu.VMEM((3, L, 128), F32), pltpu.VMEM((3, L, 128), F32),
                    pltpu.VMEM((3, T, 128), BF), pltpu.VMEM((1, 4, T, 576), BF), total,
                ],
                name="attn_bwd",
            )(lengths, idx, q_aug, k_aug, v_aug, o, d_o, *more)
            if pg > 1:
                d = lax.psum_scatter(res[0], "pg", scatter_dimension=1, tiled=True)
                res = call(products_kernel, outs, [SM] + [VM] * 7, (VM,) * 3, [total], name="products")(idx, d, *more)
            return res

        part = jax.ShapeDtypeStruct((4, 96, D), BF)
        q1, c2, *sent2 = call(
            weight_kernel,
            (jax.ShapeDtypeStruct((4, 4, 240, FB), BF), jax.ShapeDtypeStruct((4, 96, D), F32)) + (part,) * 3,
            [SM] + [ANY] * 3, (ANY,) * 5,
            [
                pltpu.VMEM((R, 9 * FB), BF), pltpu.VMEM((R, 3 * D), BF), pltpu.VMEM((R, 9 * FB), BF), pltpu.VMEM((R, 3 * D), BF),
                pltpu.VMEM((4, 4, 240, FB), BF), pltpu.VMEM((4, 96, D), F32),
                pltpu.VMEM((3, 4, 96, D), BF), pltpu.SemaphoreType.DMA((12,)), pltpu.SemaphoreType.DMA((6,)),
            ],
            name="weights",
        )(idx, kept, to_core(sent), sent)
        n, m = q1.shape[2:]
        d_o, sent2, q1 = tie(d_o, sent2, q1)
        got_z2, q1 = over_z(sent2), lax.all_to_all(q1, ("seq", "x"), 0, 0, tiled=True)
        gq_own, gq_other, gi = attn_back(d_o)
        gq_y = to_y(gq_other)
        c1, *sent1 = call(chunk_kernel, shares((n,), m), [SM, VM], (VM,) * 4, name="chunks1")(idx, q1)
        sent1, got_z2 = tie(sent1, got_z2)
        got_z1 = over_z(sent1)
        gi = lax.all_to_all(gi, ("x", "core"), 0, 0, tiled=True)
        cq, *sentq = call(chunkq_kernel, shares((GQ,), 576), [VM] * 2, (VM,) * 4, name="chunksq")(gq_own, gq_y)
        p2, *sent2 = call(sum2_kernel, shares((96,), D), [SM] + [VM] * 4, (VM,) * 4, name="sums2")(idx, c2, *got_z2)
        sent2, got_z1, sentq = tie(sent2, got_z1, sentq)
        got_zq = over_z(sentq)
        got_p2 = [f(v) for f, v in zip((to_x, to_y, to_d), sent2)]

        total = call(sum_kernel, jax.ShapeDtypeStruct((432, FB), BF), [VM] * 8, VM, name="sums")(c1, *got_z1, p2, *got_p2)
        total, got_zq = tie(total, got_zq)
        total_q = call(sumq_kernel, jax.ShapeDtypeStruct((2 * GQ, FB), BF), [VM] * 4, VM, name="sumsq")(cq, *got_zq)
        if pg > 1:
            total, total_q = (lax.psum(v.astype(F32), "pg").astype(BF) for v in (total, total_q))

        mate, mate_q = mix_a(total), mix_a(total_q)
        s1 = jnp.stack([total, mate])
        r2, s1_core = mix_b(s1), to_core(s1)
        r2, s1_core, mate_q = tie(r2, s1_core, mate_q)
        s1_q = jnp.stack([total_q, mate_q])
        r2_q = mix_b(s1_q)
        grad_input = add(d_first, *(gi[k] for k in range(4))).astype(BF).reshape(tokens.shape)
        mat, wide = jax.ShapeDtypeStruct((192, D), F32), jax.ShapeDtypeStruct((192, 8 * FB), F32)
        vec, long_vec = jax.ShapeDtypeStruct((192,), F32), jax.ShapeDtypeStruct((2 * FB,), F32)
        g_wi, g_wa, g_wo = call(
            out_ffn_kernel, (wide, mat, jax.ShapeDtypeStruct((D, D), F32)), [SM] + [VM] * 4, (VM,) * 3, name="out_ffn"
        )(idx, s1, r2, s1_core, to_core(r2))
        g_wi, g_wa, g_wo, r2_q, grad_input = tie(g_wi, g_wa, g_wo, r2_q, grad_input)
        g_wq, g_wk, g_wv, g_bq, g_bv, g_bi, *six = call(
            out_qkv_kernel, (mat, mat, mat, vec, vec, long_vec) + (vec,) * 6, [SM] + [VM] * 4, (VM,) * 12, name="out_qkv"
        )(idx, s1_q, r2_q, to_core(s1_q), to_core(r2_q))
        return (
            layer_out.reshape(tokens.shape), grad_input,
            g_wq, g_bq, g_wk, g_wv, g_bv, g_wa, six[0], six[1], six[2], g_wi, g_bi, g_wo, six[3], six[4], six[5],
        )

    return body


def solution(mesh):
    sizes = dict(mesh.shape)
    pg = sizes["ctx"] // 4
    fine = dict(zip(AX, (sizes["seq"], pg, 2, 2, sizes["wt"])))
    split = Mesh(mesh.devices.reshape(tuple(fine.values())), AX)
    rows = P(("seq", "wt"), ("pg", "x", "core"), None)
    mat, vec = P("wt", None), P("wt")
    in_specs = (
        rows, rows, P(("seq", "wt"), ("pg", "x", "core")), P(("seq", "wt"), None),
        mat, vec, mat, mat, vec, mat, vec, vec, vec, mat, vec, mat, vec, vec, vec,
    )
    out_specs = (rows, rows, mat, vec, mat, mat, vec, mat, vec, vec, vec, mat, vec, mat, vec, vec, vec)
    return jax.shard_map(make_body(fine), mesh=split, in_specs=in_specs, out_specs=out_specs, check_vma=False)
```

```python
import functools
import math

import jax
import jax.numpy as jnp
from jax import lax
from jax.experimental import pallas as pl
from jax.experimental.pallas import tpu as pltpu
from jax.sharding import Mesh
from jax.sharding import PartitionSpec as P

NEG = -1000000000.0
EPS = 1e-05
BF = jnp.bfloat16
F32 = jnp.float32
AX = ("seq", "pg", "x", "core", "wt")
VM = pl.BlockSpec(memory_space=pltpu.VMEM)
SM = pl.BlockSpec(memory_space=pltpu.SMEM)
ANY = pl.BlockSpec(memory_space=pl.ANY)
OFFS = (0, 2, 1, 3)
VMEM_LIMIT = 60 * 2**20
GQ = 112


def mm(a, b):
    return jnp.dot(a, b, preferred_element_type=F32)


def mm_nt(a, b):
    return lax.dot_general(a, b, (((1,), (1,)), ((), ())), preferred_element_type=F32)


def mm_tn(a, b):
    return lax.dot_general(a, b, (((0,), (0,)), ((), ())), preferred_element_type=F32)


def fold8(v):
    return jnp.sum(v.reshape(v.shape[0] // 8, 8, v.shape[1]), axis=0)


def limits(lengths, s, length):
    out = [jnp.int32(0)]
    for d in range(4):
        out.append(out[-1] + lengths[s, d])
    return out + [jnp.int32(length)]


def span(bounds, first, last):
    low, high = bounds[0], bounds[5]
    for d in range(1, 5):
        low = jnp.where(bounds[d] <= first, bounds[d], low)
        high = jnp.where(bounds[5 - d] > last, bounds[5 - d], high)
    return low, high


def prep_kernel(idx, wq, wk, wv, w_at, w_in, w_out, *rest):
    vecs, (w_own, pack, piece1, piece2) = rest[:9], rest[9:]
    c, h, y = idx[0], idx[2], idx[3]
    p = y * 4 + h
    FB = piece1.shape[1]
    for head in range(4):

        @pl.when(h == head)
        def _():
            a = head * 192
            for i, w in enumerate((wq, wk, wv)):
                w_own[0:192, i * 128 : (i + 1) * 128] = w[:, a : a + 128]
            w_own[0:192, 384:448] = wq[:, a + 128 : a + 192]
            w_own[0:192, 448:512] = wv[:, a + 128 : a + 192]
            w_own[0:192, 512:576] = wk[:, a + 128 : a + 192]

    row = lax.broadcasted_iota(jnp.int32, (16, 576), 0)
    bq, bv = (v[...].astype(F32).reshape(1, 192) for v in vecs[:2])
    none = jnp.zeros((1, 128), F32)
    bias = jnp.concatenate([bq[:, :128], none, bv[:, :128], bq[:, 128:], bv[:, 128:], none[:, :64]], axis=1)
    w_own[192:208, :] = jnp.where(row == 0, jnp.broadcast_to(bias, (16, 576)), 0.0).astype(BF)
    pack[0:96, :] = w_own[pl.ds(pl.multiple_of(y * 96, 16), 96), :]
    pack[96:112, :] = w_own[192:208, :]
    piece1[0:192, :] = w_in[:, pl.ds(pl.multiple_of(p * FB, 128), FB)]
    piece1[192:240, :] = w_at[pl.ds(pl.multiple_of((p // 2) * 48, 16), 48), pl.ds(pl.multiple_of(c * FB, 128), FB)]
    row = lax.broadcasted_iota(jnp.int32, (16, FB), 0)
    long = vecs[8][...].astype(F32).reshape(1, 768)
    small = [v[...].astype(F32).reshape(1, 192) for v in vecs[:8]] + [long[:, i * 192 : (i + 1) * 192] for i in range(4)]
    tall = jnp.zeros((16, FB), F32)
    for i, v in enumerate(small):
        v = jnp.concatenate([v, jnp.zeros((1, FB - 192), F32)], axis=1)
        tall = jnp.where(row == i, jnp.broadcast_to(v, (16, FB)), tall)
    piece1[240:256, :] = tall.astype(BF)
    piece2[...] = w_out[pl.ds(pl.multiple_of(c * FB + (p // 2) * 96, 16), 96), :]


def qkv_kernel(pg, lengths, idx, *refs):
    toks, (w_own, w_z1, w_z2, w_z3, w_y, q_out, k_out, v_out, w, bs, sem) = refs[:4], refs[4:]
    z, c, y, mine = idx[1], idx[2], idx[3], idx[5]
    T, D = toks[0].shape[2:]
    copies = [(w_own.at[0:192], w.at[z]), (w_own.at[192:208], bs.at[0])]
    for k, ref in enumerate((w_z1, w_z2, w_z3)):
        copies.append((ref.at[0:96], w.at[z ^ (k + 1), pl.ds(pl.multiple_of(y * 96, 16), 96)]))
        copies.append((ref.at[96:112], bs.at[k + 1]))
        copies.append((w_y.at[k, 0:96], w.at[z ^ (k + 1), pl.ds(pl.multiple_of((1 - y) * 96, 16), 96)]))
    copies = [pltpu.make_async_copy(a, b, sem.at[i]) for i, (a, b) in enumerate(copies)]
    for cp in copies:
        cp.start()
    for cp in copies:
        cp.wait()
    lane = lax.broadcasted_iota(jnp.int32, (T, 128), 1)
    row = lax.broadcasted_iota(jnp.int32, (T, 128), 0)
    lower = lane < 64
    rel = lane & 63
    zero64 = jnp.zeros((T, 64), F32)

    bias = bs[c ^ z].astype(F32)[0:1]
    for g in range(pg):
        for n, off in enumerate(OFFS):
            place = pl.multiple_of((g * 4 + (c ^ off)) * T, T)
            own = pl.multiple_of((c ^ off) * T, T)
            pos = row + place
            for s in range(2):
                qkv = mm(toks[n][g, s], w[...].reshape(D, 576)) + bias
                qkv = qkv.astype(BF).astype(F32)
                seg = jnp.zeros((T, 128), jnp.int32)
                for start in limits(lengths, s, 0)[1:5]:
                    seg = seg + (pos >= start).astype(jnp.int32)
                hot = rel == seg
                q_aug = jnp.where(hot, 1.0, 0.0)
                k_aug = jnp.where(rel < 5, jnp.where(hot, 0.0, NEG), jnp.where(rel < 11, 1.0, 0.0))
                q01, k01, v01, q2v2 = (qkv[:, j * 128 : (j + 1) * 128] for j in range(4))
                k2 = jnp.concatenate([qkv[:, 512:576], zero64], axis=1)
                for h, (k, v) in enumerate(((k01, v01), (k01, v01), (k2, q2v2))):
                    half = ~lower if h == 1 else lower
                    k_out[s, h, pl.ds(place, T)] = jnp.where(half, k, k_aug).astype(BF)
                    half = lower if h == 0 else ~lower
                    v_out[s, h, pl.ds(place, T)] = jnp.where(half, v, 1.0).astype(BF)

                def store_q():
                    for h, q in enumerate((q01, q01, q2v2)):
                        half = ~lower if h == 1 else lower
                        q_out[s, h, pl.ds(own, T)] = jnp.where(half, q * 0.125, q_aug).astype(BF)

                if pg == 1:
                    store_q()
                else:
                    pl.when(mine == g)(store_q)


def attn_fwd_kernel(KC, lengths, idx, q_ref, k_ref, v_ref, o_ref, q_out, m_s, acc_s):
    mine = idx[5]
    T, L = o_ref.shape[1], k_ref.shape[2]
    lane = lax.broadcasted_iota(jnp.int32, (T, 128), 1)
    lower = lane < 64

    def per_tile(si, _):
        s, i = si // 4, si % 4
        here = pl.multiple_of(i * T, T)
        first = (mine * 4 + i) * T
        low, high = span(limits(lengths, s, L), first, first + T - 1)
        def whole(width):
            at = pl.multiple_of(jnp.minimum(low // T * T, L - width), T)
            for h in range(3):
                sc = mm_nt(q_ref[s, h, pl.ds(here, T)], k_ref[s, h, pl.ds(at, width)])
                parts = [sc[:, j * 128 : (j + 1) * 128] for j in range(width // 128)]
                top = jnp.max(functools.reduce(jnp.maximum, parts), axis=1, keepdims=True)
                top = jnp.broadcast_to(top, (T, 128))
                p = jnp.concatenate([jnp.exp(v - top).astype(BF) for v in parts], axis=1)
                acc_s[h] = mm(p, v_ref[s, h, pl.ds(at, width)])
                m_s[h] = top

        def running():
            for h in range(3):
                m_s[h] = jnp.full((T, 128), -jnp.inf, F32)
                acc_s[h] = jnp.zeros((T, 128), F32)

            def step(kt, _):
                at = pl.multiple_of(kt * KC, KC)
                for h in range(3):
                    sc = mm_nt(q_ref[s, h, pl.ds(here, T)], k_ref[s, h, pl.ds(at, KC)])
                    old = m_s[h]
                    parts = [sc[:, j * 128 : (j + 1) * 128] for j in range(KC // 128)]
                    top = functools.reduce(jnp.maximum, parts)
                    new = jnp.maximum(old, jnp.broadcast_to(jnp.max(top, axis=1, keepdims=True), (T, 128)))
                    p = jnp.concatenate([jnp.exp(v - new).astype(BF) for v in parts], axis=1)
                    acc_s[h] = acc_s[h] * jnp.exp(old - new) + mm(p, v_ref[s, h, pl.ds(at, KC)])
                    m_s[h] = new
                return 0

            lax.fori_loop(low // KC, (high + KC - 1) // KC, step, 0)

        tiles = (high + T - 1) // T - low // T
        pl.when(tiles <= 2)(functools.partial(whole, 2 * T))
        pl.when(tiles == 3)(functools.partial(whole, 3 * T))
        if L == 4 * T:
            pl.when(tiles == 4)(functools.partial(whole, 4 * T))
        else:
            pl.when(tiles > 3)(running)
        outs = []
        for h in range(3):
            acc = acc_s[h]
            turned = pltpu.roll(acc, 64, 1)
            data = lower if h == 0 else ~lower
            total = jnp.where(data, turned, acc)
            outs.append(acc / total)
            lse = m_s[h] + jnp.log(total)
            l1 = lse.astype(BF).astype(F32)
            l2 = (lse - l1).astype(BF).astype(F32)
            l3 = lse - l1 - l2
            at = lane if h == 1 else lane - 64
            q = q_ref[s, h, pl.ds(here, T)].astype(F32)
            q = jnp.where(at == 8, -l1, jnp.where(at == 9, -l2, jnp.where(at == 10, -l3, q)))
            q_out[s, h, pl.ds(here, T)] = q.astype(BF)
        o_ref[i, :, pl.ds(pl.multiple_of(s * 128, 128), 128)] = jnp.where(lower, outs[0], outs[1]).astype(BF)

        @pl.when(s == 0)
        def _():
            o_ref[i, :, 256:384] = pltpu.roll(outs[2], 64, 1).astype(BF)

        @pl.when(s == 1)
        def _():
            o_ref[i, :, 256:384] = jnp.where(lower, o_ref[i, :, 256:384].astype(F32), outs[2]).astype(BF)

        return 0

    lax.fori_loop(0, 8, per_tile, 0)


def attn_bwd_kernel(pg, KC, lengths, idx, *refs):
    ins, (w, t0, t1, t2, t3, extra), outs, scratch = refs[:5], refs[5:11], refs[11:-6], refs[-6:]
    gq_s = scratch[-1]
    for s in range(2):
        attn_bwd(pg, KC, s, lengths, idx, *ins, *scratch[:4], outs[0].at[s] if pg > 1 else scratch[4])
        if pg == 1:
            products(s, idx, scratch[4], w, (t0, t1, t2, t3), extra, gq_s, *outs)


def attn_bwd(pg, KC, s, lengths, idx, q_ref, k_ref, v_ref, o_ref, do_ref, dq_s, dk_s, dv_s, do_s, d_ref):
    c, mine = idx[2], idx[5]
    T, L = o_ref.shape[1], k_ref.shape[2]
    bounds = limits(lengths, s, L)
    lane = lax.broadcasted_iota(jnp.int32, (T, 128), 1)
    lower = lane < 64
    zero = jnp.zeros((T, 128), F32)

    dk_s[...] = jnp.zeros_like(dk_s)
    dv_s[...] = jnp.zeros_like(dv_s)
    live = bounds[4]
    cols = slice(s * 128, (s + 1) * 128)

    def per_tile(i, _):
        here = pl.multiple_of(i * T, T)
        first = (mine * 4 + i) * T
        low, high = span(bounds, first, first + T - 1)
        high = jnp.minimum(high, live)
        pair = do_ref[i, :, cols].astype(F32)
        third = do_ref[i, :, 256:384].astype(F32)
        if s == 0:
            third = pltpu.roll(third, 64, 1)
        o_third = o_ref[i, :, 256:384].astype(F32)
        if s == 0:
            o_third = pltpu.roll(o_third, 64, 1)
        prod = pair * o_ref[i, :, cols].astype(F32)
        for h in range(3):
            data = lower if h == 0 else ~lower
            full = prod if h < 2 else third * o_third
            delta = jnp.sum(jnp.where(data, full, zero), axis=1, keepdims=True)
            d1 = delta.astype(BF).astype(F32)
            d2 = (delta - d1).astype(BF).astype(F32)
            d3 = delta - d1 - d2
            at = lane - 64 if h == 0 else lane
            aug = jnp.where(at == 8, -d1, jnp.where(at == 9, -d2, jnp.where(at == 10, -d3, zero)))
            do_s[h] = jnp.where(data, pair if h < 2 else third, aug).astype(BF)
            dq_s[h, pl.ds(here, T)] = zero

        def step(kt, _):
            at = pl.multiple_of(kt * KC, KC)
            for h in range(3):
                q = q_ref[s, h, pl.ds(here, T)]
                k = k_ref[s, h, pl.ds(at, KC)]
                d = do_s[h]
                pt = jnp.exp(mm_nt(k, q))
                ds = (pt * mm_nt(v_ref[s, h, pl.ds(at, KC)], d)).astype(BF)
                dv_s[h, pl.ds(at, KC)] += mm(pt.astype(BF), d)
                dk_s[h, pl.ds(at, KC)] += mm(ds, q)
                dq_s[h, pl.ds(here, T)] += mm_tn(ds, k)
            return 0

        lax.fori_loop(low // KC, (high + KC - 1) // KC, step, 0)
        return 0

    lax.fori_loop(0, 4, per_tile, 0)
    for g in range(pg):
        for n, off in enumerate(OFFS):
            at = pl.multiple_of((g * 4 + (c ^ off)) * T, T)
            own = pl.multiple_of((c ^ off) * T, T)
            keep = 0.125 if pg == 1 else jnp.where(mine == g, 0.125, 0.0)
            dq = [dq_s[h, pl.ds(own, T)] * keep for h in range(3)]
            dk = [dk_s[h, pl.ds(at, T)] for h in range(3)]
            dv = [dv_s[h, pl.ds(at, T)] for h in range(3)]
            d_ref[g, n, :, 0:128] = jnp.where(lower, dq[0], dq[1]).astype(BF)
            d_ref[g, n, :, 128:256] = jnp.where(lower, dk[0], dk[1]).astype(BF)
            d_ref[g, n, :, 256:384] = jnp.where(lower, dv[0], dv[1]).astype(BF)
            d_ref[g, n, :, 384:512] = jnp.where(lower, dq[2], dv[2]).astype(BF)
            d_ref[g, n, :, 512:576] = dk[2][:, 0:64].astype(BF)


def products(s, idx, d, w, toks, extra, acc, gq_own, gq_other, gi):
    zw, h, y = idx[1], idx[2], idx[3]
    D = w.shape[0]
    T = d.shape[2]
    rows = slice(s * T, (s + 1) * T)
    for n, off in enumerate(OFFS):
        gi[h ^ off, rows, :] = mm_nt(d[0, n], w[...]).astype(BF)
    v = sum(mm_tn(t[s], d[0, n]) for n, t in enumerate(toks))
    col = sum(fold8(d[0, n].astype(F32)) for n in range(4))
    if s == 0:
        acc[0:D, :] = v
        acc[D : D + 8, :] = col
        return
    acc[0:D, :] += v
    col = jnp.sum(col + acc[D : D + 8, :], axis=0, keepdims=True)
    top = lax.broadcasted_iota(jnp.int32, (8, 576), 0) == 0
    for k in range(4):
        z = zw ^ k
        tail = jnp.where(top & (h == z), col, extra[z])
        tail = jnp.concatenate([tail, jnp.zeros_like(tail)], axis=0).astype(BF)
        for ref, yy in ((gq_own, y), (gq_other, 1 - y)):
            ref[k, 0:96, :] = acc[pl.ds(pl.multiple_of(z * 192 + yy * 96, 8), 96), :].astype(BF)
            ref[k, 96:GQ, :] = tail


def gelu_parts(u):
    t = 1.0 / (1.0 + (0.3275911 * 0.7071067811865476) * jnp.abs(u))
    e = jnp.exp(-0.5 * u * u)
    poly = t * (
        0.127414796
        + t * (-0.142248368 + t * (0.7107068705 + t * (-0.7265760135 + t * 0.5307027145)))
    )
    tail = poly * e
    cdf = jnp.where(u >= 0, 1.0 - tail, tail)
    return u * cdf, cdf + u * e * 0.3989422804014327


def gather_heads(tiles):
    (pair0, third0), (pair1, third1) = tiles
    lower = lax.broadcasted_iota(jnp.int32, pair0.shape, 1) < 64
    turned = pltpu.roll(pair1, 64, 1)
    return pair0, jnp.where(lower, third0, turned), jnp.where(lower, turned, pltpu.roll(third1, 64, 1))


def ffn_kernel(
    idx, lengths, attn, tok, cot, sm_own, w_in, w_at, w_out,
    s1a, r2a, c1a, c2a, s1b, r2b, c1b, c2b,
    out, dfirst, dattn, sent, kept, extra,
    w1, w2, wa, sm, b1, att, hlow, xhat, rstd, acc, act, gp, dlow, sums, sem, osem,
):
    c, z, h, y, x, mine = (idx[i] for i in range(6))
    R, D = tok.shape
    T = attn.shape[1]
    FB = w_in.shape[1] // 8
    TR, GR = 256, 128
    first_copies = [(w_at, wa.at[z]), (sm_own.at[240:256], sm.at[0])]
    first_copies += [(s1a.at[0, k, 240:256], sm.at[k + 1]) for k in range(3)]
    copies = [(w_in, w1.at[z]), (w_out, w2.at[z])]
    for n, (ra, rb) in enumerate(((s1a, s1b), (r2a, r2b), (c1a, c1b), (c2a, c2b))):
        for k in range(2):
            p = idx[6 + 2 * n + k]
            q, half = p // 2, p % 2
            for kz in range(3):
                zz = z ^ (kz + 1)
                at = pl.ds(pl.multiple_of(half * FB, 128), FB)
                first_copies.append((ra.at[k, kz, 192:240], wa.at[zz, pl.ds(pl.multiple_of(q * 48, 16), 48), at]))
                copies.append((ra.at[k, kz, 0:192], w1.at[zz, :, pl.ds(pl.multiple_of(p * FB, 128), FB)]))
                copies.append((rb.at[k, kz], w2.at[zz, pl.ds(pl.multiple_of(half * FB + q * 96, 16), 96)]))
    many = len(first_copies)
    first_copies = [pltpu.make_async_copy(a, b, sem.at[i]) for i, (a, b) in enumerate(first_copies)]
    copies = [pltpu.make_async_copy(a, b, sem.at[many + i]) for i, (a, b) in enumerate(copies)]
    for cp in first_copies + copies:
        cp.start()

    sums[...] = jnp.zeros_like(sums)
    extra[...] = jnp.zeros_like(extra)

    lower = lax.broadcasted_iota(jnp.int32, (T, 128), 1) < 64
    for s in range(2):
        for g in range(0, 4, 2):
            tiles = []
            for n in (g, g + 1):
                third = attn[n, :, 256:384].astype(F32)
                tiles.append((
                    attn[n, :, s * 128 : (s + 1) * 128].astype(F32),
                    third if s == 0 else pltpu.roll(third, 64, 1),
                ))
            for j, tile in enumerate(gather_heads(tiles)):
                at = g * 192 + j * 128
                att[s * T : (s + 1) * T, at : at + 128] = tile.astype(BF)

    for cp in first_copies:
        cp.wait()

    small = [sm[k ^ z].astype(F32) for k in range(4)]

    def whole(i):
        return jnp.concatenate([v[i : i + 1, 0:192] for v in small], axis=1)

    b_attn, g1v, s1v, b_out, g2v, s2v = (whole(i) for i in range(2, 8))
    for k in range(4):
        row = jnp.concatenate([small[k][i : i + 1, 0:192] for i in range(8, 12)], axis=1)
        for half in range(2):
            b1[2 * k + half, 0:1, :] = row[:, half * FB : (half + 1) * FB]

    acc[...] = mm(att[...], wa[...].reshape(D, D))

    def first(r, _):
        rows = pl.ds(pl.multiple_of(r * TR, TR), TR)
        v = acc[rows, :] + tok[rows, :].astype(F32) + b_attn
        mean = jnp.mean(v, axis=-1, keepdims=True)
        v = v - mean
        rs = lax.rsqrt(jnp.mean(v * v, axis=-1, keepdims=True) + EPS)
        xh = v * rs
        xhat[rows, :] = xh
        rstd[rows, :] = jnp.broadcast_to(rs, (TR, 128))
        hid = xh * g1v + s1v
        hlow[rows, :] = hid.astype(BF)
        acc[rows, :] = hid + b_out
        return 0

    lax.fori_loop(0, R // TR, first, 0)
    for cp in copies:
        cp.wait()

    def keep(src, i, cc, at):
        to = pl.ds(pl.multiple_of(i * FB, 128), FB)

        @pl.when(c == cc)
        def _():
            pltpu.make_async_copy(src, kept.at[:, to], osem.at[at]).start()

        @pl.when(c != cc)
        def _():
            pltpu.make_async_copy(src, sent.at[:, to], osem.at[at]).start()

    def kept_all(first, count):
        for i in range(first, first + count):
            pltpu.make_async_copy(act.at[:, 0:FB], kept.at[:, 0:FB], osem.at[i]).wait()

    def forward(zz, _):
        cols = pl.ds(pl.multiple_of(zz * D, 128), D)
        u = mm(hlow[...], w1[:, :, cols].reshape(D, D)) + jnp.concatenate([b1[2 * zz, 0:1, :], b1[2 * zz + 1, 0:1, :]], axis=1)
        for r in range(R // GR):
            rows = slice(r * GR, (r + 1) * GR)
            a, d = gelu_parts(u[rows])
            act[rows, cols] = a.astype(BF)
            gp[rows, cols] = d.astype(BF)
        acc[...] += mm(act[:, cols], w2[zz])
        for half in range(2):
            src = act.at[:, pl.ds(pl.multiple_of(zz * D + half * FB, 128), FB)]
            keep(src, zz, half, 2 * zz + half)
        return 0

    lax.fori_loop(0, 4, forward, 0)

    def second(r, _):
        rows = pl.ds(pl.multiple_of(r * TR, TR), TR)
        s = r // (T // TR)
        v = acc[rows, :]
        mean = jnp.mean(v, axis=-1, keepdims=True)
        v = v - mean
        rs = lax.rsqrt(jnp.mean(v * v, axis=-1, keepdims=True) + EPS)
        xh = v * rs
        out[rows, :] = (xh * g2v + s2v).astype(BF)
        place = (mine * 4 + h) * T + r * TR - s * T
        pos = lax.broadcasted_iota(jnp.int32, (TR, D), 0) + place
        dy = jnp.where(pos < limits(lengths, s, 0)[4], cot[rows, :].astype(F32), 0.0)
        sums[4] += fold8(dy * xh)
        sums[5] += fold8(dy)
        dx = dy * g2v
        m1 = jnp.mean(dx, axis=-1, keepdims=True)
        m2 = jnp.mean(dx * xh, axis=-1, keepdims=True)
        ds = rs * (dx - m1 - xh * m2)
        low = ds.astype(BF)
        dlow[rows, :] = low
        sums[3] += fold8(low.astype(F32))
        acc[rows, :] = ds
        return 0

    lax.fori_loop(0, R // TR, second, 0)

    kept_all(0, 8)
    shared = [(att, 9), (hlow, 11), (dlow, 13)]
    shared = [pltpu.make_async_copy(v, sent.at[:, i * FB : (i + 2) * FB], osem.at[n + 16]) for n, (v, i) in enumerate(shared)]
    for cp in shared:
        cp.start()

    def backward(zz, _):
        cols = pl.ds(pl.multiple_of(zz * D, 128), D)
        da = mm_nt(dlow[...], w2[zz])
        gsum = jnp.zeros((8, D), F32)
        for r in range(R // GR):
            rows = slice(r * GR, (r + 1) * GR)
            di = (da[rows] * gp[rows, cols].astype(F32)).astype(BF)
            act[rows, cols] = di
            gsum = gsum + fold8(di.astype(F32))
        acc[...] += mm_nt(act[:, cols], w1[:, :, cols].reshape(D, D))
        for half in range(2):
            src = act.at[:, pl.ds(pl.multiple_of(zz * D + half * FB, 128), FB)]
            keep(src, 4 + zz, half, 8 + 2 * zz + half)
        gsum = jnp.sum(gsum, axis=0, keepdims=True)
        extra[zz, 3:4, :] = gsum[:, 0:576]
        extra[zz, 4:5, 0:192] = gsum[:, 576:768]
        return 0

    lax.fori_loop(0, 4, backward, 0)
    for cp in shared:
        cp.wait()

    def last(r, _):
        rows = pl.ds(pl.multiple_of(r * TR, TR), TR)
        dy = acc[rows, :]
        xh = xhat[rows, :]
        sums[1] += fold8(dy * xh)
        sums[2] += fold8(dy)
        dx = dy * g1v
        m1 = jnp.mean(dx, axis=-1, keepdims=True)
        m2 = jnp.mean(dx * xh, axis=-1, keepdims=True)
        df = rstd[rows, :1] * (dx - m1 - xh * m2)
        dfirst[rows, :] = df
        low = df.astype(BF)
        dlow[rows, :] = low
        sums[0] += fold8(low.astype(F32))
        return 0

    lax.fori_loop(0, R // TR, last, 0)
    acc[...] = mm_nt(dlow[...], wa[...].reshape(D, D))
    for g in range(0, 4, 2):
        thirds = []
        for s in range(2):
            t0, t1, t2 = (acc[s * T : (s + 1) * T, g * 192 + j * 128 : g * 192 + (j + 1) * 128] for j in range(3))
            t1r, t2r = pltpu.roll(t1, 64, 1), pltpu.roll(t2, 64, 1)
            dattn[g, :, s * 128 : (s + 1) * 128] = t0.astype(BF)
            dattn[g + 1, :, s * 128 : (s + 1) * 128] = jnp.where(lower, t1r, t2r).astype(BF)
            thirds.append((t1, t1r, t2, t2r))
        (a1, _, _, a2r), (_, b1r, b2, _) = thirds
        dattn[g, :, 256:384] = jnp.where(lower, a1, b1r).astype(BF)
        dattn[g + 1, :, 256:384] = jnp.where(lower, a2r, b2).astype(BF)
    for half in range(2):
        keep(dlow.at[:, half * FB : (half + 1) * FB], 8, half, 19 + half)
    for i in range(6):
        row = jnp.sum(sums[i], axis=0, keepdims=True)
        for k in range(4):
            at = (i % 3) * 192
            extra[k, 1 + i // 3 : 2 + i // 3, at : at + 192] = row[:, k * 192 : (k + 1) * 192]
    kept_all(8, 8)
    kept_all(19, 2)


def weight_kernel(idx, kept, mate, sent, plane, mine, s1, s2, s3, units, shared, units2, shared2, plane_s, mine_s, sent_s, sem, osem):
    z = idx[1]
    D = shared.shape[1] // 3
    FB = D // 2
    wide = 4 * FB
    copies = []
    for refs, us, sh in (((kept, sent), units, shared), ((mate, mate), units2, shared2)):
        for at, size in ((wide, wide), (0, wide), (2 * wide, FB)):
            copies.append((refs[0].at[:, at : at + size], us.at[:, at : at + size]))
        for at in (D, 2 * D, 0):
            copies.append((refs[1].at[:, 9 * FB + at : 9 * FB + at + D], sh.at[:, at : at + D]))
    order = (1, 4, 7, 10, 0, 3, 6, 9, 2, 5, 8, 11)
    copies = [pltpu.make_async_copy(*copies[n], sem.at[n]) for n in order]
    for cp in copies:
        cp.start()
    for cp in copies[:4]:
        cp.wait()
    outs = []

    def emit(src, to):
        cp = pltpu.make_async_copy(src, to, osem.at[len(outs)])
        cp.start()
        outs.append(cp)

    for k in (1, 2, 3, 0):
        cols = pl.ds(pl.multiple_of((z ^ k) * FB, 128), FB)
        v = mm_tn(units[:, cols], shared[:, 2 * D : 3 * D]) + mm_tn(units2[:, cols], shared2[:, 2 * D : 3 * D])
        for q in range(4):
            if k == 0:
                mine_s[q] = v[q * 96 : (q + 1) * 96]
            else:
                sent_s[k - 1, q] = v[q * 96 : (q + 1) * 96].astype(BF)
        if k == 0:
            emit(mine_s, mine)
        else:
            emit(sent_s.at[k - 1], (s1, s2, s3)[k - 1])
    for cp in copies[4:]:
        cp.wait()
    v = mm_tn(shared[:, 0:D], units[:, 2 * wide : 2 * wide + FB]) + mm_tn(shared2[:, 0:D], units2[:, 2 * wide : 2 * wide + FB])
    v = v.astype(BF)
    for zz in range(4):
        for q in range(4):
            plane_s[q, zz, 192:240, :] = v[zz * 192 + q * 48 : zz * 192 + (q + 1) * 48]
    for n in range(2):
        cols = slice(wide + n * D, wide + (n + 1) * D)
        v = mm_tn(shared[:, D : 2 * D], units[:, cols]) + mm_tn(shared2[:, D : 2 * D], units2[:, cols])
        v = v.astype(BF)
        for i in range(2):
            for zz in range(4):
                plane_s[2 * n + i, zz, 0:192, :] = v[zz * 192 : (zz + 1) * 192, i * FB : (i + 1) * FB]
        emit(plane_s.at[2 * n : 2 * n + 2], plane.at[2 * n : 2 * n + 2])
    for cp in outs:
        cp.wait()


def products_kernel(idx, d, w, t0, t1, t2, t3, extra, *outs):
    for s in range(2):
        products(s, idx, d.at[s], w, (t0, t1, t2, t3), extra, outs[-1], *outs[:-1])


def chunkq_kernel(own, got, *outs):
    for k, ref in enumerate(outs):
        ref[...] = (own[k].astype(F32) + got[k].astype(F32)).astype(ref.dtype)


def chunk_kernel(idx, terms, *outs):
    z = idx[1]
    for k, ref in enumerate(outs):
        ref[...] = sum(terms[q, z ^ k].astype(F32) for q in range(4)).astype(ref.dtype)


def sum2_kernel(idx, a0, a1, a2, a3, *outs):
    here = idx[3] * 2 + idx[4]
    for k, ref in enumerate(outs):
        q = here ^ k
        ref[...] = (a0[q] + sum(a[q].astype(F32) for a in (a1, a2, a3))).astype(ref.dtype)


def sum_kernel(a0, a1, a2, a3, b0, b1, b2, b3, out):
    A, B = a0.shape
    C = b0.shape[0]
    out[0:A, :] = (a0[...] + sum(a[...].astype(F32) for a in (a1, a2, a3))).astype(BF)
    v = (b0[...] + sum(b[...].astype(F32) for b in (b1, b2, b3))).astype(BF)
    out[A : A + C, :] = v[:, :B]
    out[A + C : A + 2 * C, :] = v[:, B:]


def sumq_kernel(q0, q1, q2, q3, out):
    E, W = q0.shape
    B = out.shape[1]
    v = (q0[...] + sum(q[...].astype(F32) for q in (q1, q2, q3))).astype(BF)
    out[0:E, :] = v[:, :B]
    out[E : 2 * E, :] = jnp.zeros((E, B), BF)
    out[E : 2 * E, 0 : W - B] = v[:, B:]


def out_ffn_kernel(idx, s1, r2, c1, c2, g_wi, g_wa, g_wo):
    FB = s1.shape[2]
    refs = (s1, r2, c1, c2)
    for n, ref in enumerate(refs):
        for k in range(2):
            p = idx[6 + 2 * n + k]
            g_wi[:, pl.ds(pl.multiple_of(p * FB, 128), FB)] = ref[k, 0:192, :].astype(F32)
            rows = pl.ds(pl.multiple_of((p // 2) * 48, 16), 48)
            g_wa[rows, pl.ds(pl.multiple_of((p % 2) * FB, 128), FB)] = ref[k, 192:240, :].astype(F32)
            rows = pl.ds(pl.multiple_of((p % 2) * FB + (p // 2) * 96, 16), 96)
            g_wo[rows, 0:FB] = ref[k, 240:336, :].astype(F32)
            g_wo[rows, FB : 2 * FB] = ref[k, 336:432, :].astype(F32)


def out_qkv_kernel(idx, s1, r2, c1, c2, g_wq, g_wk, g_wv, g_bq, g_bv, g_bi, *six):
    FB = s1.shape[2]
    c, z = idx[0], idx[1]
    refs = (s1, r2, c1, c2)
    lower = lax.broadcasted_iota(jnp.int32, (96, 128), 1) < 64
    left, right = jnp.zeros((16, FB), F32), jnp.zeros((16, FB), F32)
    top = lax.broadcasted_iota(jnp.int32, (16, FB), 0) == 0
    for (n, k), (m, j) in (((0, 0), (2, 0)), ((0, 1), (3, 0)), ((1, 0), (2, 1)), ((1, 1), (3, 1))):
        p = idx[6 + 2 * n + k]
        yy, xx = p // 4, (p // 2) % 2
        own, other = refs[n].at[k], refs[m].at[j]

        def tile(i, swap):
            at = slice(0, 96) if i < 3 else slice(GQ, GQ + 96)
            cols = slice((i % 3) * 128, (i % 3 + 1) * 128)
            u, v = own[at, cols].astype(F32), other[at, cols].astype(F32)
            return jnp.where((c == 0) != swap, u, v)

        rows = pl.ds(pl.multiple_of(yy * 96, 8), 96)
        for ref, i, third, low in ((g_wq, 0, 3, True), (g_wk, 1, 4, True), (g_wv, 2, 3, False)):
            ta, tb = tile(third, False), tile(third, True)
            turned = pltpu.roll(tile(i, True), 64, 1)
            if not low:
                ta = pltpu.roll(ta, 64, 1)
            else:
                tb = pltpu.roll(tb, 64, 1)
            base = xx * 384
            ref[rows, pl.ds(pl.multiple_of(base, 128), 128)] = tile(i, False)
            ref[rows, pl.ds(pl.multiple_of(base + 128, 128), 128)] = jnp.where(lower, ta, turned)
            ref[rows, pl.ds(pl.multiple_of(base + 256, 128), 128)] = jnp.where(lower, turned, tb)
        for ref, cc in ((own, c), (other, 1 - c)):
            here = (yy == 0) & (~top | (xx * 2 + cc == z))
            left = left + jnp.where(here, ref[96:GQ, :].astype(F32), 0.0)
            right = right + jnp.where(here, ref[GQ + 96 : 2 * GQ, :].astype(F32), 0.0)
    g_bq[...] = jnp.concatenate([left[0:1, 0:128], right[0:1, 0:64]], axis=1).reshape(192)
    g_bv[...] = jnp.concatenate([left[0:1, 256:384], right[0:1, 64:128]], axis=1).reshape(192)
    for i, ref in enumerate(six):
        row = 1 + i // 3
        ref[...] = (left[row : row + 1, 0:192], left[row : row + 1, 192:384], right[row : row + 1, 0:192])[i % 3].reshape(192)
    g_bi[...] = jnp.concatenate([left[3:4, :], right[3:4, 0:192], left[4:5, 0:192]], axis=1).reshape(768)


def tie(*values):
    return lax.optimization_barrier(values)


def block(shape, *at):
    return pl.BlockSpec(shape, lambda i: at)


def call(kernel, outs, in_specs, out_specs, scratch=(), name=None, grid=()):
    return pl.pallas_call(
        kernel,
        out_shape=outs,
        grid=grid,
        in_specs=in_specs,
        out_specs=out_specs,
        scratch_shapes=list(scratch),
        compiler_params=pltpu.CompilerParams(vmem_limit_bytes=VMEM_LIMIT),
        cost_estimate=pl.CostEstimate(flops=1, bytes_accessed=1, transcendentals=0),
        name=name,
    )


def make_body(sizes):
    pg = sizes["pg"]
    order = [sizes[a] for a in AX]

    def send(fn, a):
        pairs = []
        for flat in range(math.prod(order)):
            at, rest = [], flat
            for n in reversed(order):
                at.append(rest % n)
                rest //= n
            dest = 0
            for n, v in zip(order, fn(*reversed(at))):
                dest = dest * n + v
            pairs.append((flat, dest))
        return lax.ppermute(a, AX, pairs)

    to_x = functools.partial(send, lambda s, g, x, c, z: (s, g, 1 - x, c, z))
    to_y = functools.partial(send, lambda s, g, x, c, z: (1 - s, g, x, c, z))
    to_core = functools.partial(send, lambda s, g, x, c, z: (s, g, x, 1 - c, z))
    to_z = [functools.partial(send, lambda s, g, x, c, z, k=k: (s, g, x, c, z ^ k)) for k in (1, 2, 3)]
    mix_a = functools.partial(send, lambda s, g, x, c, z: (s, g, 1 - x, c, z) if c == 0 else (1 - s, g, x, c, z))
    mix_b = functools.partial(send, lambda s, g, x, c, z: (1 - s, g, x, c, z) if c == 0 else (s, g, 1 - x, c, z))

    to_d = functools.partial(send, lambda s, g, x, c, z: (1 - s, g, 1 - x, c, z))

    def over_z(sent):
        return [f(v) for f, v in zip(to_z, sent if isinstance(sent, list) else [sent] * 3)]

    def body(
        tokens, cotangent, segment_ids, lengths, w_query, b_query, w_key, w_value, b_value, w_attn, b_attn,
        ln1_gain, ln1_shift, w_inner, b_inner, w_outer, b_outer, ln2_gain, ln2_shift,
    ):
        S, T, D = tokens.shape
        R = S * T
        y, x, c = (lax.axis_index(a) for a in ("seq", "x", "core"))
        mine, z = lax.axis_index("pg"), lax.axis_index("wt")
        h = x * 2 + c
        p = y * 4 + h
        L = 4 * pg * T
        FB = w_inner.shape[1] // 8

        a_of = jnp.where(c == 0, 2, 4)
        other = p ^ 1
        mates = [p, p ^ a_of, p ^ (6 - a_of), p ^ 6, other, other ^ (6 - a_of), other ^ a_of, other ^ 6]
        idx = jnp.stack([c, z, h, y, x, mine] + mates).astype(jnp.int32)

        vecs = (b_query, b_value, b_attn, ln1_gain, ln1_shift, b_outer, ln2_gain, ln2_shift, b_inner)
        w_own, pack, piece1, piece2 = call(
            prep_kernel,
            (
                jax.ShapeDtypeStruct((208, 576), BF), jax.ShapeDtypeStruct((GQ, 576), BF),
                jax.ShapeDtypeStruct((256, FB), BF), jax.ShapeDtypeStruct((96, D), BF),
            ),
            [SM] + [VM] * 15, (VM,) * 4, name="prep",
        )(idx, w_query, w_key, w_value, w_attn, w_inner, w_outer, *vecs)
        w_z = over_z(pack)
        tok_x, tok_c = to_x(tokens), to_core(tokens)
        w_z, tok_x, tok_c, piece1 = tie(w_z, tok_x, tok_c, piece1)
        w_y, tok_xc = to_y(jnp.stack(w_z)), to_core(tok_x)
        z1 = over_z(piece1)
        w_y, tok_xc, z1, piece2 = tie(w_y, tok_xc, z1, piece2)
        z2 = over_z(piece2)
        one = jnp.stack(z1)
        tok_xc, one = tie(tok_xc, one)
        one_a = mix_a(one)

        toks = [t[None] for t in (tokens, tok_x, tok_c, tok_xc)]
        if pg > 1:
            toks = [lax.all_gather(t, "pg", axis=0, tiled=True) for t in toks]
        head = jax.ShapeDtypeStruct((S, 3, L, 128), BF)
        own_head = jax.ShapeDtypeStruct((S, 3, 4 * T, 128), BF)
        q_aug, k_aug, v_aug, w_qkv = call(
            functools.partial(qkv_kernel, pg),
            (own_head, head, head, jax.ShapeDtypeStruct((4, 192, 576), BF)),
            [SM, SM] + [VM] * 4 + [ANY] * 5,
            (VM,) * 4,
            [pltpu.VMEM((4, 16, 576), BF), pltpu.SemaphoreType.DMA((11,))],
            name="qkv",
        )(lengths, idx, *toks, w_own, *w_z, w_y)
        w_qkv = w_qkv.reshape(D, 576)
        q_aug, one_a, z2 = tie(q_aug, one_a, z2)
        one, two = jnp.stack([one, one_a]), jnp.stack(z2)
        q_aug, one, two = tie(q_aug, one, two)
        one_b, two_a = mix_b(one), mix_a(two)
        o, q_aug = call(
            functools.partial(attn_fwd_kernel, 1024),
            (jax.ShapeDtypeStruct((4, T, 384), BF), own_head),
            [SM, SM] + [VM] * 3,
            (VM,) * 2,
            [pltpu.VMEM((3, T, 128), F32), pltpu.VMEM((3, T, 128), F32)],
            name="attn_fwd",
        )(lengths, idx, q_aug, k_aug, v_aug)
        o, one_b, two_a = tie(o, one_b, two_a)
        attn = lax.all_to_all(o, ("x", "core"), 0, 0, tiled=True)
        two = jnp.stack([two, two_a])
        two_b = mix_b(two)
        one = (one, one_b, to_core(one), to_core(one_b))
        attn, two_b = tie(attn, two_b)
        two = (two, two_b, to_core(two), to_core(two_b))

        layer_out, d_first, d_attn, sent, kept, extra = call(
            ffn_kernel,
            (
                jax.ShapeDtypeStruct((R, D), BF), jax.ShapeDtypeStruct((R, D), F32), jax.ShapeDtypeStruct((4, T, 384), BF),
                jax.ShapeDtypeStruct((R, 15 * FB), BF), jax.ShapeDtypeStruct((R, 9 * FB), BF), jax.ShapeDtypeStruct((4, 8, 576), F32),
            ),
            [SM, SM] + [VM] * 3 + [ANY] * 12,
            (VM, VM, VM, ANY, ANY, VM),
            [
                pltpu.VMEM((4, 192, 8 * FB), BF),
                pltpu.VMEM((4, 2 * FB, D), BF),
                pltpu.VMEM((4, 192, D), BF),
                pltpu.VMEM((4, 16, FB), BF),
                pltpu.VMEM((8, 8, FB), F32),
                pltpu.VMEM((R, D), BF),
                pltpu.VMEM((R, D), BF),
                pltpu.VMEM((R, D), F32),
                pltpu.VMEM((R, 128), F32),
                pltpu.VMEM((R, D), F32),
                pltpu.VMEM((R, 8 * FB), BF),
                pltpu.VMEM((R, 8 * FB), BF),
                pltpu.VMEM((R, D), BF),
                pltpu.VMEM((8, 8, D), F32),
                pltpu.SemaphoreType.DMA((79,)),
                pltpu.SemaphoreType.DMA((21,)),
            ],
            name="ffn",
        )(
            idx, lengths, attn, tokens.reshape(R, D), cotangent.reshape(R, D), piece1, w_inner, w_attn, w_outer, *one, *two
        )

        d_o = lax.all_to_all(d_attn, ("x", "core"), 0, 0, tiled=True)

        def add(*parts):
            return sum(v.astype(F32) for v in parts)

        def shares(n, m):
            return jax.ShapeDtypeStruct((*n, m), F32), *(jax.ShapeDtypeStruct((*n, m), BF),) * 3

        def attn_back(d_o):
            part = jax.ShapeDtypeStruct((4, GQ, 576), BF)
            outs = (part, part, jax.ShapeDtypeStruct((4, R, D), BF))
            more = (w_qkv, tokens, tok_x, tok_c, tok_xc, extra)
            total = pltpu.VMEM((D + 8, 576), F32)
            res = call(
                functools.partial(attn_bwd_kernel, pg, 512),
                outs if pg == 1 else (jax.ShapeDtypeStruct((S, pg, 4, T, 576), BF),),
                [SM, SM] + [VM] * 5 + [VM if pg == 1 else ANY] * 6,
                (VM,) * (3 if pg == 1 else 1),
                [
                    pltpu.VMEM((3, 4 * T, 128), F32), pltpu.VMEM((3, L, 128), F32), pltpu.VMEM((3, L, 128), F32),
                    pltpu.VMEM((3, T, 128), BF), pltpu.VMEM((1, 4, T, 576), BF), total,
                ],
                name="attn_bwd",
            )(lengths, idx, q_aug, k_aug, v_aug, o, d_o, *more)
            if pg > 1:
                d = lax.psum_scatter(res[0], "pg", scatter_dimension=1, tiled=True)
                res = call(products_kernel, outs, [SM] + [VM] * 7, (VM,) * 3, [total], name="products")(idx, d, *more)
            return res

        part = jax.ShapeDtypeStruct((4, 96, D), BF)
        q1, c2, *sent2 = call(
            weight_kernel,
            (jax.ShapeDtypeStruct((4, 4, 240, FB), BF), jax.ShapeDtypeStruct((4, 96, D), F32)) + (part,) * 3,
            [SM] + [ANY] * 3, (ANY,) * 5,
            [
                pltpu.VMEM((R, 9 * FB), BF), pltpu.VMEM((R, 3 * D), BF), pltpu.VMEM((R, 9 * FB), BF), pltpu.VMEM((R, 3 * D), BF),
                pltpu.VMEM((4, 4, 240, FB), BF), pltpu.VMEM((4, 96, D), F32),
                pltpu.VMEM((3, 4, 96, D), BF), pltpu.SemaphoreType.DMA((12,)), pltpu.SemaphoreType.DMA((6,)),
            ],
            name="weights",
        )(idx, kept, to_core(sent), sent)
        n, m = q1.shape[2:]
        d_o, sent2, q1 = tie(d_o, sent2, q1)
        got_z2, q1 = over_z(sent2), lax.all_to_all(q1, ("seq", "x"), 0, 0, tiled=True)
        gq_own, gq_other, gi = attn_back(d_o)
        gq_y = to_y(gq_other)
        c1, *sent1 = call(chunk_kernel, shares((n,), m), [SM, VM], (VM,) * 4, name="chunks1")(idx, q1)
        sent1, got_z2 = tie(sent1, got_z2)
        got_z1 = over_z(sent1)
        gi = lax.all_to_all(gi, ("x", "core"), 0, 0, tiled=True)
        cq, *sentq = call(chunkq_kernel, shares((GQ,), 576), [VM] * 2, (VM,) * 4, name="chunksq")(gq_own, gq_y)
        p2, *sent2 = call(sum2_kernel, shares((96,), D), [SM] + [VM] * 4, (VM,) * 4, name="sums2")(idx, c2, *got_z2)
        sent2, got_z1, sentq = tie(sent2, got_z1, sentq)
        got_zq = over_z(sentq)
        got_p2 = [f(v) for f, v in zip((to_x, to_y, to_d), sent2)]

        total = call(sum_kernel, jax.ShapeDtypeStruct((432, FB), BF), [VM] * 8, VM, name="sums")(c1, *got_z1, p2, *got_p2)
        total, got_zq = tie(total, got_zq)
        total_q = call(sumq_kernel, jax.ShapeDtypeStruct((2 * GQ, FB), BF), [VM] * 4, VM, name="sumsq")(cq, *got_zq)
        if pg > 1:
            total, total_q = (lax.psum(v.astype(F32), "pg").astype(BF) for v in (total, total_q))

        mate = mix_a(total)
        mate, total_q = tie(mate, total_q)
        mate_q = mix_a(total_q)
        s1 = jnp.stack([total, mate])
        r2, s1_core = mix_b(s1), to_core(s1)
        s1_q = jnp.stack([total_q, mate_q])
        r2_q = mix_b(s1_q)
        r2, s1_core, s1_q = tie(r2, s1_core, s1_q)
        grad_input = add(d_first, *(gi[k] for k in range(4))).astype(BF).reshape(tokens.shape)
        mat, wide = jax.ShapeDtypeStruct((192, D), F32), jax.ShapeDtypeStruct((192, 8 * FB), F32)
        vec, long_vec = jax.ShapeDtypeStruct((192,), F32), jax.ShapeDtypeStruct((2 * FB,), F32)
        g_wi, g_wa, g_wo = call(
            out_ffn_kernel, (wide, mat, jax.ShapeDtypeStruct((D, D), F32)), [SM] + [VM] * 4, (VM,) * 3, name="out_ffn"
        )(idx, s1, r2, s1_core, to_core(r2))
        g_wi, g_wa, g_wo, r2_q, grad_input = tie(g_wi, g_wa, g_wo, r2_q, grad_input)
        g_wq, g_wk, g_wv, g_bq, g_bv, g_bi, *six = call(
            out_qkv_kernel, (mat, mat, mat, vec, vec, long_vec) + (vec,) * 6, [SM] + [VM] * 4, (VM,) * 12, name="out_qkv"
        )(idx, s1_q, r2_q, to_core(s1_q), to_core(r2_q))
        return (
            layer_out.reshape(tokens.shape), grad_input,
            g_wq, g_bq, g_wk, g_wv, g_bv, g_wa, six[0], six[1], six[2], g_wi, g_bi, g_wo, six[3], six[4], six[5],
        )

    return body


def solution(mesh):
    sizes = dict(mesh.shape)
    pg = sizes["ctx"] // 4
    fine = dict(zip(AX, (sizes["seq"], pg, 2, 2, sizes["wt"])))
    split = Mesh(mesh.devices.reshape(tuple(fine.values())), AX)
    rows = P(("seq", "wt"), ("pg", "x", "core"), None)
    mat, vec = P("wt", None), P("wt")
    in_specs = (
        rows, rows, P(("seq", "wt"), ("pg", "x", "core")), P(("seq", "wt"), None),
        mat, vec, mat, mat, vec, mat, vec, vec, vec, mat, vec, mat, vec, vec, vec,
    )
    out_specs = (rows, rows, mat, vec, mat, mat, vec, mat, vec, vec, vec, mat, vec, mat, vec, vec, vec)
    return jax.shard_map(make_body(fine), mesh=split, in_specs=in_specs, out_specs=out_specs, check_vma=False)
```
